256 devices in a mesh: row: 32 (over x_hi, z, core), col: 8 (over x_lo, y).
Axes of the slice: x: 4 (x_hi: 2, x_lo: 2; x = x_hi * 2 + x_lo), y: 4, z: 8, core: 2. Of those that a mesh axis runs over, the one named last changes fastest.
Arguments:
- pair_input: bfloat16 [1024, 1024, 128], P('row', 'col'), may hold values from -16 to 16
- token_mask: int32 [1024], replicated, may hold values 0 or 1
- in_gain: float32 [2, 128], replicated, may hold values from 0.5 to 2
- proj_weight: bfloat16 [2, 128, 512], replicated, may hold values from -0.5 to 0.5
- gate_weight: bfloat16 [2, 128, 128], replicated, may hold values from -0.5 to 0.5
- out_gain: float32 [2, 128], replicated, may hold values from 0.5 to 2
- out_weight: bfloat16 [2, 128, 128], replicated, may hold values from -0.5 to 0.5
Outputs:
- pair_out: bfloat16 [1024, 1024, 128], P('row', 'col')
The draws below stay inside these ranges and needn't reach their ends.
All inputs are finite; a program needn't handle non-finite values.
Results may differ from the reference program's by a relative error of at most 0.008.
Values may be sent and summed in bfloat16 or wider, within the bound.
No kernel may reach another device: no remote copies, remote signals or barrier semaphores. Data moves between devices by JAX's collectives and lax.ppermute only.
A program may use at most 64 MiB of HBM per device.

```python
import math
import jax
import jax.numpy as jnp
from jax import lax

PAIR_WIDTH = 128
TRI_HIDDEN = 128
TOKENS = 1024


def draw_pair_input(key, part):
    key = jax.random.fold_in(key, 17)
    value_key, cell_key, chan_key = jax.random.split(key, 3)
    cell_scale = jnp.exp(jax.random.uniform(cell_key, (TOKENS, TOKENS, 1), jnp.float32, -0.6931, 0.6931))
    chan_scale = jnp.exp(jax.random.uniform(chan_key, (PAIR_WIDTH,), jnp.float32, -0.6931, 0.6931))
    raw_values = jnp.clip(jax.random.normal(value_key, (TOKENS, TOKENS, PAIR_WIDTH), jnp.float32), -4.0, 4.0)
    return (raw_values * cell_scale * chan_scale).astype(jnp.bfloat16)


def touch_ends(result, key, least, high):
    spot = [jax.random.randint(jax.random.fold_in(key, axis), (), 0, length) for axis, length in enumerate(result.shape)]
    main_axis = result.shape.index(max(result.shape))
    beside = spot[:main_axis] + [(spot[main_axis] + 1) % result.shape[main_axis]] + spot[main_axis + 1:]
    return result.at[tuple(spot)].set(least).at[tuple(beside)].set(high)


def scatter_about(key, shape, deviation, limit, held_as=jnp.bfloat16):
    result = deviation * jax.random.normal(key, shape, jnp.float32)
    return jnp.clip(result, min=-limit, max=limit).astype(held_as)


def setup_inputs(seed: int = 0) -> dict:
    key_list = jax.random.split(jax.random.key(seed), 8)
    return {
        "pair_input": draw_pair_input(jax.random.fold_in(key_list[7], 71), 0),
        "token_mask": touch_ends((jax.random.randint(key_list[1], (TOKENS,), 0, 8) < 7).astype(jnp.int32), jax.random.fold_in(key_list[1], 1), 0, 1),
        "in_gain": jnp.clip(jnp.exp(jax.random.uniform(key_list[2], (2, PAIR_WIDTH), jnp.float32, math.log(0.5), math.log(2.0))), 0.5, 2.0),
        "proj_weight": scatter_about(key_list[3], (2, PAIR_WIDTH, 4 * TRI_HIDDEN), PAIR_WIDTH ** -0.5, 0.5),
        "gate_weight": scatter_about(key_list[4], (2, PAIR_WIDTH, PAIR_WIDTH), PAIR_WIDTH ** -0.5, 0.5),
        "out_gain": jnp.clip(jnp.exp(jax.random.uniform(key_list[5], (2, TRI_HIDDEN), jnp.float32, math.log(0.5), math.log(2.0))), 0.5, 2.0),
        "out_weight": scatter_about(key_list[6], (2, TRI_HIDDEN, PAIR_WIDTH), TRI_HIDDEN ** -0.5, 0.5),
    }


EPSILON = 1e-05

def norm_axis(values, gain, axis):
    average = lax.optimization_barrier(jnp.mean(values, axis=axis, keepdims=True))
    centred = values - average
    variance = lax.optimization_barrier(jnp.mean(centred * centred, axis=axis, keepdims=True))
    return centred * lax.rsqrt(variance + EPSILON) * gain

def triangle(current, mask_float, in_gain, proj_weight, gate_weight, out_gain, out_weight, outgoing):
    row_block = math.gcd(TOKENS, 64)
    block_count = TOKENS // row_block
    width = TRI_HIDDEN

    def project(block_index):
        offset = (block_index * row_block).astype(jnp.int32)
        cells = lax.dynamic_slice_in_dim(current, offset, row_block, 0).astype(jnp.float32)
        normed = norm_axis(cells, in_gain, -1).astype(jnp.bfloat16)
        flat = normed.reshape(row_block * TOKENS, PAIR_WIDTH)
        projected = jnp.dot(flat, proj_weight, preferred_element_type=jnp.float32).reshape(row_block, TOKENS, 4 * width)
        mask_rows = lax.dynamic_slice_in_dim(mask_float, offset, row_block, 0)
        pair_mask = (mask_rows[:, None] * mask_float[None, :])[:, :, None]
        left_proj = (jax.nn.sigmoid(projected[..., :width]) * projected[..., width:2 * width] * pair_mask).astype(jnp.bfloat16)
        right_proj = (jax.nn.sigmoid(projected[..., 2 * width:3 * width]) * projected[..., 3 * width:] * pair_mask).astype(jnp.bfloat16)
        gate_values = jax.nn.sigmoid(jnp.dot(flat, gate_weight, preferred_element_type=jnp.float32)).reshape(row_block, TOKENS, PAIR_WIDTH)
        return (left_proj, right_proj, gate_values)
    left_all, right_all, gate_all = lax.map(project, jnp.arange(block_count, dtype=jnp.int32))
    left_all = jnp.moveaxis(left_all.reshape(TOKENS, TOKENS, width), 2, 0)
    right_all = jnp.moveaxis(right_all.reshape(TOKENS, TOKENS, width), 2, 0)
    gate_all = gate_all.reshape(TOKENS, TOKENS, PAIR_WIDTH)
    chan_block = math.gcd(width, 8)

    def contract(block_index):
        offset = (block_index * chan_block).astype(jnp.int32)
        left_block = lax.dynamic_slice_in_dim(left_all, offset, chan_block, 0).astype(jnp.float32)
        right_block = lax.dynamic_slice_in_dim(right_all, offset, chan_block, 0).astype(jnp.float32)
        if outgoing:
            summed = jnp.einsum('cik,cjk->cij', left_block, right_block)
        else:
            summed = jnp.einsum('cki,ckj->cij', left_block, right_block)
        return summed.astype(jnp.bfloat16)
    product = lax.map(contract, jnp.arange(width // chan_block, dtype=jnp.int32)).reshape(width, TOKENS, TOKENS)

    def finish(block_index):
        offset = (block_index * row_block).astype(jnp.int32)
        hidden_block = lax.dynamic_slice_in_dim(product, offset, row_block, 1).astype(jnp.float32)
        normed_hidden = norm_axis(hidden_block, out_gain[:, None, None], 0)
        normed_hidden = lax.optimization_barrier(normed_hidden.astype(jnp.bfloat16)).astype(jnp.float32)
        update = jnp.einsum('hrq,hc->rqc', normed_hidden, out_weight.astype(jnp.float32))
        cells = lax.dynamic_slice_in_dim(current, offset, row_block, 0).astype(jnp.float32)
        gate_block = lax.dynamic_slice_in_dim(gate_all, offset, row_block, 0)
        return (cells + gate_block * update).astype(jnp.bfloat16)
    return lax.map(finish, jnp.arange(block_count, dtype=jnp.int32)).reshape(TOKENS, TOKENS, PAIR_WIDTH)

def reference(pair_input, token_mask, in_gain, proj_weight, gate_weight, out_gain, out_weight):
    mask_float = token_mask.astype(jnp.float32)
    current = pair_input
    for module_index in range(2):
        current = triangle(current, mask_float, in_gain[module_index], proj_weight[module_index], gate_weight[module_index], out_gain[module_index], out_weight[module_index], module_index == 0)
    return current
```

```python
import functools

import jax
import jax.numpy as jnp
from jax import lax
from jax.experimental import pallas as pl
from jax.experimental.pallas import tpu as pltpu
from jax.sharding import Mesh, PartitionSpec as P

EPSILON = 1e-05
CHAN = 128
ROWS = 32
COLS = 128
STEP = 16
SUB = 4
PEERS = ("xh", "z", "xl", "y")
F32 = jnp.float32
BF16 = jnp.bfloat16
PARAMS = pltpu.CompilerParams(vmem_limit_bytes=40 * 1024 * 1024)


def sigmoid(values):
    return 0.5 * jnp.tanh(0.5 * values) + 0.5


def whole(shape):
    return pl.BlockSpec(shape, lambda *_: (0,) * len(shape))


SMEM = pl.BlockSpec(memory_space=pltpu.SMEM)


def layer_norm_lanes(cells, factor):
    average = jnp.mean(cells, axis=-1, keepdims=True)
    centred = cells - average
    variance = jnp.mean(centred * centred, axis=-1, keepdims=True)
    return centred * lax.rsqrt(variance + EPSILON) * factor


def project_rows(rows, row_masks, gain_mask, weight_ref, left_scratch, right_scratch, first):
    normed = [
        layer_norm_lanes(row, gain_mask * row_mask).astype(BF16)
        for row, row_mask in zip(rows, row_masks)
    ]
    flat = jnp.concatenate(normed, axis=0)
    projected = lax.dot_general(
        weight_ref[...], flat, (((1,), (1,)), ((), ())), preferred_element_type=F32
    )
    left = sigmoid(projected[:CHAN]) * projected[CHAN : 2 * CHAN]
    right = sigmoid(projected[2 * CHAN : 3 * CHAN]) * projected[3 * CHAN :]
    for index in range(len(rows)):
        place = pl.ds((first + index) * CHAN, CHAN)
        lanes = slice(index * COLS, (index + 1) * COLS)
        left_scratch[place, :] = left[:, lanes]
        right_scratch[place, :] = right[:, lanes]


def emit_projections(left_scratch, right_scratch, out_ref):
    def body(chan, carry):
        place = pl.ds(chan, STEP, stride=CHAN)
        out_ref[chan, 0] = left_scratch[place, :].astype(BF16)
        out_ref[chan, 1] = right_scratch[place, :].astype(BF16)
        return carry

    lax.fori_loop(0, CHAN, body, 0, unroll=8)


def project_kernel(row_mask_ref, cells_ref, gain_mask_ref, weight_ref, out_ref, left_scratch, right_scratch):
    base = pl.program_id(0) * STEP
    for first in range(0, STEP, SUB):
        rows = [cells_ref[first + index].astype(F32) for index in range(SUB)]
        masks = [row_mask_ref[base + first + index] for index in range(SUB)]
        project_rows(rows, masks, gain_mask_ref[...], weight_ref, left_scratch, right_scratch, first)
    emit_projections(left_scratch, right_scratch, out_ref)


CELLS = pl.BlockSpec((STEP, COLS, CHAN), lambda step: (step, 0, 0))
PAIRS = pl.BlockSpec((CHAN, 2, STEP, COLS), lambda step: (0, 0, step, 0))
HIDDEN = pl.BlockSpec((CHAN, STEP, COLS), lambda step: (0, step, 0))
PROJ_SCRATCH = [pltpu.VMEM((STEP * CHAN, COLS), F32)] * 2


def project(cells, row_mask, gain_mask, weight):
    return pl.pallas_call(
        project_kernel,
        grid=(ROWS // STEP,),
        in_specs=[SMEM, CELLS, whole((COLS, CHAN)), whole((4 * CHAN, CHAN))],
        out_specs=PAIRS,
        out_shape=jax.ShapeDtypeStruct((CHAN, 2, ROWS, COLS), BF16),
        scratch_shapes=PROJ_SCRATCH,
        compiler_params=PARAMS,
        name="project",
    )(row_mask, cells, gain_mask, weight)


def gate_kernel(cells_ref, gain_ref, weight_ref, out_ref):
    cells = cells_ref[...].astype(F32).reshape(STEP * COLS, CHAN)
    normed = layer_norm_lanes(cells, gain_ref[...]).astype(BF16)
    gate = sigmoid(jnp.dot(normed, weight_ref[...], preferred_element_type=F32))
    out_ref[...] = gate.reshape(STEP, COLS, CHAN)


def output_gate(cells, gain, weight):
    return pl.pallas_call(
        gate_kernel,
        grid=(ROWS // STEP,),
        in_specs=[CELLS, whole((1, CHAN)), whole((CHAN, CHAN))],
        out_specs=CELLS,
        out_shape=jax.ShapeDtypeStruct((ROWS, COLS, CHAN), F32),
        compiler_params=PARAMS,
        cost_estimate=pl.CostEstimate(
            flops=2 * ROWS * COLS * CHAN * CHAN, bytes_accessed=3 << 20, transcendentals=ROWS * COLS * CHAN
        ),
        name="output_gate",
    )(cells, gain.reshape(1, CHAN), weight)


def normed_hidden_rows(gain_ref, hidden_ref, scratch):
    hidden = hidden_ref[...].astype(F32)
    average = jnp.mean(hidden, axis=0)
    centred = hidden - average[None]
    scale = lax.rsqrt(jnp.mean(centred * centred, axis=0) + EPSILON)

    def body(chan, carry):
        values = (hidden_ref[chan].astype(F32) - average) * scale * gain_ref[chan]
        scratch[pl.ds(pl.multiple_of(chan * STEP, STEP), STEP), :] = values
        return carry

    lax.fori_loop(0, CHAN, body, 0, unroll=8)


def updated_row(index, scratch, weight_ref, cells_ref, gate_ref):
    hidden = scratch[pl.ds(index, CHAN, stride=STEP), :].astype(BF16)
    update = lax.dot_general(
        hidden, weight_ref[...], (((0,), (0,)), ((), ())), preferred_element_type=F32
    )
    return (cells_ref[index].astype(F32) + gate_ref[index] * update).astype(BF16)


def finish_kernel(gain_ref, hidden_ref, cells_ref, gate_ref, weight_ref, out_ref, scratch):
    normed_hidden_rows(gain_ref, hidden_ref, scratch)
    for index in range(STEP):
        out_ref[index] = updated_row(index, scratch, weight_ref, cells_ref, gate_ref)


def finish(hidden, cells, gate, gain, weight):
    return pl.pallas_call(
        finish_kernel,
        grid=(ROWS // STEP,),
        in_specs=[SMEM, HIDDEN, CELLS, CELLS, whole((CHAN, CHAN))],
        out_specs=CELLS,
        out_shape=jax.ShapeDtypeStruct((ROWS, COLS, CHAN), BF16),
        scratch_shapes=[pltpu.VMEM((CHAN * STEP, COLS), F32)],
        compiler_params=PARAMS,
        name="finish",
    )(gain, hidden, cells, gate, weight)


def finish_project_kernel(
    gain_ref, row_mask_ref, hidden_ref, cells_ref, gate_ref, weight_ref, gain_mask_ref, proj_ref,
    cells_out, pairs_out, scratch, left_scratch, right_scratch,
):
    base = pl.program_id(0) * STEP
    normed_hidden_rows(gain_ref, hidden_ref, scratch)
    for first in range(0, STEP, SUB):
        rows = []
        for index in range(first, first + SUB):
            row = updated_row(index, scratch, weight_ref, cells_ref, gate_ref)
            cells_out[index] = row
            rows.append(row.astype(F32))
        masks = [row_mask_ref[base + first + index] for index in range(SUB)]
        project_rows(rows, masks, gain_mask_ref[...], proj_ref, left_scratch, right_scratch, first)
    emit_projections(left_scratch, right_scratch, pairs_out)


def finish_project(hidden, cells, gate, gain, weight, row_mask, gain_mask, proj):
    return pl.pallas_call(
        finish_project_kernel,
        grid=(ROWS // STEP,),
        in_specs=[
            SMEM, SMEM, HIDDEN, CELLS, CELLS, whole((CHAN, CHAN)), whole((COLS, CHAN)), whole((4 * CHAN, CHAN)),
        ],
        out_specs=[CELLS, PAIRS],
        out_shape=[
            jax.ShapeDtypeStruct((ROWS, COLS, CHAN), BF16),
            jax.ShapeDtypeStruct((CHAN, 2, ROWS, COLS), BF16),
        ],
        scratch_shapes=[pltpu.VMEM((CHAN * STEP, COLS), F32)] + PROJ_SCRATCH,
        compiler_params=PARAMS,
        name="finish_project",
    )(gain, row_mask, hidden, cells, gate, weight, gain_mask, proj)


GROUPS = 16
BLOCKS = 8
TOKENS = BLOCKS * COLS


def outgoing_kernel(core_ref, pairs_ref, other_ref, out_ref, left, right):
    core = core_ref[0]
    for block in range(BLOCKS):
        lanes = slice(block * COLS, (block + 1) * COLS)
        left[:, :, lanes] = pairs_ref[:, block, 0]
        right[:, core, :, lanes] = pairs_ref[:, block, 1]
        right[:, 1 - core, :, lanes] = other_ref[:, block]
    left_rows = left[...].reshape(GROUPS * ROWS, TOKENS)
    for block in range(0, BLOCKS, 2):
        groups = slice(block * 2, block * 2 + 4)
        product = lax.dot_general(
            left_rows,
            right[groups].reshape(2 * COLS, TOKENS),
            (((1,), (1,)), ((), ())),
            preferred_element_type=F32,
        ).astype(BF16)
        for half in range(2):
            out_ref[:, block + half] = product[:, half * COLS : (half + 1) * COLS].reshape(GROUPS, ROWS, COLS)


def outgoing(core, pairs, other):
    return pl.pallas_call(
        outgoing_kernel,
        in_specs=[SMEM, whole((GROUPS, BLOCKS, 2, ROWS, COLS)), whole((GROUPS, BLOCKS, ROWS, COLS))],
        out_specs=whole((GROUPS, BLOCKS, ROWS, COLS)),
        grid=(1,),
        out_shape=jax.ShapeDtypeStruct((GROUPS, BLOCKS, ROWS, COLS), BF16),
        scratch_shapes=[
            pltpu.VMEM((GROUPS, ROWS, TOKENS), BF16),
            pltpu.VMEM((GROUPS, 2, ROWS, TOKENS), BF16),
        ],
        compiler_params=PARAMS,
        name="outgoing",
    )(core, pairs, other)


def incoming_kernel(core_ref, left_ref, right_ref, send_ref, keep_ref, right, total):
    core = core_ref[0]

    @pl.when(pl.program_id(0) == 0)
    def _():
        for block in range(BLOCKS):
            lanes = slice(block * COLS, (block + 1) * COLS)
            right[:, lanes] = right_ref[:, block, 0].reshape(GROUPS * ROWS, COLS)

    total[...] = lax.dot_general(
        left_ref[:, 0, 0].reshape(GROUPS * ROWS, COLS),
        right[...],
        (((0,), (0,)), ((), ())),
        preferred_element_type=F32,
    ).reshape(4, ROWS, TOKENS)
    for half in range(2):
        send_ref[half] = total[2 * half + 1 - core].astype(BF16)
        keep_ref[half] = total[2 * half + core]


def incoming(core, pairs):
    part = pl.BlockSpec((2, ROWS, TOKENS), lambda step: (step, 0, 0))
    return pl.pallas_call(
        incoming_kernel,
        grid=(BLOCKS,),
        in_specs=[
            SMEM,
            pl.BlockSpec((GROUPS, 1, 1, ROWS, COLS), lambda step: (0, step, 0, 0, 0)),
            pl.BlockSpec((GROUPS, BLOCKS, 1, ROWS, COLS), lambda step: (0, 0, 1, 0, 0)),
        ],
        out_specs=[part, part],
        out_shape=[
            jax.ShapeDtypeStruct((GROUPS, ROWS, TOKENS), BF16),
            jax.ShapeDtypeStruct((GROUPS, ROWS, TOKENS), F32),
        ],
        scratch_shapes=[pltpu.VMEM((GROUPS * ROWS, TOKENS), BF16), pltpu.VMEM((4, ROWS, TOKENS), F32)],
        compiler_params=PARAMS,
        name="incoming",
    )(core, pairs, pairs)


def join_kernel(keep_ref, other_ref, out_ref):
    total = (keep_ref[...] + other_ref[...].astype(F32)).astype(BF16)
    for block in range(BLOCKS):
        out_ref[:, block] = total[:, :, block * COLS : (block + 1) * COLS]


def join(keep, other):
    part = pl.BlockSpec((4, ROWS, TOKENS), lambda step: (step, 0, 0))
    return pl.pallas_call(
        join_kernel,
        grid=(GROUPS // 4,),
        in_specs=[part, part],
        out_specs=pl.BlockSpec((4, BLOCKS, ROWS, COLS), lambda step: (step, 0, 0, 0)),
        out_shape=jax.ShapeDtypeStruct((GROUPS, BLOCKS, ROWS, COLS), BF16),
        compiler_params=PARAMS,
        name="join",
    )(keep, other)


def exchange(values):
    return lax.all_to_all(values, PEERS, split_axis=0, concat_axis=0, tiled=True)


def to_other_core(values):
    return lax.ppermute(values, "c", [(0, 1), (1, 0)])


def per_device(pair_input, token_mask, in_gain, proj_weight, gate_weight, out_gain, out_weight):
    mask = token_mask.astype(F32)
    core = lax.axis_index("c").astype(jnp.int32).reshape(1)
    row_mask = lax.dynamic_slice_in_dim(mask, lax.axis_index(("xh", "z", "c")) * ROWS, ROWS, 0)
    col_mask = lax.dynamic_slice_in_dim(mask, lax.axis_index(("xl", "y")) * COLS, COLS, 0)
    gain_mask = col_mask[None, :, None] * in_gain[:, None, :]
    proj = jnp.swapaxes(proj_weight, 1, 2)

    pairs = exchange(project(pair_input, row_mask, gain_mask[0], proj[0]))
    gate = output_gate(pair_input, in_gain[0], gate_weight[0])
    pairs = pairs.reshape(GROUPS, BLOCKS, 2, ROWS, COLS)
    other = to_other_core(pairs[:, :, 1])
    product = outgoing(core, pairs, other)
    hidden = exchange(product.reshape(CHAN, ROWS, COLS))
    cells, pairs = finish_project(
        hidden, pair_input, gate, out_gain[0], out_weight[0], row_mask, gain_mask[1], proj[1]
    )

    pairs = exchange(pairs)
    gate = output_gate(cells, in_gain[1], gate_weight[1])
    send, keep = incoming(core, pairs.reshape(GROUPS, BLOCKS, 2, ROWS, COLS))
    product = join(keep, to_other_core(send))
    hidden = exchange(product.reshape(CHAN, ROWS, COLS))
    return finish(hidden, cells, gate, out_gain[1], out_weight[1])


def solution(mesh):
    split = Mesh(mesh.devices.reshape(2, 8, 2, 2, 4), ("xh", "z", "c", "xl", "y"))
    cells = P(("xh", "z", "c"), ("xl", "y"), None)
    return jax.shard_map(
        per_device, mesh=split, in_specs=(cells, P(), P(), P(), P(), P(), P()), out_specs=cells, check_vma=False
    )
```

```python
import functools

import jax
import jax.numpy as jnp
from jax import lax
from jax.experimental import pallas as pl
from jax.experimental.pallas import tpu as pltpu
from jax.sharding import Mesh, PartitionSpec as P

EPSILON = 1e-05
CHAN = 128
ROWS = 32
COLS = 128
SUB = 4
CHAN_PITCH = CHAN + 1
ROW_PITCH = ROWS + 1
PEERS = ("xh", "z", "xl", "y")
F32 = jnp.float32
BF16 = jnp.bfloat16
PARAMS = pltpu.CompilerParams(vmem_limit_bytes=40 * 1024 * 1024)


def sigmoid(values):
    return 0.5 * jnp.tanh(0.5 * values) + 0.5


SMEM = pl.BlockSpec(memory_space=pltpu.SMEM)
VMEM = pl.BlockSpec(memory_space=pltpu.VMEM)


def kernel_call(kernel, name, in_specs, out_shape, scratch_shapes=(), cost=None):
    return pl.pallas_call(
        kernel,
        in_specs=in_specs,
        out_specs=jax.tree.map(lambda _: VMEM, out_shape),
        out_shape=out_shape,
        scratch_shapes=scratch_shapes,
        compiler_params=PARAMS,
        cost_estimate=cost,
        name=name,
    )


def layer_norm_lanes(cells, factor):
    average = jnp.mean(cells, axis=-1, keepdims=True)
    centred = cells - average
    variance = jnp.mean(centred * centred, axis=-1, keepdims=True)
    return centred * lax.rsqrt(variance + EPSILON) * factor


def masked_gain(place_ref, gain_ref, module, col_mask_ref):
    cols = col_mask_ref[pl.ds(place_ref[1], 1), :].astype(F32)
    return jnp.transpose(jnp.broadcast_to(cols, (CHAN, COLS))) * gain_ref[module : module + 1, :]


def row_mask(place_ref, row_mask_ref, index):
    return row_mask_ref[place_ref[0] + index].astype(F32)


def project_rows(rows, row_masks, gain_mask, weight_ref, left_scratch, right_scratch, first):
    normed = [
        layer_norm_lanes(row, gain_mask * mask).astype(BF16) for row, mask in zip(rows, row_masks)
    ]
    projected = lax.dot_general(
        weight_ref[...], jnp.concatenate(normed, axis=0), (((1,), (1,)), ((), ())), preferred_element_type=F32
    )
    left = sigmoid(projected[:CHAN]) * projected[CHAN : 2 * CHAN]
    right = sigmoid(projected[2 * CHAN : 3 * CHAN]) * projected[3 * CHAN :]
    for index in range(len(rows)):
        place = pl.ds((first + index) * CHAN_PITCH, CHAN)
        lanes = slice(index * COLS, (index + 1) * COLS)
        left_scratch[place, :] = left[:, lanes]
        right_scratch[place, :] = right[:, lanes]


def emit_projections(left_scratch, right_scratch, out_ref):
    def body(chan, carry):
        place = pl.ds(chan, ROWS, stride=CHAN_PITCH)
        out_ref[chan, 0] = left_scratch[place, :].astype(BF16)
        out_ref[chan, 1] = right_scratch[place, :].astype(BF16)
        return carry

    lax.fori_loop(0, CHAN, body, 0, unroll=8)


def project_kernel(place_ref, row_mask_ref, col_mask_ref, gain_ref, cells_ref, weight_ref, out_ref, left, right):
    gain_mask = masked_gain(place_ref, gain_ref, 0, col_mask_ref)
    for first in range(0, ROWS, SUB):
        rows = [cells_ref[first + index].astype(F32) for index in range(SUB)]
        masks = [row_mask(place_ref, row_mask_ref, first + index) for index in range(SUB)]
        project_rows(rows, masks, gain_mask, weight_ref, left, right, first)
    emit_projections(left, right, out_ref)


PROJ_SCRATCH = [pltpu.VMEM((ROWS * CHAN_PITCH, COLS), F32)] * 2
PAIRS = jax.ShapeDtypeStruct((CHAN, 2, ROWS, COLS), BF16)
CELLS = jax.ShapeDtypeStruct((ROWS, COLS, CHAN), BF16)


def project(place, mask, mask_rows, gain, cells, weight):
    call = kernel_call(
        project_kernel, "project", [SMEM, SMEM, VMEM, VMEM, VMEM, VMEM], PAIRS, PROJ_SCRATCH
    )
    return call(place, mask, mask_rows, gain, cells, weight)


def gate_kernel(module, gain_ref, cells_ref, weight_ref, out_ref):
    for first in range(0, ROWS, SUB):
        cells = cells_ref[first : first + SUB].astype(F32).reshape(SUB * COLS, CHAN)
        normed = layer_norm_lanes(cells, gain_ref[module : module + 1, :]).astype(BF16)
        gate = sigmoid(jnp.dot(normed, weight_ref[module], preferred_element_type=F32))
        out_ref[first : first + SUB] = gate.reshape(SUB, COLS, CHAN)


def output_gate(module, gain, cells, weight):
    call = kernel_call(
        functools.partial(gate_kernel, module),
        "output_gate",
        [VMEM, VMEM, VMEM],
        jax.ShapeDtypeStruct((ROWS, COLS, CHAN), F32),
        cost=pl.CostEstimate(
            flops=2 * ROWS * COLS * CHAN * CHAN, bytes_accessed=3 << 20, transcendentals=ROWS * COLS * CHAN
        ),
    )
    return call(gain, cells, weight)


def normed_hidden_rows(module, gain_ref, hidden_ref, scratch):
    for first in range(0, ROWS, 16):
        rows = slice(first, first + 16)
        hidden = hidden_ref[:, rows].astype(F32)
        average = jnp.mean(hidden, axis=0)
        centred = hidden - average[None]
        scale = lax.rsqrt(jnp.mean(centred * centred, axis=0) + EPSILON)

        def body(chan, carry):
            values = (hidden_ref[chan, rows].astype(F32) - average) * scale * gain_ref[module, chan]
            scratch[pl.ds(chan * ROW_PITCH + first, 16), :] = values
            return carry

        lax.fori_loop(0, CHAN, body, 0, unroll=8)


def updated_row(module, index, scratch, weight_ref, cells_ref, gate_ref):
    hidden = scratch[pl.ds(index, CHAN, stride=ROW_PITCH), :].astype(BF16)
    update = lax.dot_general(
        hidden, weight_ref[module], (((0,), (0,)), ((), ())), preferred_element_type=F32
    )
    return (cells_ref[index].astype(F32) + gate_ref[index] * update).astype(BF16)


HIDDEN_SCRATCH = pltpu.VMEM((CHAN * ROW_PITCH, COLS), F32)


def finish_kernel(gain_ref, hidden_ref, cells_ref, gate_ref, weight_ref, out_ref, scratch):
    normed_hidden_rows(1, gain_ref, hidden_ref, scratch)
    for index in range(ROWS):
        out_ref[index] = updated_row(1, index, scratch, weight_ref, cells_ref, gate_ref)


def finish(gain, hidden, cells, gate, weight):
    call = kernel_call(finish_kernel, "finish", [SMEM, VMEM, VMEM, VMEM, VMEM], CELLS, [HIDDEN_SCRATCH])
    return call(gain, hidden, cells, gate, weight)


def finish_project_kernel(
    place_ref, row_mask_ref, col_mask_ref, in_gain_ref, out_gain_ref, hidden_ref, cells_ref, gate_ref,
    weight_ref, proj_ref, cells_out, pairs_out, scratch, left, right,
):
    gain_mask = masked_gain(place_ref, in_gain_ref, 1, col_mask_ref)
    normed_hidden_rows(0, out_gain_ref, hidden_ref, scratch)
    for first in range(0, ROWS, SUB):
        rows = []
        for index in range(first, first + SUB):
            row = updated_row(0, index, scratch, weight_ref, cells_ref, gate_ref)
            cells_out[index] = row
            rows.append(row.astype(F32))
        masks = [row_mask(place_ref, row_mask_ref, first + index) for index in range(SUB)]
        project_rows(rows, masks, gain_mask, proj_ref, left, right, first)
    emit_projections(left, right, pairs_out)


def finish_project(place, mask, mask_rows, in_gain, out_gain, hidden, cells, gate, weight, proj):
    call = kernel_call(
        finish_project_kernel,
        "finish_project",
        [SMEM, SMEM, VMEM, VMEM, SMEM] + [VMEM] * 5,
        [CELLS, PAIRS],
        [HIDDEN_SCRATCH] + PROJ_SCRATCH,
    )
    return call(place, mask, mask_rows, in_gain, out_gain, hidden, cells, gate, weight, proj)


GROUPS = 16
BLOCKS = 8
TOKENS = BLOCKS * COLS
HALF = GROUPS * ROWS
PRODUCT = jax.ShapeDtypeStruct((GROUPS, BLOCKS, ROWS, COLS), BF16)


def block_lanes(block):
    return slice(block * COLS, (block + 1) * COLS)


def outgoing_kernel(place_ref, pairs_ref, other_ref, out_ref, left, right):
    core = place_ref[2]
    for block in range(BLOCKS):
        left[:, :, block_lanes(block)] = pairs_ref[:, block, 0]
        right[:, core, :, block_lanes(block)] = pairs_ref[:, block, 1]
        right[:, 1 - core, :, block_lanes(block)] = other_ref[:, block]
    left_rows = left[...].reshape(HALF, TOKENS)
    for block in range(0, BLOCKS, 2):
        groups = slice(block * 2, block * 2 + 4)
        product = lax.dot_general(
            left_rows,
            right[groups].reshape(2 * COLS, TOKENS),
            (((1,), (1,)), ((), ())),
            preferred_element_type=F32,
        ).astype(BF16)
        for half in range(2):
            out_ref[:, block + half] = product[:, block_lanes(half)].reshape(GROUPS, ROWS, COLS)


def outgoing(place, pairs, other):
    call = kernel_call(
        outgoing_kernel,
        "outgoing",
        [SMEM, VMEM, VMEM],
        PRODUCT,
        [pltpu.VMEM((GROUPS, ROWS, TOKENS), BF16), pltpu.VMEM((GROUPS, 2, ROWS, TOKENS), BF16)],
    )
    return call(place, pairs, other)


def incoming_send_kernel(place_ref, pairs_ref, send_ref, left_ref, right_ref, turned):
    core = place_ref[2]
    for block in range(BLOCKS):
        right_ref[:, block_lanes(block)] = pairs_ref[:, block, 1].reshape(HALF, COLS)
        left = pairs_ref[:, block, 0].reshape(HALF, COLS)
        turned[2 * block : 2 * block + 2] = jnp.transpose(left).reshape(2, 2, ROWS, HALF)
    left_ref[...] = turned[:, core].reshape(HALF, HALF)
    send_ref[...] = jnp.dot(
        turned[:, 1 - core].reshape(HALF, HALF), right_ref[...], preferred_element_type=F32
    ).astype(BF16)


def incoming_send(place, pairs):
    call = kernel_call(
        incoming_send_kernel,
        "incoming_send",
        [SMEM, VMEM],
        [
            jax.ShapeDtypeStruct((HALF, TOKENS), BF16),
            jax.ShapeDtypeStruct((HALF, HALF), BF16),
            jax.ShapeDtypeStruct((HALF, TOKENS), BF16),
        ],
        [pltpu.VMEM((GROUPS, 2, ROWS, HALF), BF16)],
    )
    return call(place, pairs)


def incoming_kernel(left_ref, right_ref, other_ref, out_ref):
    left = left_ref[...]
    for block in range(0, BLOCKS, 2):
        lanes = slice(block * COLS, (block + 2) * COLS)
        total = jnp.dot(left, right_ref[:, lanes], preferred_element_type=F32)
        product = (total + other_ref[:, lanes].astype(F32)).astype(BF16)
        for half in range(2):
            out_ref[:, block + half] = product[:, block_lanes(half)].reshape(GROUPS, ROWS, COLS)


def incoming(left, right, other):
    return kernel_call(incoming_kernel, "incoming", [VMEM, VMEM, VMEM], PRODUCT)(left, right, other)


def exchange(values):
    return lax.all_to_all(values, PEERS, split_axis=0, concat_axis=0, tiled=True)


def to_other_core(values):
    return lax.ppermute(values, "c", [(0, 1), (1, 0)])


def per_device(pair_input, token_mask, in_gain, proj_weight, gate_weight, out_gain, out_weight):
    place = jnp.stack(
        [lax.axis_index(("xh", "z", "c")) * ROWS, lax.axis_index(("xl", "y")), lax.axis_index("c")]
    ).astype(jnp.int32)
    masks = (place, token_mask, token_mask.reshape(BLOCKS, COLS))
    proj = jnp.swapaxes(proj_weight, 1, 2)

    pairs = exchange(project(*masks, in_gain, pair_input, proj[0])).reshape(GROUPS, BLOCKS, 2, ROWS, COLS)
    other = to_other_core(pairs[:, :, 1])
    gate = output_gate(0, in_gain, pair_input, gate_weight)
    product, gate = lax.optimization_barrier((outgoing(place, pairs, other), gate))
    hidden = exchange(product.reshape(CHAN, ROWS, COLS))
    cells, pairs = finish_project(
        *masks, in_gain, out_gain, hidden, pair_input, gate, out_weight, proj[1]
    )

    pairs = exchange(pairs).reshape(GROUPS, BLOCKS, 2, ROWS, COLS)
    send, left, right = incoming_send(place, pairs)
    other = to_other_core(send)
    gate = output_gate(1, in_gain, cells, gate_weight)
    product, gate = lax.optimization_barrier((incoming(left, right, other), gate))
    hidden = exchange(product.reshape(CHAN, ROWS, COLS))
    return finish(out_gain, hidden, cells, gate, out_weight)


def solution(mesh):
    split = Mesh(mesh.devices.reshape(2, 8, 2, 2, 4), ("xh", "z", "c", "xl", "y"))
    cells = P(("xh", "z", "c"), ("xl", "y"), None)
    return jax.shard_map(
        per_device, mesh=split, in_specs=(cells, P(), P(), P(), P(), P(), P()), out_specs=cells, check_vma=False
    )
```

```python
import functools

import jax
import jax.numpy as jnp
from jax import lax
from jax.experimental import pallas as pl
from jax.experimental.pallas import tpu as pltpu
from jax.sharding import Mesh, PartitionSpec as P

EPSILON = 1e-05
CHAN = 128
ROWS = 32
COLS = 128
SUB = 4
CHUNK = 8
CHAN_PITCH = CHAN + 1
ROW_PITCH = ROWS + 1
PEERS = ("xh", "z", "xl", "y")
F32 = jnp.float32
BF16 = jnp.bfloat16
MIB = 1024 * 1024


def sigmoid(values):
    return 0.5 * jnp.tanh(0.5 * values) + 0.5


SMEM = pl.BlockSpec(memory_space=pltpu.SMEM)
VMEM = pl.BlockSpec(memory_space=pltpu.VMEM)


def kernel_call(kernel, name, in_specs, out_shape, scratch_shapes=(), cost=None, vmem=40):
    return pl.pallas_call(
        kernel,
        in_specs=in_specs,
        out_specs=jax.tree.map(lambda _: VMEM, out_shape),
        out_shape=out_shape,
        scratch_shapes=scratch_shapes,
        compiler_params=pltpu.CompilerParams(vmem_limit_bytes=vmem * MIB),
        cost_estimate=cost,
        name=name,
    )


HBM = pl.BlockSpec(memory_space=pltpu.HBM)
PROJ_SCRATCH = [pltpu.VMEM((ROWS * CHAN_PITCH, COLS), F32)] * 2
HIDDEN_SCRATCH = pltpu.VMEM((CHAN * ROW_PITCH, COLS), F32)
PAIRS = jax.ShapeDtypeStruct((CHAN, 2, ROWS, COLS), BF16)
CELLS = jax.ShapeDtypeStruct((ROWS, COLS, CHAN), BF16)
TURNED = jax.ShapeDtypeStruct((ROWS, CHAN, COLS), BF16)
GATE = jax.ShapeDtypeStruct((ROWS, CHAN, COLS), F32)


def layer_norm(turned, factor):
    average = jnp.mean(turned, axis=0, keepdims=True)
    centred = turned - average
    variance = jnp.mean(centred * centred, axis=0, keepdims=True)
    return centred * lax.rsqrt(variance + EPSILON) * factor


def channel_column(gain_ref, module):
    return jnp.transpose(jnp.broadcast_to(gain_ref[module : module + 1, :], (COLS, CHAN)))


def masked_gain(place_ref, gain_ref, module, col_mask_ref):
    return channel_column(gain_ref, module) * col_mask_ref[pl.ds(place_ref[1], 1), :].astype(F32)


def row_mask(place_ref, row_mask_ref, index):
    return row_mask_ref[place_ref[0] + index].astype(F32)


def project_rows(rows, row_masks, gain_mask, weight, left_scratch, right_scratch, first):
    normed = [layer_norm(row, gain_mask * mask).astype(BF16) for row, mask in zip(rows, row_masks)]
    projected = jnp.dot(weight[...], jnp.concatenate(normed, axis=1), preferred_element_type=F32)
    left = sigmoid(projected[:CHAN]) * projected[CHAN : 2 * CHAN]
    right = sigmoid(projected[2 * CHAN : 3 * CHAN]) * projected[3 * CHAN :]
    for index in range(len(rows)):
        place = pl.ds((first + index) * CHAN_PITCH, CHAN)
        lanes = slice(index * COLS, (index + 1) * COLS)
        left_scratch[place, :] = left[:, lanes]
        right_scratch[place, :] = right[:, lanes]


def emit_projections(left_scratch, right_scratch, out_ref):
    def body(chan, carry):
        place = pl.ds(chan, ROWS, stride=CHAN_PITCH)
        out_ref[chan, 0] = left_scratch[place, :].astype(BF16)
        out_ref[chan, 1] = right_scratch[place, :].astype(BF16)
        return carry

    lax.fori_loop(0, CHAN, body, 0, unroll=8)


def project_kernel(
    place_ref, row_mask_ref, col_mask_hbm, gain_hbm, cells_hbm, weight_hbm, out_ref, turned_out,
    cells_ref, weight_ref, col_mask_ref, gain_ref, weight_turned, left, right, sems,
):
    cell_copies = [
        pltpu.make_async_copy(
            cells_hbm.at[pl.ds(first, CHUNK)], cells_ref.at[pl.ds(first, CHUNK)], sems.at[first // CHUNK]
        )
        for first in range(0, ROWS, CHUNK)
    ]
    small_copies = [
        pltpu.make_async_copy(weight_hbm.at[0], weight_ref, sems.at[ROWS // CHUNK]),
        pltpu.make_async_copy(col_mask_hbm, col_mask_ref, sems.at[ROWS // CHUNK + 1]),
        pltpu.make_async_copy(gain_hbm, gain_ref, sems.at[ROWS // CHUNK + 2]),
    ]
    for copy in small_copies + cell_copies:
        copy.start()
    for copy in small_copies:
        copy.wait()
    gain_mask = masked_gain(place_ref, gain_ref, 0, col_mask_ref)
    weight_turned[...] = jnp.transpose(weight_ref[...])
    for first in range(0, ROWS, SUB):
        if first % CHUNK == 0:
            cell_copies[first // CHUNK].wait()
        rows = []
        for index in range(first, first + SUB):
            row = jnp.transpose(cells_ref[index])
            turned_out[index] = row
            rows.append(row.astype(F32))
        masks = [row_mask(place_ref, row_mask_ref, first + index) for index in range(SUB)]
        project_rows(rows, masks, gain_mask, weight_turned, left, right, first)
    emit_projections(left, right, out_ref)


def project(place, mask, mask_rows, gain, cells, weight):
    call = kernel_call(
        project_kernel,
        "project",
        [SMEM, SMEM, HBM, HBM, HBM, HBM],
        [PAIRS, TURNED],
        [
            pltpu.VMEM((ROWS, COLS, CHAN), BF16),
            pltpu.VMEM((CHAN, 4 * CHAN), BF16),
            pltpu.VMEM(mask_rows.shape, jnp.int32),
            pltpu.VMEM(gain.shape, F32),
            pltpu.VMEM((4 * CHAN, CHAN), BF16),
        ]
        + PROJ_SCRATCH
        + [pltpu.SemaphoreType.DMA((ROWS // CHUNK + 3,))],
        vmem=56,
    )
    return call(place, mask, mask_rows, gain, cells, weight)


def gate_kernel(module, gain_ref, cells_ref, weight_ref, out_ref):
    gain = channel_column(gain_ref, module)
    weight = jnp.transpose(weight_ref[module])
    for first in range(0, ROWS, SUB):
        rows = [layer_norm(cells_ref[first + index].astype(F32), gain).astype(BF16) for index in range(SUB)]
        gate = sigmoid(jnp.dot(weight, jnp.concatenate(rows, axis=1), preferred_element_type=F32))
        for index in range(SUB):
            out_ref[first + index] = gate[:, index * COLS : (index + 1) * COLS]


def output_gate(module, gain, cells, weight):
    call = kernel_call(
        functools.partial(gate_kernel, module),
        "output_gate",
        [VMEM, VMEM, VMEM],
        GATE,
        cost=pl.CostEstimate(
            flops=2 * ROWS * COLS * CHAN * CHAN, bytes_accessed=3 << 20, transcendentals=ROWS * COLS * CHAN
        ),
    )
    return call(gain, cells, weight)


def normed_hidden_rows(module, gain_ref, hidden_ref, scratch):
    for first in range(0, ROWS, 16):
        rows = slice(first, first + 16)
        hidden = hidden_ref[:, rows].astype(F32)
        average = jnp.mean(hidden, axis=0)
        centred = hidden - average[None]
        scale = lax.rsqrt(jnp.mean(centred * centred, axis=0) + EPSILON)

        def body(chan, carry):
            values = (hidden_ref[chan, rows].astype(F32) - average) * scale * gain_ref[module, chan]
            scratch[pl.ds(chan * ROW_PITCH + first, 16), :] = values
            return carry

        lax.fori_loop(0, CHAN, body, 0, unroll=8)


def updated_rows(first, scratch, weight, cells_ref, gate_ref):
    hidden = [
        scratch[pl.ds(first + index, CHAN, stride=ROW_PITCH), :].astype(BF16) for index in range(SUB)
    ]
    update = jnp.dot(weight, jnp.concatenate(hidden, axis=1), preferred_element_type=F32)
    return [
        (
            cells_ref[first + index].astype(F32)
            + gate_ref[first + index] * update[:, index * COLS : (index + 1) * COLS]
        ).astype(BF16)
        for index in range(SUB)
    ]


def finish_kernel(gain_ref, hidden_ref, cells_ref, gate_ref, weight_ref, out_hbm, scratch, out_ref, sems):
    normed_hidden_rows(1, gain_ref, hidden_ref, scratch)
    weight = jnp.transpose(weight_ref[1])
    copies = []
    for first in range(0, ROWS, SUB):
        for index, row in enumerate(updated_rows(first, scratch, weight, cells_ref, gate_ref)):
            out_ref[first + index] = jnp.transpose(row)
        if (first + SUB) % CHUNK == 0:
            rows = pl.ds(first + SUB - CHUNK, CHUNK)
            copies.append(pltpu.make_async_copy(out_ref.at[rows], out_hbm.at[rows], sems.at[first // CHUNK]))
            copies[-1].start()
    for copy in copies:
        copy.wait()


def finish(gain, hidden, cells, gate, weight):
    return pl.pallas_call(
        finish_kernel,
        in_specs=[SMEM, VMEM, VMEM, VMEM, VMEM],
        out_specs=HBM,
        out_shape=CELLS,
        scratch_shapes=[
            HIDDEN_SCRATCH,
            pltpu.VMEM((ROWS, COLS, CHAN), BF16),
            pltpu.SemaphoreType.DMA((ROWS // CHUNK,)),
        ],
        compiler_params=pltpu.CompilerParams(vmem_limit_bytes=40 * MIB),
        name="finish",
    )(gain, hidden, cells, gate, weight)


def finish_project_kernel(
    place_ref, row_mask_ref, col_mask_ref, in_gain_ref, out_gain_ref, hidden_ref, cells_ref, gate_ref,
    weight_ref, proj_ref, cells_out, pairs_out, scratch, proj_turned, left, right,
):
    gain_mask = masked_gain(place_ref, in_gain_ref, 1, col_mask_ref)
    normed_hidden_rows(0, out_gain_ref, hidden_ref, scratch)
    weight = jnp.transpose(weight_ref[0])
    proj_turned[...] = jnp.transpose(proj_ref[1])
    for first in range(0, ROWS, SUB):
        rows = updated_rows(first, scratch, weight, cells_ref, gate_ref)
        for index, row in enumerate(rows):
            cells_out[first + index] = row
        masks = [row_mask(place_ref, row_mask_ref, first + index) for index in range(SUB)]
        rows = [row.astype(F32) for row in rows]
        project_rows(rows, masks, gain_mask, proj_turned, left, right, first)
    emit_projections(left, right, pairs_out)


def finish_project(place, mask, mask_rows, in_gain, out_gain, hidden, cells, gate, weight, proj):
    call = kernel_call(
        finish_project_kernel,
        "finish_project",
        [SMEM, SMEM, VMEM, VMEM, SMEM] + [VMEM] * 5,
        [TURNED, PAIRS],
        [HIDDEN_SCRATCH, pltpu.VMEM((4 * CHAN, CHAN), BF16)] + PROJ_SCRATCH,
    )
    return call(place, mask, mask_rows, in_gain, out_gain, hidden, cells, gate, weight, proj)


GROUPS = 16
BLOCKS = 8
TOKENS = BLOCKS * COLS
HALF = GROUPS * ROWS
PRODUCT = jax.ShapeDtypeStruct((GROUPS, BLOCKS, ROWS, COLS), BF16)


def block_lanes(block):
    return slice(block * COLS, (block + 1) * COLS)


def outgoing_kernel(place_ref, pairs_ref, other_ref, out_ref, left, right):
    core = place_ref[2]
    for block in range(BLOCKS):
        left[:, :, block_lanes(block)] = pairs_ref[:, block, 0]
        right[:, core, :, block_lanes(block)] = pairs_ref[:, block, 1]
        right[:, 1 - core, :, block_lanes(block)] = other_ref[:, block]
    left_rows = left[...].reshape(HALF, TOKENS)
    for block in range(0, BLOCKS, 2):
        groups = slice(block * 2, block * 2 + 4)
        product = lax.dot_general(
            left_rows,
            right[groups].reshape(2 * COLS, TOKENS),
            (((1,), (1,)), ((), ())),
            preferred_element_type=F32,
        ).astype(BF16)
        for half in range(2):
            out_ref[:, block + half] = product[:, block_lanes(half)].reshape(GROUPS, ROWS, COLS)


def outgoing(place, pairs, other):
    call = kernel_call(
        outgoing_kernel,
        "outgoing",
        [SMEM, VMEM, VMEM],
        PRODUCT,
        [pltpu.VMEM((GROUPS, ROWS, TOKENS), BF16), pltpu.VMEM((GROUPS, 2, ROWS, TOKENS), BF16)],
    )
    return call(place, pairs, other)


def incoming_send_kernel(place_ref, pairs_ref, send_ref, left_ref, right_ref, turned):
    core = place_ref[2]
    for block in range(BLOCKS):
        right_ref[:, block_lanes(block)] = pairs_ref[:, block, 1].reshape(HALF, COLS)
        left = pairs_ref[:, block, 0].reshape(HALF, COLS)
        turned[2 * block : 2 * block + 2] = jnp.transpose(left).reshape(2, 2, ROWS, HALF)
    left_ref[...] = turned[:, core].reshape(HALF, HALF)
    send_ref[...] = jnp.dot(
        turned[:, 1 - core].reshape(HALF, HALF), right_ref[...], preferred_element_type=F32
    ).astype(BF16)


def incoming_send(place, pairs):
    call = kernel_call(
        incoming_send_kernel,
        "incoming_send",
        [SMEM, VMEM],
        [
            jax.ShapeDtypeStruct((HALF, TOKENS), BF16),
            jax.ShapeDtypeStruct((HALF, HALF), BF16),
            jax.ShapeDtypeStruct((HALF, TOKENS), BF16),
        ],
        [pltpu.VMEM((GROUPS, 2, ROWS, HALF), BF16)],
    )
    return call(place, pairs)


def incoming_kernel(left_ref, right_ref, other_ref, out_ref):
    left = left_ref[...]
    for block in range(0, BLOCKS, 2):
        lanes = slice(block * COLS, (block + 2) * COLS)
        total = jnp.dot(left, right_ref[:, lanes], preferred_element_type=F32)
        product = (total + other_ref[:, lanes].astype(F32)).astype(BF16)
        for half in range(2):
            out_ref[:, block + half] = product[:, block_lanes(half)].reshape(GROUPS, ROWS, COLS)


def incoming(left, right, other):
    return kernel_call(incoming_kernel, "incoming", [VMEM, VMEM, VMEM], PRODUCT)(left, right, other)


def exchange(values):
    return lax.all_to_all(values, PEERS, split_axis=0, concat_axis=0, tiled=True)


def to_other_core(values):
    return lax.ppermute(values, "c", [(0, 1), (1, 0)])


def per_device(pair_input, token_mask, in_gain, proj_weight, gate_weight, out_gain, out_weight):
    place = jnp.stack(
        [lax.axis_index(("xh", "z", "c")) * ROWS, lax.axis_index(("xl", "y")), lax.axis_index("c")]
    ).astype(jnp.int32)
    masks = (place, token_mask, token_mask.reshape(BLOCKS, COLS))

    pairs, cells = project(*masks, in_gain, pair_input, proj_weight)
    pairs = exchange(pairs).reshape(GROUPS, BLOCKS, 2, ROWS, COLS)
    other = to_other_core(pairs[:, :, 1])
    gate = output_gate(0, in_gain, cells, gate_weight)
    product, gate = lax.optimization_barrier((outgoing(place, pairs, other), gate))
    hidden = exchange(product.reshape(CHAN, ROWS, COLS))
    cells, pairs = finish_project(*masks, in_gain, out_gain, hidden, cells, gate, out_weight, proj_weight)

    pairs = exchange(pairs).reshape(GROUPS, BLOCKS, 2, ROWS, COLS)
    send, left, right = incoming_send(place, pairs)
    other = to_other_core(send)
    gate = output_gate(1, in_gain, cells, gate_weight)
    product, gate = lax.optimization_barrier((incoming(left, right, other), gate))
    hidden = exchange(product.reshape(CHAN, ROWS, COLS))
    return finish(out_gain, hidden, cells, gate, out_weight)


def solution(mesh):
    split = Mesh(mesh.devices.reshape(2, 8, 2, 2, 4), ("xh", "z", "c", "xl", "y"))
    cells = P(("xh", "z", "c"), ("xl", "y"), None)
    return jax.shard_map(
        per_device, mesh=split, in_specs=(cells, P(), P(), P(), P(), P(), P()), out_specs=cells, check_vma=False
    )
```

```python
import functools

import jax
import jax.numpy as jnp
from jax import lax
from jax.experimental import pallas as pl
from jax.experimental.pallas import tpu as pltpu
from jax.sharding import Mesh, PartitionSpec as P

EPSILON = 1e-05
CHAN = 128
ROWS = 32
COLS = 128
SUB = 16
CHUNK = 16
SPAN = 32
CHAN_PITCH = CHAN + 1
ROW_PITCH = ROWS + 1
PEERS = ("xh", "z", "xl", "y")
F32 = jnp.float32
BF16 = jnp.bfloat16
MIB = 1024 * 1024


def sigmoid(values):
    return 0.5 * jnp.tanh(0.5 * values) + 0.5


VMEM = pl.BlockSpec(memory_space=pltpu.VMEM)


def kernel_call(kernel, name, in_specs, out_shape, scratch_shapes=(), cost=None, vmem=40):
    return pl.pallas_call(
        kernel,
        in_specs=in_specs,
        out_specs=jax.tree.map(lambda _: VMEM, out_shape),
        out_shape=out_shape,
        scratch_shapes=scratch_shapes,
        compiler_params=pltpu.CompilerParams(vmem_limit_bytes=vmem * MIB),
        cost_estimate=cost,
        name=name,
    )


HBM = pl.BlockSpec(memory_space=pltpu.HBM)
PROJ_SCRATCH = [pltpu.VMEM((COLS, COLS), F32)] + [pltpu.VMEM((ROWS * CHAN_PITCH, COLS), F32)] * 2
HIDDEN_SCRATCH = [pltpu.VMEM((CHAN, COLS), F32), pltpu.VMEM((CHAN * ROW_PITCH, COLS), F32)]
PAIRS = jax.ShapeDtypeStruct((CHAN, 2, ROWS, COLS), BF16)
CELLS = jax.ShapeDtypeStruct((ROWS, COLS, CHAN), BF16)
TURNED = jax.ShapeDtypeStruct((ROWS, CHAN, COLS), BF16)
GATE = jax.ShapeDtypeStruct((ROWS, CHAN, COLS), F32)


def layer_norm(turned, factor):
    average = jnp.mean(turned, axis=0, keepdims=True)
    centred = turned - average
    variance = jnp.mean(centred * centred, axis=0, keepdims=True)
    return centred * lax.rsqrt(variance + EPSILON) * factor


def channel_column(gain_ref, module):
    return jnp.transpose(jnp.broadcast_to(gain_ref[module : module + 1, :], (COLS, CHAN)))


def masked_gain(gain_ref, module, col_mask_ref):
    block = lax.axis_index(("xl", "y"))
    return channel_column(gain_ref, module) * col_mask_ref[pl.ds(block, 1), :].astype(F32)


def set_row_masks(mask_ref, scratch):
    block = lax.axis_index(("xh", "z", "c")) // (COLS // ROWS)
    tokens = jnp.broadcast_to(mask_ref[pl.ds(block, 1), :].astype(F32), (COLS, COLS))
    scratch[...] = jnp.transpose(tokens)


def row_mask(scratch, index):
    start = lax.axis_index(("xh", "z", "c")) % (COLS // ROWS) * ROWS
    return scratch[pl.ds(start + index, 1), :]


def project_rows(rows, row_masks, gain_mask, weight, left_scratch, right_scratch, first):
    normed = [layer_norm(row, gain_mask * mask).astype(BF16) for row, mask in zip(rows, row_masks)]
    projected = jnp.dot(weight[...], jnp.concatenate(normed, axis=1), preferred_element_type=F32)
    left = sigmoid(projected[:CHAN]) * projected[CHAN : 2 * CHAN]
    right = sigmoid(projected[2 * CHAN : 3 * CHAN]) * projected[3 * CHAN :]
    for index in range(len(rows)):
        place = pl.ds((first + index) * CHAN_PITCH, CHAN)
        lanes = slice(index * COLS, (index + 1) * COLS)
        left_scratch[place, :] = left[:, lanes]
        right_scratch[place, :] = right[:, lanes]


def emit_projections(left_scratch, right_scratch, out_ref, first=0, count=CHAN):
    def body(chan, carry):
        place = pl.ds(chan, ROWS, stride=CHAN_PITCH)
        out_ref[chan, 0] = left_scratch[place, :].astype(BF16)
        out_ref[chan, 1] = right_scratch[place, :].astype(BF16)
        return carry

    lax.fori_loop(first, first + count, body, 0, unroll=8)


def project_kernel(
    mask_hbm, gain_hbm, cells_hbm, weight_hbm, pairs_hbm, turned_hbm,
    cells_ref, weight_ref, mask_ref, gain_ref, weight_turned, row_masks, left, right, pairs_ref, turned_ref, sems,
):
    chunks = ROWS // CHUNK
    rows_of = [pl.ds(index * CHUNK, CHUNK) for index in range(chunks)]
    small_copies = [
        pltpu.make_async_copy(weight_hbm.at[0], weight_ref, sems.at[0]),
        pltpu.make_async_copy(mask_hbm, mask_ref, sems.at[1]),
        pltpu.make_async_copy(gain_hbm, gain_ref, sems.at[2]),
    ]
    cell_copies = [
        pltpu.make_async_copy(cells_hbm.at[rows], cells_ref.at[rows], sems.at[3 + index])
        for index, rows in enumerate(rows_of)
    ]
    turned_copies = [
        pltpu.make_async_copy(turned_ref.at[rows], turned_hbm.at[rows], sems.at[3 + chunks + index])
        for index, rows in enumerate(rows_of)
    ]
    for copy in small_copies + cell_copies:
        copy.start()
    for copy in small_copies:
        copy.wait()
    gain_mask = masked_gain(gain_ref, 0, mask_ref)
    set_row_masks(mask_ref, row_masks)
    weight_turned[...] = jnp.transpose(weight_ref[...])
    for first in range(0, ROWS, SUB):
        if first % CHUNK == 0:
            cell_copies[first // CHUNK].wait()
        rows = []
        for index in range(first, first + SUB):
            row = jnp.transpose(cells_ref[index])
            turned_ref[index] = row
            rows.append(row.astype(F32))
        if (first + SUB) % CHUNK == 0:
            turned_copies[first // CHUNK].start()
        masks = [row_mask(row_masks, first + index) for index in range(SUB)]
        project_rows(rows, masks, gain_mask, weight_turned, left, right, first)
    pair_copies = []
    for first in range(0, CHAN, SPAN):
        emit_projections(left, right, pairs_ref, first, SPAN)
        span = pl.ds(first, SPAN)
        pair_copies.append(
            pltpu.make_async_copy(
                pairs_ref.at[span], pairs_hbm.at[span], sems.at[3 + 2 * chunks + first // SPAN]
            )
        )
        pair_copies[-1].start()
    for copy in turned_copies + pair_copies:
        copy.wait()


def project(mask, gain, cells, weight):
    return pl.pallas_call(
        project_kernel,
        in_specs=[HBM, HBM, HBM, HBM],
        out_specs=[HBM, HBM],
        out_shape=[PAIRS, TURNED],
        scratch_shapes=[
            pltpu.VMEM((ROWS, COLS, CHAN), BF16),
            pltpu.VMEM((CHAN, 4 * CHAN), BF16),
            pltpu.VMEM(mask.shape, jnp.int32),
            pltpu.VMEM(gain.shape, F32),
            pltpu.VMEM((4 * CHAN, CHAN), BF16),
            *PROJ_SCRATCH,
            pltpu.VMEM(PAIRS.shape, BF16),
            pltpu.VMEM(TURNED.shape, BF16),
            pltpu.SemaphoreType.DMA((3 + 2 * (ROWS // CHUNK) + CHAN // SPAN,)),
        ],
        compiler_params=pltpu.CompilerParams(vmem_limit_bytes=56 * MIB),
        name="project",
    )(mask, gain, cells, weight)


def gate_kernel(module, gain_ref, cells_ref, weight_ref, out_ref):
    gain = channel_column(gain_ref, module)
    weight = jnp.transpose(weight_ref[module])
    for first in range(0, ROWS, SUB):
        rows = [layer_norm(cells_ref[first + index].astype(F32), gain).astype(BF16) for index in range(SUB)]
        gate = sigmoid(jnp.dot(weight, jnp.concatenate(rows, axis=1), preferred_element_type=F32))
        for index in range(SUB):
            out_ref[first + index] = gate[:, index * COLS : (index + 1) * COLS]


def output_gate(module, gain, cells, weight):
    call = kernel_call(
        functools.partial(gate_kernel, module),
        "output_gate",
        [VMEM, VMEM, VMEM],
        GATE,
        cost=pl.CostEstimate(
            flops=2 * ROWS * COLS * CHAN * CHAN, bytes_accessed=3 << 20, transcendentals=ROWS * COLS * CHAN
        ),
    )
    return call(gain, cells, weight)


def normed_hidden_rows(module, gain_ref, hidden_ref, gains, scratch):
    gains[...] = channel_column(gain_ref, module)
    for first in range(0, ROWS, 16):
        rows = slice(first, first + 16)
        hidden = hidden_ref[:, rows].astype(F32)
        average = jnp.mean(hidden, axis=0)
        centred = hidden - average[None]
        scale = lax.rsqrt(jnp.mean(centred * centred, axis=0) + EPSILON)

        def body(chan, carry):
            values = (hidden_ref[chan, rows].astype(F32) - average) * scale * gains[pl.ds(chan, 1), :]
            scratch[pl.ds(chan * ROW_PITCH + first, 16), :] = values
            return carry

        lax.fori_loop(0, CHAN, body, 0, unroll=8)


def updated_rows(first, scratch, weight, cells_ref, gate_ref):
    hidden = [
        scratch[pl.ds(first + index, CHAN, stride=ROW_PITCH), :].astype(BF16) for index in range(SUB)
    ]
    update = jnp.dot(weight, jnp.concatenate(hidden, axis=1), preferred_element_type=F32)
    return [
        (
            cells_ref[first + index].astype(F32)
            + gate_ref[first + index] * update[:, index * COLS : (index + 1) * COLS]
        ).astype(BF16)
        for index in range(SUB)
    ]


def finish_kernel(gain_ref, hidden_ref, cells_ref, gate_ref, weight_ref, out_hbm, gains, scratch, out_ref, sems):
    normed_hidden_rows(1, gain_ref, hidden_ref, gains, scratch)
    weight = jnp.transpose(weight_ref[1])
    copies = []
    for first in range(0, ROWS, SUB):
        for index, row in enumerate(updated_rows(first, scratch, weight, cells_ref, gate_ref)):
            out_ref[first + index] = jnp.transpose(row)
        if (first + SUB) % CHUNK == 0:
            rows = pl.ds(first + SUB - CHUNK, CHUNK)
            copies.append(pltpu.make_async_copy(out_ref.at[rows], out_hbm.at[rows], sems.at[first // CHUNK]))
            copies[-1].start()
    for copy in copies:
        copy.wait()


def finish(gain, hidden, cells, gate, weight):
    return pl.pallas_call(
        finish_kernel,
        in_specs=[VMEM] * 5,
        out_specs=HBM,
        out_shape=CELLS,
        scratch_shapes=[
            *HIDDEN_SCRATCH,
            pltpu.VMEM((ROWS, COLS, CHAN), BF16),
            pltpu.SemaphoreType.DMA((ROWS // CHUNK,)),
        ],
        compiler_params=pltpu.CompilerParams(vmem_limit_bytes=40 * MIB),
        name="finish",
    )(gain, hidden, cells, gate, weight)


def finish_project_kernel(
    mask_ref, in_gain_ref, out_gain_ref, hidden_ref, cells_ref, gate_ref, weight_ref, proj_ref,
    cells_out, pairs_out, gains, scratch, proj_turned, row_masks, left, right,
):
    gain_mask = masked_gain(in_gain_ref, 1, mask_ref)
    set_row_masks(mask_ref, row_masks)
    normed_hidden_rows(0, out_gain_ref, hidden_ref, gains, scratch)
    weight = jnp.transpose(weight_ref[0])
    proj_turned[...] = jnp.transpose(proj_ref[1])
    for first in range(0, ROWS, SUB):
        rows = updated_rows(first, scratch, weight, cells_ref, gate_ref)
        for index, row in enumerate(rows):
            cells_out[first + index] = row
        masks = [row_mask(row_masks, first + index) for index in range(SUB)]
        rows = [row.astype(F32) for row in rows]
        project_rows(rows, masks, gain_mask, proj_turned, left, right, first)
    emit_projections(left, right, pairs_out)


def finish_project(mask, in_gain, out_gain, hidden, cells, gate, weight, proj):
    call = kernel_call(
        finish_project_kernel,
        "finish_project",
        [VMEM] * 8,
        [TURNED, PAIRS],
        HIDDEN_SCRATCH + [pltpu.VMEM((4 * CHAN, CHAN), BF16)] + PROJ_SCRATCH,
    )
    return call(mask, in_gain, out_gain, hidden, cells, gate, weight, proj)


GROUPS = 16
BLOCKS = 8
TOKENS = BLOCKS * COLS
HALF = GROUPS * ROWS
PRODUCT = jax.ShapeDtypeStruct((GROUPS, BLOCKS, ROWS, COLS), BF16)


def block_lanes(block):
    return slice(block * COLS, (block + 1) * COLS)


def outgoing_kernel(pairs_ref, other_ref, out_ref, left, right):
    core = lax.axis_index("c")
    for block in range(BLOCKS):
        left[:, :, block_lanes(block)] = pairs_ref[:, block, 0]
        right[:, core, :, block_lanes(block)] = pairs_ref[:, block, 1]
        right[:, 1 - core, :, block_lanes(block)] = other_ref[:, block]
    left_rows = left[...].reshape(HALF, TOKENS)
    for block in range(0, BLOCKS, 2):
        groups = slice(block * 2, block * 2 + 4)
        product = lax.dot_general(
            left_rows,
            right[groups].reshape(2 * COLS, TOKENS),
            (((1,), (1,)), ((), ())),
            preferred_element_type=F32,
        ).astype(BF16)
        for half in range(2):
            out_ref[:, block + half] = product[:, block_lanes(half)].reshape(GROUPS, ROWS, COLS)


def outgoing(pairs, other):
    call = kernel_call(
        outgoing_kernel,
        "outgoing",
        [VMEM, VMEM],
        PRODUCT,
        [pltpu.VMEM((GROUPS, ROWS, TOKENS), BF16), pltpu.VMEM((GROUPS, 2, ROWS, TOKENS), BF16)],
    )
    return call(pairs, other)


def incoming_send_kernel(pairs_ref, send_ref, left_ref, right_ref, turned):
    core = lax.axis_index("c")
    for block in range(BLOCKS):
        right_ref[:, block_lanes(block)] = pairs_ref[:, block, 1].reshape(HALF, COLS)
        left = pairs_ref[:, block, 0].reshape(HALF, COLS)
        turned[2 * block : 2 * block + 2] = jnp.transpose(left).reshape(2, 2, ROWS, HALF)
    left_ref[...] = turned[:, core].reshape(HALF, HALF)
    send_ref[...] = jnp.dot(
        turned[:, 1 - core].reshape(HALF, HALF), right_ref[...], preferred_element_type=F32
    ).astype(BF16)


def incoming_send(pairs):
    call = kernel_call(
        incoming_send_kernel,
        "incoming_send",
        [VMEM],
        [
            jax.ShapeDtypeStruct((HALF, TOKENS), BF16),
            jax.ShapeDtypeStruct((HALF, HALF), BF16),
            jax.ShapeDtypeStruct((HALF, TOKENS), BF16),
        ],
        [pltpu.VMEM((GROUPS, 2, ROWS, HALF), BF16)],
    )
    return call(pairs)


def incoming_kernel(left_ref, right_ref, other_ref, out_ref):
    left = left_ref[...]
    for block in range(0, BLOCKS, 2):
        lanes = slice(block * COLS, (block + 2) * COLS)
        total = jnp.dot(left, right_ref[:, lanes], preferred_element_type=F32)
        product = (total + other_ref[:, lanes].astype(F32)).astype(BF16)
        for half in range(2):
            out_ref[:, block + half] = product[:, block_lanes(half)].reshape(GROUPS, ROWS, COLS)


def incoming(left, right, other):
    return kernel_call(incoming_kernel, "incoming", [VMEM, VMEM, VMEM], PRODUCT)(left, right, other)


def exchange(values):
    return lax.all_to_all(values, PEERS, split_axis=0, concat_axis=0, tiled=True)


def to_other_core(values):
    return lax.ppermute(values, "c", [(0, 1), (1, 0)])


def per_device(pair_input, token_mask, in_gain, proj_weight, gate_weight, out_gain, out_weight):
    mask = token_mask.reshape(BLOCKS, COLS)

    pairs, cells = project(mask, in_gain, pair_input, proj_weight)
    pairs = exchange(pairs).reshape(GROUPS, BLOCKS, 2, ROWS, COLS)
    other = to_other_core(pairs[:, :, 1])
    gate = output_gate(0, in_gain, cells, gate_weight)
    product, gate = lax.optimization_barrier((outgoing(pairs, other), gate))
    hidden = exchange(product.reshape(CHAN, ROWS, COLS))
    cells, pairs = finish_project(mask, in_gain, out_gain, hidden, cells, gate, out_weight, proj_weight)

    pairs = exchange(pairs).reshape(GROUPS, BLOCKS, 2, ROWS, COLS)
    send, left, right = incoming_send(pairs)
    other = to_other_core(send)
    gate = output_gate(1, in_gain, cells, gate_weight)
    product, gate = lax.optimization_barrier((incoming(left, right, other), gate))
    hidden = exchange(product.reshape(CHAN, ROWS, COLS))
    return finish(out_gain, hidden, cells, gate, out_weight)


def solution(mesh):
    split = Mesh(mesh.devices.reshape(2, 8, 2, 2, 4), ("xh", "z", "c", "xl", "y"))
    cells = P(("xh", "z", "c"), ("xl", "y"), None)
    return jax.shard_map(
        per_device, mesh=split, in_specs=(cells, P(), P(), P(), P(), P(), P()), out_specs=cells, check_vma=False
    )
```

```python
import functools

import jax
import jax.numpy as jnp
from jax import lax
from jax.experimental import pallas as pl
from jax.experimental.pallas import tpu as pltpu
from jax.sharding import Mesh, PartitionSpec as P

EPSILON = 1e-05
CHAN = 128
ROWS = 32
COLS = 128
SUB = 16
CHUNK = 16
SPAN = 4
CHAN_PITCH = CHAN + 1
ROW_PITCH = ROWS + 1
DEVICES = ("xh", "z", "c", "xl", "y")
PLACES = 16
BLOCKS = 8
PART = 16
F32 = jnp.float32
BF16 = jnp.bfloat16
MIB = 1024 * 1024


def sigmoid(values):
    return 0.5 * jnp.tanh(0.5 * values) + 0.5


VMEM = pl.BlockSpec(memory_space=pltpu.VMEM)


def kernel_call(kernel, name, in_specs, out_shape, scratch_shapes=(), cost=None, vmem=40):
    return pl.pallas_call(
        kernel,
        in_specs=in_specs,
        out_specs=jax.tree.map(lambda _: VMEM, out_shape),
        out_shape=out_shape,
        scratch_shapes=scratch_shapes,
        compiler_params=pltpu.CompilerParams(vmem_limit_bytes=vmem * MIB),
        cost_estimate=cost,
        name=name,
    )


HBM = pl.BlockSpec(memory_space=pltpu.HBM)
PROJ_SCRATCH = [pltpu.VMEM((COLS, COLS), F32)] + [pltpu.VMEM((ROWS * CHAN_PITCH, COLS), F32)] * 2
HIDDEN_SCRATCH = [pltpu.VMEM((CHAN, COLS), F32), pltpu.VMEM((CHAN * ROW_PITCH, COLS), F32)]
PAIRS = jax.ShapeDtypeStruct((PLACES, 2, BLOCKS, 2, PART, COLS), BF16)
CELLS = jax.ShapeDtypeStruct((ROWS, COLS, CHAN), BF16)
TURNED = jax.ShapeDtypeStruct((ROWS, CHAN, COLS), BF16)
GATE = jax.ShapeDtypeStruct((ROWS, CHAN, COLS), F32)


def layer_norm(turned, factor):
    average = jnp.mean(turned, axis=0, keepdims=True)
    centred = turned - average
    variance = jnp.mean(centred * centred, axis=0, keepdims=True)
    return centred * lax.rsqrt(variance + EPSILON) * factor


def channel_column(gain_ref, module):
    return jnp.transpose(jnp.broadcast_to(gain_ref[module : module + 1, :], (COLS, CHAN)))


def masked_gain(gain_ref, module, col_mask_ref):
    block = lax.axis_index(("xl", "y"))
    return channel_column(gain_ref, module) * col_mask_ref[pl.ds(block, 1), :].astype(F32)


def set_row_masks(mask_ref, scratch):
    block = lax.axis_index(("xh", "z", "c")) // (COLS // ROWS)
    tokens = jnp.broadcast_to(mask_ref[pl.ds(block, 1), :].astype(F32), (COLS, COLS))
    scratch[...] = jnp.transpose(tokens)


def row_mask(scratch, index):
    start = lax.axis_index(("xh", "z", "c")) % (COLS // ROWS) * ROWS
    return scratch[pl.ds(start + index, 1), :]


def project_rows(rows, row_masks, gain_mask, weight, left_scratch, right_scratch, first):
    normed = [layer_norm(row, gain_mask * mask).astype(BF16) for row, mask in zip(rows, row_masks)]
    projected = jnp.dot(weight[...], jnp.concatenate(normed, axis=1), preferred_element_type=F32)
    left = sigmoid(projected[:CHAN]) * projected[CHAN : 2 * CHAN]
    right = sigmoid(projected[2 * CHAN : 3 * CHAN]) * projected[3 * CHAN :]
    for index in range(len(rows)):
        place = pl.ds((first + index) * CHAN_PITCH, CHAN)
        lanes = slice(index * COLS, (index + 1) * COLS)
        left_scratch[place, :] = left[:, lanes]
        right_scratch[place, :] = right[:, lanes]


def emit_projections(left_scratch, right_scratch, out_ref, first=0, count=PLACES):
    def body(place, carry):
        for block in range(BLOCKS):
            for core in range(2):
                rows = pl.ds(core * PART * CHAN_PITCH + place * BLOCKS + block, PART, stride=CHAN_PITCH)
                out_ref[place, core, block, 0] = left_scratch[rows, :].astype(BF16)
                out_ref[place, core, block, 1] = right_scratch[rows, :].astype(BF16)
        return carry

    lax.fori_loop(first, first + count, body, 0)


def project_kernel(
    mask_hbm, gain_hbm, cells_hbm, weight_hbm, pairs_hbm, turned_hbm,
    cells_ref, weight_ref, mask_ref, gain_ref, weight_turned, row_masks, left, right, pairs_ref, turned_ref, sems,
):
    chunks = ROWS // CHUNK
    rows_of = [pl.ds(index * CHUNK, CHUNK) for index in range(chunks)]
    small_copies = [
        pltpu.make_async_copy(weight_hbm.at[0], weight_ref, sems.at[0]),
        pltpu.make_async_copy(mask_hbm, mask_ref, sems.at[1]),
        pltpu.make_async_copy(gain_hbm, gain_ref, sems.at[2]),
    ]
    cell_copies = [
        pltpu.make_async_copy(cells_hbm.at[rows], cells_ref.at[rows], sems.at[3 + index])
        for index, rows in enumerate(rows_of)
    ]
    turned_copies = [
        pltpu.make_async_copy(turned_ref.at[rows], turned_hbm.at[rows], sems.at[3 + chunks + index])
        for index, rows in enumerate(rows_of)
    ]
    for copy in small_copies + cell_copies:
        copy.start()
    for copy in small_copies:
        copy.wait()
    gain_mask = masked_gain(gain_ref, 0, mask_ref)
    set_row_masks(mask_ref, row_masks)
    weight_turned[...] = jnp.transpose(weight_ref[...])
    for first in range(0, ROWS, SUB):
        if first % CHUNK == 0:
            cell_copies[first // CHUNK].wait()
        rows = []
        for index in range(first, first + SUB):
            row = jnp.transpose(cells_ref[index])
            turned_ref[index] = row
            rows.append(row.astype(F32))
        if (first + SUB) % CHUNK == 0:
            turned_copies[first // CHUNK].start()
        masks = [row_mask(row_masks, first + index) for index in range(SUB)]
        project_rows(rows, masks, gain_mask, weight_turned, left, right, first)
    pair_copies = []
    for first in range(0, PLACES, SPAN):
        emit_projections(left, right, pairs_ref, first, SPAN)
        span = pl.ds(first, SPAN)
        pair_copies.append(
            pltpu.make_async_copy(
                pairs_ref.at[span], pairs_hbm.at[span], sems.at[3 + 2 * chunks + first // SPAN]
            )
        )
        pair_copies[-1].start()
    for copy in turned_copies + pair_copies:
        copy.wait()


def project(mask, gain, cells, weight):
    return pl.pallas_call(
        project_kernel,
        in_specs=[HBM, HBM, HBM, HBM],
        out_specs=[HBM, HBM],
        out_shape=[PAIRS, TURNED],
        scratch_shapes=[
            pltpu.VMEM((ROWS, COLS, CHAN), BF16),
            pltpu.VMEM((CHAN, 4 * CHAN), BF16),
            pltpu.VMEM(mask.shape, jnp.int32),
            pltpu.VMEM(gain.shape, F32),
            pltpu.VMEM((4 * CHAN, CHAN), BF16),
            *PROJ_SCRATCH,
            pltpu.VMEM(PAIRS.shape, BF16),
            pltpu.VMEM(TURNED.shape, BF16),
            pltpu.SemaphoreType.DMA((3 + 2 * (ROWS // CHUNK) + PLACES // SPAN,)),
        ],
        compiler_params=pltpu.CompilerParams(vmem_limit_bytes=56 * MIB),
        name="project",
    )(mask, gain, cells, weight)


def gate_kernel(module, gain_ref, cells_ref, weight_ref, out_ref):
    gain = channel_column(gain_ref, module)
    weight = jnp.transpose(weight_ref[module])
    for first in range(0, ROWS, SUB):
        rows = [layer_norm(cells_ref[first + index].astype(F32), gain).astype(BF16) for index in range(SUB)]
        gate = sigmoid(jnp.dot(weight, jnp.concatenate(rows, axis=1), preferred_element_type=F32))
        for index in range(SUB):
            out_ref[first + index] = gate[:, index * COLS : (index + 1) * COLS]


def output_gate(module, gain, cells, weight):
    call = kernel_call(
        functools.partial(gate_kernel, module),
        "output_gate",
        [VMEM, VMEM, VMEM],
        GATE,
        cost=pl.CostEstimate(
            flops=2 * ROWS * COLS * CHAN * CHAN, bytes_accessed=3 << 20, transcendentals=ROWS * COLS * CHAN
        ),
    )
    return call(gain, cells, weight)


def normed_hidden_rows(module, gain_ref, hidden_ref, gains, scratch):
    gains[...] = channel_column(gain_ref, module)
    for core in range(2):
        hidden = hidden_ref[:, core].astype(F32).reshape(CHAN, PART, COLS)
        average = jnp.mean(hidden, axis=0)
        centred = hidden - average[None]
        scale = lax.rsqrt(jnp.mean(centred * centred, axis=0) + EPSILON)

        def body(place, carry):
            for block in range(BLOCKS):
                chan = place * BLOCKS + block
                values = (hidden_ref[place, core, block].astype(F32) - average) * scale * gains[pl.ds(chan, 1), :]
                scratch[pl.ds(chan * ROW_PITCH + core * PART, PART), :] = values
            return carry

        lax.fori_loop(0, PLACES, body, 0)


def updated_rows(first, scratch, weight, cells_ref, gate_ref):
    hidden = [
        scratch[pl.ds(first + index, CHAN, stride=ROW_PITCH), :].astype(BF16) for index in range(SUB)
    ]
    update = jnp.dot(weight, jnp.concatenate(hidden, axis=1), preferred_element_type=F32)
    return [
        (
            cells_ref[first + index].astype(F32)
            + gate_ref[first + index] * update[:, index * COLS : (index + 1) * COLS]
        ).astype(BF16)
        for index in range(SUB)
    ]


def finish_kernel(gain_ref, hidden_ref, cells_ref, gate_ref, weight_ref, out_hbm, gains, scratch, out_ref, sems):
    normed_hidden_rows(1, gain_ref, hidden_ref, gains, scratch)
    weight = jnp.transpose(weight_ref[1])
    copies = []
    for first in range(0, ROWS, SUB):
        for index, row in enumerate(updated_rows(first, scratch, weight, cells_ref, gate_ref)):
            out_ref[first + index] = jnp.transpose(row)
        if (first + SUB) % CHUNK == 0:
            rows = pl.ds(first + SUB - CHUNK, CHUNK)
            copies.append(pltpu.make_async_copy(out_ref.at[rows], out_hbm.at[rows], sems.at[first // CHUNK]))
            copies[-1].start()
    for copy in copies:
        copy.wait()


def finish(gain, hidden, cells, gate, weight):
    return pl.pallas_call(
        finish_kernel,
        in_specs=[VMEM] * 5,
        out_specs=HBM,
        out_shape=CELLS,
        scratch_shapes=[
            *HIDDEN_SCRATCH,
            pltpu.VMEM((ROWS, COLS, CHAN), BF16),
            pltpu.SemaphoreType.DMA((ROWS // CHUNK,)),
        ],
        compiler_params=pltpu.CompilerParams(vmem_limit_bytes=40 * MIB),
        name="finish",
    )(gain, hidden, cells, gate, weight)


def finish_project_kernel(
    mask_ref, in_gain_ref, out_gain_ref, hidden_ref, cells_ref, gate_ref, weight_ref, proj_ref,
    cells_out, pairs_out, gains, scratch, proj_turned, row_masks, left, right,
):
    gain_mask = masked_gain(in_gain_ref, 1, mask_ref)
    set_row_masks(mask_ref, row_masks)
    normed_hidden_rows(0, out_gain_ref, hidden_ref, gains, scratch)
    weight = jnp.transpose(weight_ref[0])
    proj_turned[...] = jnp.transpose(proj_ref[1])
    for first in range(0, ROWS, SUB):
        rows = updated_rows(first, scratch, weight, cells_ref, gate_ref)
        for index, row in enumerate(rows):
            cells_out[first + index] = row
        masks = [row_mask(row_masks, first + index) for index in range(SUB)]
        rows = [row.astype(F32) for row in rows]
        project_rows(rows, masks, gain_mask, proj_turned, left, right, first)
    emit_projections(left, right, pairs_out)


def finish_project(mask, in_gain, out_gain, hidden, cells, gate, weight, proj):
    call = kernel_call(
        finish_project_kernel,
        "finish_project",
        [VMEM] * 8,
        [TURNED, PAIRS],
        HIDDEN_SCRATCH + [pltpu.VMEM((4 * CHAN, CHAN), BF16)] + PROJ_SCRATCH,
    )
    return call(mask, in_gain, out_gain, hidden, cells, gate, weight, proj)


GROUPS = 32
TOKENS = BLOCKS * COLS
HALF = GROUPS * PART
PRODUCT = jax.ShapeDtypeStruct((GROUPS, BLOCKS, PART, COLS), BF16)


def block_lanes(block):
    return slice(block * COLS, (block + 1) * COLS)


def outgoing_kernel(pairs_ref, other_ref, out_ref, left, right):
    core = lax.axis_index("c")
    for block in range(BLOCKS):
        left[:, :, block_lanes(block)] = pairs_ref[:, block, 0]
        right[:, core, :, block_lanes(block)] = pairs_ref[:, block, 1]
        right[:, 1 - core, :, block_lanes(block)] = other_ref[:, block]
    left_rows = left[...].reshape(HALF, TOKENS)
    for block in range(0, BLOCKS, 2):
        groups = slice(block * 4, block * 4 + 8)
        product = lax.dot_general(
            left_rows,
            right[groups].reshape(2 * COLS, TOKENS),
            (((1,), (1,)), ((), ())),
            preferred_element_type=F32,
        ).astype(BF16)
        for half in range(2):
            out_ref[:, block + half] = product[:, block_lanes(half)].reshape(GROUPS, PART, COLS)


def outgoing(pairs, other):
    call = kernel_call(
        outgoing_kernel,
        "outgoing",
        [VMEM, VMEM],
        PRODUCT,
        [pltpu.VMEM((GROUPS, PART, TOKENS), BF16), pltpu.VMEM((GROUPS, 2, PART, TOKENS), BF16)],
    )
    return call(pairs, other)


def incoming_send_kernel(pairs_ref, send_ref, left_ref, right_ref, turned):
    core = lax.axis_index("c")
    for block in range(BLOCKS):
        right_ref[:, block_lanes(block)] = pairs_ref[:, block, 1].reshape(HALF, COLS)
        left = pairs_ref[:, block, 0].reshape(HALF, COLS)
        turned[4 * block : 4 * block + 4] = jnp.transpose(left).reshape(4, 2, PART, HALF)
    left_ref[...] = turned[:, core].reshape(HALF, HALF)
    send_ref[...] = jnp.dot(
        turned[:, 1 - core].reshape(HALF, HALF), right_ref[...], preferred_element_type=F32
    ).astype(BF16)


def incoming_send(pairs):
    call = kernel_call(
        incoming_send_kernel,
        "incoming_send",
        [VMEM],
        [
            jax.ShapeDtypeStruct((HALF, TOKENS), BF16),
            jax.ShapeDtypeStruct((HALF, HALF), BF16),
            jax.ShapeDtypeStruct((HALF, TOKENS), BF16),
        ],
        [pltpu.VMEM((GROUPS, 2, PART, HALF), BF16)],
    )
    return call(pairs)


def incoming_kernel(left_ref, right_ref, other_ref, out_ref):
    left = left_ref[...]
    for block in range(0, BLOCKS, 2):
        lanes = slice(block * COLS, (block + 2) * COLS)
        total = jnp.dot(left, right_ref[:, lanes], preferred_element_type=F32)
        product = (total + other_ref[:, lanes].astype(F32)).astype(BF16)
        for half in range(2):
            out_ref[:, block + half] = product[:, block_lanes(half)].reshape(GROUPS, PART, COLS)


def incoming(left, right, other):
    return kernel_call(incoming_kernel, "incoming", [VMEM, VMEM, VMEM], PRODUCT)(left, right, other)


def exchange(values):
    return lax.all_to_all(values, DEVICES, split_axis=0, concat_axis=0, tiled=True)


def exchange_pairs(pairs):
    received = exchange(pairs.reshape(2 * CHAN, 2, PART, COLS))
    return received.reshape(GROUPS, BLOCKS, 2, PART, COLS)


def exchange_product(product):
    return exchange(product.reshape(2 * CHAN, PART, COLS)).reshape(PLACES, 2, BLOCKS, PART, COLS)


def to_other_core(values):
    return lax.ppermute(values, "c", [(0, 1), (1, 0)])


def per_device(pair_input, token_mask, in_gain, proj_weight, gate_weight, out_gain, out_weight):
    mask = token_mask.reshape(BLOCKS, COLS)

    pairs, cells = project(mask, in_gain, pair_input, proj_weight)
    pairs = exchange_pairs(pairs)
    other = to_other_core(pairs[:, :, 1])
    gate = output_gate(0, in_gain, cells, gate_weight)
    product, gate = lax.optimization_barrier((outgoing(pairs, other), gate))
    hidden = exchange_product(product)
    cells, pairs = finish_project(mask, in_gain, out_gain, hidden, cells, gate, out_weight, proj_weight)

    pairs = exchange_pairs(pairs)
    send, left, right = incoming_send(pairs)
    other = to_other_core(send)
    gate = output_gate(1, in_gain, cells, gate_weight)
    product, gate = lax.optimization_barrier((incoming(left, right, other), gate))
    hidden = exchange_product(product)
    return finish(out_gain, hidden, cells, gate, out_weight)


def solution(mesh):
    split = Mesh(mesh.devices.reshape(2, 8, 2, 2, 4), ("xh", "z", "c", "xl", "y"))
    cells = P(("xh", "z", "c"), ("xl", "y"), None)
    return jax.shard_map(
        per_device, mesh=split, in_specs=(cells, P(), P(), P(), P(), P(), P()), out_specs=cells, check_vma=False
    )
```

```python
import functools

import jax
import jax.numpy as jnp
from jax import lax
from jax.experimental import pallas as pl
from jax.experimental.pallas import tpu as pltpu
from jax.sharding import Mesh, PartitionSpec as P

EPSILON = 1e-05
CHAN = 128
ROWS = 32
COLS = 128
SUB = 16
CHUNK = 16
SPAN = 4
CHAN_PITCH = CHAN + 1
ROW_PITCH = ROWS + 1
DEVICES = ("xh", "z", "c", "xl", "y")
PLACES = 16
BLOCKS = 8
PART = 16
F32 = jnp.float32
BF16 = jnp.bfloat16
MIB = 1024 * 1024


def sigmoid(values):
    return 0.5 * jnp.tanh(0.5 * values) + 0.5


VMEM = pl.BlockSpec(memory_space=pltpu.VMEM)


def kernel_call(kernel, name, in_specs, out_shape, scratch_shapes=(), cost=None, vmem=40):
    return pl.pallas_call(
        kernel,
        in_specs=in_specs,
        out_specs=jax.tree.map(lambda _: VMEM, out_shape),
        out_shape=out_shape,
        scratch_shapes=scratch_shapes,
        compiler_params=pltpu.CompilerParams(vmem_limit_bytes=vmem * MIB),
        cost_estimate=cost,
        name=name,
    )


HBM = pl.BlockSpec(memory_space=pltpu.HBM)
PROJ_SCRATCH = [pltpu.VMEM((COLS, COLS), F32)] + [pltpu.VMEM((ROWS * CHAN_PITCH + CHAN, COLS), F32)] * 2
HIDDEN_SCRATCH = [pltpu.VMEM((CHAN, COLS), F32), pltpu.VMEM((CHAN * ROW_PITCH + ROWS, COLS), F32)]
PAIRS = jax.ShapeDtypeStruct((PLACES, 2, BLOCKS, 2, PART, COLS), BF16)
CELLS = jax.ShapeDtypeStruct((ROWS, COLS, CHAN), BF16)
TURNED = jax.ShapeDtypeStruct((ROWS, CHAN, COLS), BF16)
GATE = jax.ShapeDtypeStruct((ROWS, CHAN, COLS), F32)


def layer_norm(turned, factor):
    average = jnp.mean(turned, axis=0, keepdims=True)
    centred = turned - average
    variance = jnp.mean(centred * centred, axis=0, keepdims=True)
    return centred * lax.rsqrt(variance + EPSILON) * factor


def by_part(columns):
    starts = [group * ROWS + core * PART for core in range(2) for group in range(COLS // ROWS)]
    return jnp.concatenate([columns[start : start + PART] for start in starts], axis=0)


def natural(columns):
    starts = [core * (COLS // 2) + group * PART for group in range(COLS // ROWS) for core in range(2)]
    return jnp.concatenate([columns[start : start + PART] for start in starts], axis=0)


def channel_column(gain_ref, module):
    return jnp.transpose(jnp.broadcast_to(gain_ref[module : module + 1, :], (COLS, CHAN)))


def masked_gain(gain_ref, module, col_mask_ref):
    block = lax.axis_index(("xl", "y"))
    tokens = jnp.broadcast_to(col_mask_ref[pl.ds(block, 1), :].astype(F32), (COLS, COLS))
    return channel_column(gain_ref, module) * jnp.transpose(by_part(jnp.transpose(tokens)))


def set_row_masks(mask_ref, scratch):
    block = lax.axis_index(("xh", "z", "c")) // (COLS // ROWS)
    tokens = jnp.broadcast_to(mask_ref[pl.ds(block, 1), :].astype(F32), (COLS, COLS))
    scratch[...] = jnp.transpose(tokens)


def row_mask(scratch, index):
    start = lax.axis_index(("xh", "z", "c")) % (COLS // ROWS) * ROWS
    return scratch[pl.ds(start + index, 1), :]


def project_rows(rows, row_masks, gain_mask, weight, left_scratch, right_scratch, first):
    normed = [layer_norm(row, gain_mask * mask).astype(BF16) for row, mask in zip(rows, row_masks)]
    projected = jnp.dot(weight[...], jnp.concatenate(normed, axis=1), preferred_element_type=F32)
    left = sigmoid(projected[:CHAN]) * projected[CHAN : 2 * CHAN]
    right = sigmoid(projected[2 * CHAN : 3 * CHAN]) * projected[3 * CHAN :]
    for index in range(len(rows)):
        place = pl.ds((first + index) * CHAN_PITCH, CHAN)
        lanes = slice(index * COLS, (index + 1) * COLS)
        left_scratch[place, :] = left[:, lanes]
        right_scratch[place, :] = right[:, lanes]


def emit_projections(left_scratch, right_scratch, out_ref, first=0, count=PLACES):
    def body(place, carry):
        for block in range(BLOCKS):
            for core in range(2):
                rows = pl.ds(core * PART * CHAN_PITCH + place * BLOCKS + block, PART, stride=CHAN_PITCH)
                out_ref[place, core, block, 0] = left_scratch[rows, :].astype(BF16)
                out_ref[place, core, block, 1] = right_scratch[rows, :].astype(BF16)
        return carry

    lax.fori_loop(first, first + count, body, 0)


def project_kernel(
    mask_hbm, gain_hbm, cells_hbm, weight_hbm, pairs_hbm, turned_hbm,
    cells_ref, weight_ref, mask_ref, gain_ref, weight_turned, row_masks, left, right, pairs_ref, turned_ref, sems,
):
    chunks = ROWS // CHUNK
    rows_of = [pl.ds(index * CHUNK, CHUNK) for index in range(chunks)]
    small_copies = [
        pltpu.make_async_copy(weight_hbm.at[0], weight_ref, sems.at[0]),
        pltpu.make_async_copy(mask_hbm, mask_ref, sems.at[1]),
        pltpu.make_async_copy(gain_hbm, gain_ref, sems.at[2]),
    ]
    cell_copies = [
        pltpu.make_async_copy(cells_hbm.at[rows], cells_ref.at[rows], sems.at[3 + index])
        for index, rows in enumerate(rows_of)
    ]
    turned_copies = [
        pltpu.make_async_copy(turned_ref.at[rows], turned_hbm.at[rows], sems.at[3 + chunks + index])
        for index, rows in enumerate(rows_of)
    ]
    for copy in small_copies + cell_copies:
        copy.start()
    for copy in small_copies:
        copy.wait()
    gain_mask = masked_gain(gain_ref, 0, mask_ref)
    set_row_masks(mask_ref, row_masks)
    weight_turned[...] = jnp.transpose(weight_ref[...])
    for first in range(0, ROWS, SUB):
        if first % CHUNK == 0:
            cell_copies[first // CHUNK].wait()
        rows = []
        for index in range(first, first + SUB):
            row = jnp.transpose(by_part(cells_ref[index]))
            turned_ref[index] = row
            rows.append(row.astype(F32))
        if (first + SUB) % CHUNK == 0:
            turned_copies[first // CHUNK].start()
        masks = [row_mask(row_masks, first + index) for index in range(SUB)]
        project_rows(rows, masks, gain_mask, weight_turned, left, right, first)
    pair_copies = []
    for first in range(0, PLACES, SPAN):
        emit_projections(left, right, pairs_ref, first, SPAN)
        span = pl.ds(first, SPAN)
        pair_copies.append(
            pltpu.make_async_copy(
                pairs_ref.at[span], pairs_hbm.at[span], sems.at[3 + 2 * chunks + first // SPAN]
            )
        )
        pair_copies[-1].start()
    for copy in turned_copies + pair_copies:
        copy.wait()


def project(mask, gain, cells, weight):
    return pl.pallas_call(
        project_kernel,
        in_specs=[HBM, HBM, HBM, HBM],
        out_specs=[HBM, HBM],
        out_shape=[PAIRS, TURNED],
        scratch_shapes=[
            pltpu.VMEM((ROWS, COLS, CHAN), BF16),
            pltpu.VMEM((CHAN, 4 * CHAN), BF16),
            pltpu.VMEM(mask.shape, jnp.int32),
            pltpu.VMEM(gain.shape, F32),
            pltpu.VMEM((4 * CHAN, CHAN), BF16),
            *PROJ_SCRATCH,
            pltpu.VMEM(PAIRS.shape, BF16),
            pltpu.VMEM(TURNED.shape, BF16),
            pltpu.SemaphoreType.DMA((3 + 2 * (ROWS // CHUNK) + PLACES // SPAN,)),
        ],
        compiler_params=pltpu.CompilerParams(vmem_limit_bytes=56 * MIB),
        name="project",
    )(mask, gain, cells, weight)


def gate_kernel(module, gain_ref, cells_ref, weight_ref, out_ref):
    gain = channel_column(gain_ref, module)
    weight = jnp.transpose(weight_ref[module])
    for first in range(0, ROWS, SUB):
        rows = [layer_norm(cells_ref[first + index].astype(F32), gain).astype(BF16) for index in range(SUB)]
        gate = sigmoid(jnp.dot(weight, jnp.concatenate(rows, axis=1), preferred_element_type=F32))
        for index in range(SUB):
            out_ref[first + index] = gate[:, index * COLS : (index + 1) * COLS]


def output_gate(module, gain, cells, weight):
    call = kernel_call(
        functools.partial(gate_kernel, module),
        "output_gate",
        [VMEM, VMEM, VMEM],
        GATE,
        cost=pl.CostEstimate(
            flops=2 * ROWS * COLS * CHAN * CHAN, bytes_accessed=3 << 20, transcendentals=ROWS * COLS * CHAN
        ),
    )
    return call(gain, cells, weight)


def normed_hidden_rows(module, gain_ref, hidden_ref, gains, scratch):
    gains[...] = channel_column(gain_ref, module)
    for core in range(2):
        hidden = hidden_ref[:, core].astype(F32).reshape(CHAN, PART, COLS)
        average = jnp.mean(hidden, axis=0)
        centred = hidden - average[None]
        scale = lax.rsqrt(jnp.mean(centred * centred, axis=0) + EPSILON)

        def body(place, carry):
            for block in range(BLOCKS):
                chan = place * BLOCKS + block
                values = (hidden_ref[place, core, block].astype(F32) - average) * scale * gains[pl.ds(chan, 1), :]
                scratch[pl.ds(chan * ROW_PITCH + core * PART, PART), :] = values
            return carry

        lax.fori_loop(0, PLACES, body, 0)


def updated_rows(first, scratch, weight, cells_ref, gate_ref):
    hidden = [
        scratch[pl.ds(first + index, CHAN, stride=ROW_PITCH), :].astype(BF16) for index in range(SUB)
    ]
    update = jnp.dot(weight, jnp.concatenate(hidden, axis=1), preferred_element_type=F32)
    return [
        (
            cells_ref[first + index].astype(F32)
            + gate_ref[first + index] * update[:, index * COLS : (index + 1) * COLS]
        ).astype(BF16)
        for index in range(SUB)
    ]


def finish_kernel(gain_ref, hidden_ref, cells_ref, gate_ref, weight_ref, out_hbm, gains, scratch, out_ref, sems):
    normed_hidden_rows(1, gain_ref, hidden_ref, gains, scratch)
    weight = jnp.transpose(weight_ref[1])
    copies = []
    for first in range(0, ROWS, SUB):
        for index, row in enumerate(updated_rows(first, scratch, weight, cells_ref, gate_ref)):
            out_ref[first + index] = natural(jnp.transpose(row))
        if (first + SUB) % CHUNK == 0:
            rows = pl.ds(first + SUB - CHUNK, CHUNK)
            copies.append(pltpu.make_async_copy(out_ref.at[rows], out_hbm.at[rows], sems.at[first // CHUNK]))
            copies[-1].start()
    for copy in copies:
        copy.wait()


def finish(gain, hidden, cells, gate, weight):
    return pl.pallas_call(
        finish_kernel,
        in_specs=[VMEM] * 5,
        out_specs=HBM,
        out_shape=CELLS,
        scratch_shapes=[
            *HIDDEN_SCRATCH,
            pltpu.VMEM((ROWS, COLS, CHAN), BF16),
            pltpu.SemaphoreType.DMA((ROWS // CHUNK,)),
        ],
        compiler_params=pltpu.CompilerParams(vmem_limit_bytes=40 * MIB),
        name="finish",
    )(gain, hidden, cells, gate, weight)


def finish_project_kernel(
    mask_ref, in_gain_ref, out_gain_ref, hidden_ref, cells_ref, gate_ref, weight_ref, proj_ref,
    cells_out, pairs_out, gains, scratch, proj_turned, row_masks, left, right,
):
    gain_mask = masked_gain(in_gain_ref, 1, mask_ref)
    set_row_masks(mask_ref, row_masks)
    normed_hidden_rows(0, out_gain_ref, hidden_ref, gains, scratch)
    weight = jnp.transpose(weight_ref[0])
    proj_turned[...] = jnp.transpose(proj_ref[1])
    for first in range(0, ROWS, SUB):
        rows = updated_rows(first, scratch, weight, cells_ref, gate_ref)
        for index, row in enumerate(rows):
            cells_out[first + index] = row
        masks = [row_mask(row_masks, first + index) for index in range(SUB)]
        rows = [row.astype(F32) for row in rows]
        project_rows(rows, masks, gain_mask, proj_turned, left, right, first)
    emit_projections(left, right, pairs_out)


def finish_project(mask, in_gain, out_gain, hidden, cells, gate, weight, proj):
    call = kernel_call(
        finish_project_kernel,
        "finish_project",
        [VMEM] * 8,
        [TURNED, PAIRS],
        HIDDEN_SCRATCH + [pltpu.VMEM((4 * CHAN, CHAN), BF16)] + PROJ_SCRATCH,
    )
    return call(mask, in_gain, out_gain, hidden, cells, gate, weight, proj)


GROUPS = 32
TOKENS = BLOCKS * COLS
HALF = GROUPS * PART
PRODUCT = jax.ShapeDtypeStruct((GROUPS, BLOCKS, PART, COLS), BF16)


def block_lanes(block):
    return slice(block * COLS, (block + 1) * COLS)


def take_right_kernel(pairs_ref, out_ref):
    out_ref[...] = pairs_ref[:, :, 1]


def take_right(pairs):
    shape = jax.ShapeDtypeStruct((GROUPS, BLOCKS, PART, COLS), BF16)
    return kernel_call(take_right_kernel, "take_right", [VMEM], shape)(pairs)


def product_half(left_ref, right, block):
    rows = right[block * (COLS // 2) : (block + 2) * (COLS // 2)]
    return lax.dot_general(left_ref[...], rows, (((1,), (1,)), ((), ())), preferred_element_type=F32)


def outgoing_own_kernel(pairs_ref, left_ref, own_ref, right):
    for block in range(BLOCKS):
        left_ref[:, block_lanes(block)] = pairs_ref[:, block, 0].reshape(HALF, COLS)
        right[:, block_lanes(block)] = pairs_ref[:, block, 1].reshape(HALF, COLS)
    for pair in range(BLOCKS // 2):
        own_ref[:, block_lanes(pair)] = product_half(left_ref, right, 2 * pair)


def outgoing_own(pairs):
    call = kernel_call(
        outgoing_own_kernel,
        "outgoing_own",
        [VMEM],
        [jax.ShapeDtypeStruct((HALF, TOKENS), BF16), jax.ShapeDtypeStruct((HALF, HALF), F32)],
        [pltpu.VMEM((HALF, TOKENS), BF16)],
        cost=pl.CostEstimate(flops=2 * HALF * HALF * TOKENS, bytes_accessed=4 << 20, transcendentals=0),
    )
    return call(pairs)


def outgoing_kernel(left_ref, own_ref, other_ref, out_ref, right):
    own_first = lax.axis_index("c") == 0
    lower = lax.broadcasted_iota(jnp.int32, (HALF, COLS), 1) < COLS // 2
    for block in range(BLOCKS):
        right[:, block_lanes(block)] = other_ref[:, block].reshape(HALF, COLS)
    for pair in range(BLOCKS // 2):
        own = own_ref[:, block_lanes(pair)]
        other = product_half(left_ref, right, 2 * pair)
        first = jnp.where(own_first, own, other)
        second = jnp.where(own_first, other, own)
        even = jnp.where(lower, first, pltpu.roll(second, COLS // 2, 1)).astype(BF16)
        odd = jnp.where(lower, pltpu.roll(first, COLS // 2, 1), second).astype(BF16)
        out_ref[:, 2 * pair] = even.reshape(GROUPS, PART, COLS)
        out_ref[:, 2 * pair + 1] = odd.reshape(GROUPS, PART, COLS)


def outgoing(left, own, other):
    call = kernel_call(
        outgoing_kernel, "outgoing", [VMEM, VMEM, VMEM], PRODUCT, [pltpu.VMEM((HALF, TOKENS), BF16)]
    )
    return call(left, own, other)


def incoming_send_kernel(pairs_ref, send_ref, left_ref, right_ref, turned):
    core = lax.axis_index("c")
    for block in range(BLOCKS):
        right_ref[:, block_lanes(block)] = pairs_ref[:, block, 1].reshape(HALF, COLS)
        left = pairs_ref[:, block, 0].reshape(HALF, COLS)
        turned[:, block] = jnp.transpose(left).reshape(2, COLS // 2, HALF)
    left_ref[...] = turned[core].reshape(HALF, HALF)
    send_ref[...] = jnp.dot(
        turned[1 - core].reshape(HALF, HALF), right_ref[...], preferred_element_type=F32
    ).astype(BF16)


def incoming_send(pairs):
    call = kernel_call(
        incoming_send_kernel,
        "incoming_send",
        [VMEM],
        [
            jax.ShapeDtypeStruct((HALF, TOKENS), BF16),
            jax.ShapeDtypeStruct((HALF, HALF), BF16),
            jax.ShapeDtypeStruct((HALF, TOKENS), BF16),
        ],
        [pltpu.VMEM((2, BLOCKS, COLS // 2, HALF), BF16)],
    )
    return call(pairs)


def incoming_kernel(left_ref, right_ref, other_ref, out_ref):
    left = left_ref[...]
    for block in range(0, BLOCKS, 2):
        lanes = slice(block * COLS, (block + 2) * COLS)
        total = jnp.dot(left, right_ref[:, lanes], preferred_element_type=F32)
        product = (total + other_ref[:, lanes].astype(F32)).astype(BF16)
        for half in range(2):
            out_ref[:, block + half] = product[:, block_lanes(half)].reshape(GROUPS, PART, COLS)


def incoming(left, right, other):
    return kernel_call(incoming_kernel, "incoming", [VMEM, VMEM, VMEM], PRODUCT)(left, right, other)


def exchange(values):
    return lax.all_to_all(values, DEVICES, split_axis=0, concat_axis=0, tiled=True)


def exchange_pairs(pairs):
    received = exchange(pairs.reshape(2 * CHAN, 2, PART, COLS))
    return received.reshape(GROUPS, BLOCKS, 2, PART, COLS)


def exchange_product(product):
    return exchange(product.reshape(2 * CHAN, PART, COLS)).reshape(PLACES, 2, BLOCKS, PART, COLS)


def to_other_core(values):
    return lax.ppermute(values, "c", [(0, 1), (1, 0)])


def per_device(pair_input, token_mask, in_gain, proj_weight, gate_weight, out_gain, out_weight):
    mask = token_mask.reshape(BLOCKS, COLS)

    pairs, cells = project(mask, in_gain, pair_input, proj_weight)
    pairs = exchange_pairs(pairs)
    other = to_other_core(take_right(pairs))
    left, own = outgoing_own(pairs)
    gate = output_gate(0, in_gain, cells, gate_weight)
    product, gate = lax.optimization_barrier((outgoing(left, own, other), gate))
    hidden = exchange_product(product)
    cells, pairs = finish_project(mask, in_gain, out_gain, hidden, cells, gate, out_weight, proj_weight)

    pairs = exchange_pairs(pairs)
    send, left, right = incoming_send(pairs)
    other = to_other_core(send)
    gate = output_gate(1, in_gain, cells, gate_weight)
    product, gate = lax.optimization_barrier((incoming(left, right, other), gate))
    hidden = exchange_product(product)
    return finish(out_gain, hidden, cells, gate, out_weight)


def solution(mesh):
    split = Mesh(mesh.devices.reshape(2, 8, 2, 2, 4), ("xh", "z", "c", "xl", "y"))
    cells = P(("xh", "z", "c"), ("xl", "y"), None)
    return jax.shard_map(
        per_device, mesh=split, in_specs=(cells, P(), P(), P(), P(), P(), P()), out_specs=cells, check_vma=False
    )
```

```python
import functools

import jax
import jax.numpy as jnp
from jax import lax
from jax.experimental import pallas as pl
from jax.experimental.pallas import tpu as pltpu
from jax.sharding import Mesh, PartitionSpec as P

EPSILON = 1e-05
CHAN = 128
ROWS = 32
COLS = 128
SUB = 16
CHUNK = 16
SPAN = 4
CHAN_PITCH = CHAN + 1
ROW_PITCH = ROWS + 1
DEVICES = ("xh", "z", "c", "xl", "y")
PLACES = 16
BLOCKS = 8
PART = 16
F32 = jnp.float32
BF16 = jnp.bfloat16
MIB = 1024 * 1024


def sigmoid(values):
    return 0.5 * jnp.tanh(0.5 * values) + 0.5


VMEM = pl.BlockSpec(memory_space=pltpu.VMEM)


def kernel_call(kernel, name, in_specs, out_shape, scratch_shapes=(), cost=None, vmem=40):
    return pl.pallas_call(
        kernel,
        in_specs=in_specs,
        out_specs=jax.tree.map(lambda _: VMEM, out_shape),
        out_shape=out_shape,
        scratch_shapes=scratch_shapes,
        compiler_params=pltpu.CompilerParams(vmem_limit_bytes=vmem * MIB),
        cost_estimate=cost,
        name=name,
    )


HBM = pl.BlockSpec(memory_space=pltpu.HBM)
PROJ_SCRATCH = [pltpu.VMEM((COLS, COLS), F32)] + [pltpu.VMEM((ROWS * CHAN_PITCH + CHAN, COLS), F32)] * 2
HIDDEN_SCRATCH = [pltpu.VMEM((CHAN, COLS), F32), pltpu.VMEM((CHAN * ROW_PITCH + ROWS, COLS), F32)]
PAIRS = jax.ShapeDtypeStruct((PLACES, 2, BLOCKS, 2, PART, COLS), BF16)
CELLS = jax.ShapeDtypeStruct((ROWS, COLS, CHAN), BF16)
TURNED = jax.ShapeDtypeStruct((ROWS, CHAN, COLS), BF16)
GATE = jax.ShapeDtypeStruct((ROWS, CHAN, COLS), F32)


def layer_norm(turned, factor):
    average = jnp.mean(turned, axis=0, keepdims=True)
    centred = turned - average
    variance = jnp.mean(centred * centred, axis=0, keepdims=True)
    return centred * lax.rsqrt(variance + EPSILON) * factor


def channel_column(gain_ref, module):
    return jnp.transpose(jnp.broadcast_to(gain_ref[module : module + 1, :], (COLS, CHAN)))


def masked_gain(gain_ref, module, col_mask_ref):
    block = lax.axis_index(("xl", "y"))
    return channel_column(gain_ref, module) * col_mask_ref[pl.ds(block, 1), :].astype(F32)


def set_row_masks(mask_ref, scratch):
    block = lax.axis_index(("xh", "z", "c")) // (COLS // ROWS)
    tokens = jnp.broadcast_to(mask_ref[pl.ds(block, 1), :].astype(F32), (COLS, COLS))
    scratch[...] = jnp.transpose(tokens)


def row_mask(scratch, index):
    start = lax.axis_index(("xh", "z", "c")) % (COLS // ROWS) * ROWS
    return scratch[pl.ds(start + index, 1), :]


def project_rows(rows, row_masks, gain_mask, weight, left_scratch, right_scratch, first):
    normed = [layer_norm(row, gain_mask * mask).astype(BF16) for row, mask in zip(rows, row_masks)]
    projected = jnp.dot(weight[...], jnp.concatenate(normed, axis=1), preferred_element_type=F32)
    left = sigmoid(projected[:CHAN]) * projected[CHAN : 2 * CHAN]
    right = sigmoid(projected[2 * CHAN : 3 * CHAN]) * projected[3 * CHAN :]
    for index in range(len(rows)):
        place = pl.ds((first + index) * CHAN_PITCH, CHAN)
        lanes = slice(index * COLS, (index + 1) * COLS)
        left_scratch[place, :] = left[:, lanes]
        right_scratch[place, :] = right[:, lanes]


def emit_projections(left_scratch, right_scratch, out_ref, first=0, count=PLACES):
    def body(place, carry):
        for block in range(BLOCKS):
            for core in range(2):
                rows = pl.ds(core * PART * CHAN_PITCH + place * BLOCKS + block, PART, stride=CHAN_PITCH)
                out_ref[place, core, block, 0] = left_scratch[rows, :].astype(BF16)
                out_ref[place, core, block, 1] = right_scratch[rows, :].astype(BF16)
        return carry

    lax.fori_loop(first, first + count, body, 0)


def project_kernel(
    mask_hbm, gain_hbm, cells_hbm, weight_hbm, pairs_hbm, turned_hbm,
    cells_ref, weight_ref, mask_ref, gain_ref, weight_turned, row_masks, left, right, pairs_ref, turned_ref, sems,
):
    chunks = ROWS // CHUNK
    rows_of = [pl.ds(index * CHUNK, CHUNK) for index in range(chunks)]
    small_copies = [
        pltpu.make_async_copy(weight_hbm.at[0], weight_ref, sems.at[0]),
        pltpu.make_async_copy(mask_hbm, mask_ref, sems.at[1]),
        pltpu.make_async_copy(gain_hbm, gain_ref, sems.at[2]),
    ]
    cell_copies = [
        pltpu.make_async_copy(cells_hbm.at[rows], cells_ref.at[rows], sems.at[3 + index])
        for index, rows in enumerate(rows_of)
    ]
    turned_copies = [
        pltpu.make_async_copy(turned_ref.at[rows], turned_hbm.at[rows], sems.at[3 + chunks + index])
        for index, rows in enumerate(rows_of)
    ]
    for copy in small_copies + cell_copies:
        copy.start()
    for copy in small_copies:
        copy.wait()
    gain_mask = masked_gain(gain_ref, 0, mask_ref)
    set_row_masks(mask_ref, row_masks)
    weight_turned[...] = jnp.transpose(weight_ref[...])
    for first in range(0, ROWS, SUB):
        if first % CHUNK == 0:
            cell_copies[first // CHUNK].wait()
        rows = []
        for index in range(first, first + SUB):
            row = jnp.transpose(cells_ref[index])
            turned_ref[index] = row
            rows.append(row.astype(F32))
        if (first + SUB) % CHUNK == 0:
            turned_copies[first // CHUNK].start()
        masks = [row_mask(row_masks, first + index) for index in range(SUB)]
        project_rows(rows, masks, gain_mask, weight_turned, left, right, first)
    pair_copies = []
    for first in range(0, PLACES, SPAN):
        emit_projections(left, right, pairs_ref, first, SPAN)
        span = pl.ds(first, SPAN)
        pair_copies.append(
            pltpu.make_async_copy(
                pairs_ref.at[span], pairs_hbm.at[span], sems.at[3 + 2 * chunks + first // SPAN]
            )
        )
        pair_copies[-1].start()
    for copy in turned_copies + pair_copies:
        copy.wait()


def project(mask, gain, cells, weight):
    return pl.pallas_call(
        project_kernel,
        in_specs=[HBM, HBM, HBM, HBM],
        out_specs=[HBM, HBM],
        out_shape=[PAIRS, TURNED],
        scratch_shapes=[
            pltpu.VMEM((ROWS, COLS, CHAN), BF16),
            pltpu.VMEM((CHAN, 4 * CHAN), BF16),
            pltpu.VMEM(mask.shape, jnp.int32),
            pltpu.VMEM(gain.shape, F32),
            pltpu.VMEM((4 * CHAN, CHAN), BF16),
            *PROJ_SCRATCH,
            pltpu.VMEM(PAIRS.shape, BF16),
            pltpu.VMEM(TURNED.shape, BF16),
            pltpu.SemaphoreType.DMA((3 + 2 * (ROWS // CHUNK) + PLACES // SPAN,)),
        ],
        compiler_params=pltpu.CompilerParams(vmem_limit_bytes=56 * MIB),
        name="project",
    )(mask, gain, cells, weight)


def gate_kernel(module, gain_ref, cells_ref, weight_ref, out_ref):
    gain = channel_column(gain_ref, module)
    weight = jnp.transpose(weight_ref[module])
    for first in range(0, ROWS, SUB):
        rows = [layer_norm(cells_ref[first + index].astype(F32), gain).astype(BF16) for index in range(SUB)]
        gate = sigmoid(jnp.dot(weight, jnp.concatenate(rows, axis=1), preferred_element_type=F32))
        for index in range(SUB):
            out_ref[first + index] = gate[:, index * COLS : (index + 1) * COLS]


def output_gate(module, gain, cells, weight):
    call = kernel_call(
        functools.partial(gate_kernel, module),
        "output_gate",
        [VMEM, VMEM, VMEM],
        GATE,
        cost=pl.CostEstimate(
            flops=2 * ROWS * COLS * CHAN * CHAN, bytes_accessed=3 << 20, transcendentals=ROWS * COLS * CHAN
        ),
    )
    return call(gain, cells, weight)


def normed_hidden_rows(module, gain_ref, hidden_ref, gains, scratch):
    gains[...] = channel_column(gain_ref, module)
    for core in range(2):
        hidden = hidden_ref[:, core].astype(F32).reshape(CHAN, PART, COLS)
        average = jnp.mean(hidden, axis=0)
        centred = hidden - average[None]
        scale = lax.rsqrt(jnp.mean(centred * centred, axis=0) + EPSILON)

        def body(place, carry):
            for block in range(BLOCKS):
                chan = place * BLOCKS + block
                values = (hidden_ref[place, core, block].astype(F32) - average) * scale * gains[pl.ds(chan, 1), :]
                scratch[pl.ds(chan * ROW_PITCH + core * PART, PART), :] = values
            return carry

        lax.fori_loop(0, PLACES, body, 0)


def updated_rows(first, scratch, weight, cells_ref, gate_ref):
    hidden = [
        scratch[pl.ds(first + index, CHAN, stride=ROW_PITCH), :].astype(BF16) for index in range(SUB)
    ]
    update = jnp.dot(weight, jnp.concatenate(hidden, axis=1), preferred_element_type=F32)
    return [
        (
            cells_ref[first + index].astype(F32)
            + gate_ref[first + index] * update[:, index * COLS : (index + 1) * COLS]
        ).astype(BF16)
        for index in range(SUB)
    ]


def finish_kernel(gain_ref, hidden_ref, cells_ref, gate_ref, weight_ref, out_hbm, gains, scratch, out_ref, sems):
    normed_hidden_rows(1, gain_ref, hidden_ref, gains, scratch)
    weight = jnp.transpose(weight_ref[1])
    copies = []
    for first in range(0, ROWS, SUB):
        for index, row in enumerate(updated_rows(first, scratch, weight, cells_ref, gate_ref)):
            out_ref[first + index] = jnp.transpose(row)
        if (first + SUB) % CHUNK == 0:
            rows = pl.ds(first + SUB - CHUNK, CHUNK)
            copies.append(pltpu.make_async_copy(out_ref.at[rows], out_hbm.at[rows], sems.at[first // CHUNK]))
            copies[-1].start()
    for copy in copies:
        copy.wait()


def finish(gain, hidden, cells, gate, weight):
    return pl.pallas_call(
        finish_kernel,
        in_specs=[VMEM] * 5,
        out_specs=HBM,
        out_shape=CELLS,
        scratch_shapes=[
            *HIDDEN_SCRATCH,
            pltpu.VMEM((ROWS, COLS, CHAN), BF16),
            pltpu.SemaphoreType.DMA((ROWS // CHUNK,)),
        ],
        compiler_params=pltpu.CompilerParams(vmem_limit_bytes=40 * MIB),
        name="finish",
    )(gain, hidden, cells, gate, weight)


def finish_project_kernel(
    mask_ref, in_gain_ref, out_gain_ref, hidden_ref, cells_ref, gate_ref, weight_ref, proj_ref,
    cells_out, pairs_out, gains, scratch, proj_turned, row_masks, left, right,
):
    gain_mask = masked_gain(in_gain_ref, 1, mask_ref)
    set_row_masks(mask_ref, row_masks)
    normed_hidden_rows(0, out_gain_ref, hidden_ref, gains, scratch)
    weight = jnp.transpose(weight_ref[0])
    proj_turned[...] = jnp.transpose(proj_ref[1])
    for first in range(0, ROWS, SUB):
        rows = updated_rows(first, scratch, weight, cells_ref, gate_ref)
        for index, row in enumerate(rows):
            cells_out[first + index] = row
        masks = [row_mask(row_masks, first + index) for index in range(SUB)]
        rows = [row.astype(F32) for row in rows]
        project_rows(rows, masks, gain_mask, proj_turned, left, right, first)
    emit_projections(left, right, pairs_out)


def finish_project(mask, in_gain, out_gain, hidden, cells, gate, weight, proj):
    call = kernel_call(
        finish_project_kernel,
        "finish_project",
        [VMEM] * 8,
        [TURNED, PAIRS],
        HIDDEN_SCRATCH + [pltpu.VMEM((4 * CHAN, CHAN), BF16)] + PROJ_SCRATCH,
    )
    return call(mask, in_gain, out_gain, hidden, cells, gate, weight, proj)


GROUPS = 32
TOKENS = BLOCKS * COLS
HALF = GROUPS * PART
PRODUCT = jax.ShapeDtypeStruct((GROUPS, BLOCKS, PART, COLS), BF16)


def block_lanes(block):
    return slice(block * COLS, (block + 1) * COLS)


def take_right_kernel(pairs_ref, out_ref):
    out_ref[...] = pairs_ref[:, :, 1]


def take_right(pairs):
    shape = jax.ShapeDtypeStruct((GROUPS, BLOCKS, PART, COLS), BF16)
    return kernel_call(take_right_kernel, "take_right", [VMEM], shape)(pairs)


def outgoing_kernel(pairs_ref, other_ref, out_ref, left, right):
    core = lax.axis_index("c")
    for block in range(BLOCKS):
        left[:, :, block_lanes(block)] = pairs_ref[:, block, 0]
        right[:, core, :, block_lanes(block)] = pairs_ref[:, block, 1]
        right[:, 1 - core, :, block_lanes(block)] = other_ref[:, block]
    left_rows = left[...].reshape(HALF, TOKENS)
    for block in range(0, BLOCKS, 2):
        groups = slice(block * 4, block * 4 + 8)
        product = lax.dot_general(
            left_rows,
            right[groups].reshape(2 * COLS, TOKENS),
            (((1,), (1,)), ((), ())),
            preferred_element_type=F32,
        ).astype(BF16)
        for half in range(2):
            out_ref[:, block + half] = product[:, block_lanes(half)].reshape(GROUPS, PART, COLS)


def outgoing(pairs, other):
    call = kernel_call(
        outgoing_kernel,
        "outgoing",
        [VMEM, VMEM],
        PRODUCT,
        [pltpu.VMEM((GROUPS, PART, TOKENS), BF16), pltpu.VMEM((GROUPS, 2, PART, TOKENS), BF16)],
    )
    return call(pairs, other)


def incoming_send_kernel(pairs_ref, send_ref, left_ref, right_ref, turned):
    core = lax.axis_index("c")
    for block in range(BLOCKS):
        right_ref[:, block_lanes(block)] = pairs_ref[:, block, 1].reshape(HALF, COLS)
        left = pairs_ref[:, block, 0].reshape(HALF, COLS)
        turned[4 * block : 4 * block + 4] = jnp.transpose(left).reshape(4, 2, PART, HALF)
    left_ref[...] = turned[:, core].reshape(HALF, HALF)
    send_ref[...] = jnp.dot(
        turned[:, 1 - core].reshape(HALF, HALF), right_ref[...], preferred_element_type=F32
    ).astype(BF16)


def incoming_send(pairs):
    call = kernel_call(
        incoming_send_kernel,
        "incoming_send",
        [VMEM],
        [
            jax.ShapeDtypeStruct((HALF, TOKENS), BF16),
            jax.ShapeDtypeStruct((HALF, HALF), BF16),
            jax.ShapeDtypeStruct((HALF, TOKENS), BF16),
        ],
        [pltpu.VMEM((GROUPS, 2, PART, HALF), BF16)],
    )
    return call(pairs)


def incoming_kernel(left_ref, right_ref, other_ref, out_ref):
    left = left_ref[...]
    for block in range(0, BLOCKS, 2):
        lanes = slice(block * COLS, (block + 2) * COLS)
        total = jnp.dot(left, right_ref[:, lanes], preferred_element_type=F32)
        product = (total + other_ref[:, lanes].astype(F32)).astype(BF16)
        for half in range(2):
            out_ref[:, block + half] = product[:, block_lanes(half)].reshape(GROUPS, PART, COLS)


def incoming(left, right, other):
    return kernel_call(incoming_kernel, "incoming", [VMEM, VMEM, VMEM], PRODUCT)(left, right, other)


def exchange(values):
    return lax.all_to_all(values, DEVICES, split_axis=0, concat_axis=0, tiled=True)


def exchange_pairs(pairs):
    received = exchange(pairs.reshape(2 * CHAN, 2, PART, COLS))
    return received.reshape(GROUPS, BLOCKS, 2, PART, COLS)


def exchange_product(product):
    return exchange(product.reshape(2 * CHAN, PART, COLS)).reshape(PLACES, 2, BLOCKS, PART, COLS)


def to_other_core(values):
    return lax.ppermute(values, "c", [(0, 1), (1, 0)])


def per_device(pair_input, token_mask, in_gain, proj_weight, gate_weight, out_gain, out_weight):
    mask = token_mask.reshape(BLOCKS, COLS)

    pairs, cells = project(mask, in_gain, pair_input, proj_weight)
    pairs = exchange_pairs(pairs)
    other = to_other_core(take_right(pairs))
    gate = output_gate(0, in_gain, cells, gate_weight)
    product, gate = lax.optimization_barrier((outgoing(pairs, other), gate))
    hidden = exchange_product(product)
    cells, pairs = finish_project(mask, in_gain, out_gain, hidden, cells, gate, out_weight, proj_weight)

    pairs = exchange_pairs(pairs)
    send, left, right = incoming_send(pairs)
    other = to_other_core(send)
    gate = output_gate(1, in_gain, cells, gate_weight)
    product, gate = lax.optimization_barrier((incoming(left, right, other), gate))
    hidden = exchange_product(product)
    return finish(out_gain, hidden, cells, gate, out_weight)


def solution(mesh):
    split = Mesh(mesh.devices.reshape(2, 8, 2, 2, 4), ("xh", "z", "c", "xl", "y"))
    cells = P(("xh", "z", "c"), ("xl", "y"), None)
    return jax.shard_map(
        per_device, mesh=split, in_specs=(cells, P(), P(), P(), P(), P(), P()), out_specs=cells, check_vma=False
    )
```

```python
import functools

import jax
import jax.numpy as jnp
from jax import lax
from jax.experimental import pallas as pl
from jax.experimental.pallas import tpu as pltpu
from jax.sharding import Mesh, PartitionSpec as P

EPSILON = 1e-05
CHAN = 128
ROWS = 32
COLS = 128
GROUPS = 16
DEPTH = 8
BLOCKS = 8
SUB = 16
CHUNK = 16
SPAN = 32
CHAN_PITCH = CHAN + 1
ROW_PITCH = ROWS + 1
PEERS = ("xh", "z", "xl", "y")
PLANE = ("xh", "xl", "y")
F32 = jnp.float32
BF16 = jnp.bfloat16
MIB = 1024 * 1024


def sigmoid(values):
    return 0.5 * jnp.tanh(0.5 * values) + 0.5


VMEM = pl.BlockSpec(memory_space=pltpu.VMEM)


def kernel_call(kernel, name, in_specs, out_shape, scratch_shapes=(), cost=None, vmem=40):
    return pl.pallas_call(
        kernel,
        in_specs=in_specs,
        out_specs=jax.tree.map(lambda _: VMEM, out_shape),
        out_shape=out_shape,
        scratch_shapes=scratch_shapes,
        compiler_params=pltpu.CompilerParams(vmem_limit_bytes=vmem * MIB),
        cost_estimate=cost,
        name=name,
    )


HBM = pl.BlockSpec(memory_space=pltpu.HBM)
PROJ_SCRATCH = [pltpu.VMEM((COLS, COLS), F32)] + [pltpu.VMEM((ROWS * CHAN_PITCH + CHAN, COLS), F32)] * 2
HIDDEN_SCRATCH = [pltpu.VMEM((CHAN, COLS), F32), pltpu.VMEM((CHAN * ROW_PITCH + ROWS, COLS), F32)]
PAIRS = jax.ShapeDtypeStruct((CHAN, 2, ROWS, COLS), BF16)
CELLS = jax.ShapeDtypeStruct((ROWS, COLS, CHAN), BF16)
TURNED = jax.ShapeDtypeStruct((ROWS, CHAN, COLS), BF16)
GATE = jax.ShapeDtypeStruct((ROWS, CHAN, COLS), F32)


def layer_norm(turned, factor):
    average = jnp.mean(turned, axis=0, keepdims=True)
    centred = turned - average
    variance = jnp.mean(centred * centred, axis=0, keepdims=True)
    return centred * lax.rsqrt(variance + EPSILON) * factor


def channel_column(gain_ref, module):
    return jnp.transpose(jnp.broadcast_to(gain_ref[module : module + 1, :], (COLS, CHAN)))


def masked_gain(gain_ref, module, col_mask_ref):
    block = lax.axis_index(("xl", "y"))
    return channel_column(gain_ref, module) * col_mask_ref[pl.ds(block, 1), :].astype(F32)


def set_row_masks(mask_ref, scratch):
    block = lax.axis_index(("xh", "z", "c")) // (COLS // ROWS)
    tokens = jnp.broadcast_to(mask_ref[pl.ds(block, 1), :].astype(F32), (COLS, COLS))
    scratch[...] = jnp.transpose(tokens)


def row_mask(scratch, index):
    start = lax.axis_index(("xh", "z", "c")) % (COLS // ROWS) * ROWS
    return scratch[pl.ds(start + index, 1), :]


def project_rows(rows, row_masks, gain_mask, weight, left_scratch, right_scratch, first):
    normed = [layer_norm(row, gain_mask * mask).astype(BF16) for row, mask in zip(rows, row_masks)]
    projected = jnp.dot(weight[...], jnp.concatenate(normed, axis=1), preferred_element_type=F32)
    left = sigmoid(projected[:CHAN]) * projected[CHAN : 2 * CHAN]
    right = sigmoid(projected[2 * CHAN : 3 * CHAN]) * projected[3 * CHAN :]
    for index in range(len(rows)):
        place = pl.ds((first + index) * CHAN_PITCH, CHAN)
        lanes = slice(index * COLS, (index + 1) * COLS)
        left_scratch[place, :] = left[:, lanes]
        right_scratch[place, :] = right[:, lanes]


def emit_projections(left_scratch, right_scratch, out_ref, first=0, count=CHAN):
    def body(chan, carry):
        place = pl.ds(chan, ROWS, stride=CHAN_PITCH)
        out_ref[chan, 0] = left_scratch[place, :].astype(BF16)
        out_ref[chan, 1] = right_scratch[place, :].astype(BF16)
        return carry

    lax.fori_loop(first, first + count, body, 0, unroll=8)


def project_kernel(
    mask_hbm, gain_hbm, cells_hbm, weight_hbm, pairs_hbm, turned_hbm,
    cells_ref, weight_ref, mask_ref, gain_ref, weight_turned, row_masks, left, right, pairs_ref, turned_ref, sems,
):
    chunks = ROWS // CHUNK
    rows_of = [pl.ds(index * CHUNK, CHUNK) for index in range(chunks)]
    small_copies = [
        pltpu.make_async_copy(weight_hbm.at[0], weight_ref, sems.at[0]),
        pltpu.make_async_copy(mask_hbm, mask_ref, sems.at[1]),
        pltpu.make_async_copy(gain_hbm, gain_ref, sems.at[2]),
    ]
    cell_copies = [
        pltpu.make_async_copy(cells_hbm.at[rows], cells_ref.at[rows], sems.at[3 + index])
        for index, rows in enumerate(rows_of)
    ]
    turned_copies = [
        pltpu.make_async_copy(turned_ref.at[rows], turned_hbm.at[rows], sems.at[3 + chunks + index])
        for index, rows in enumerate(rows_of)
    ]
    for copy in small_copies + cell_copies:
        copy.start()
    for copy in small_copies:
        copy.wait()
    gain_mask = masked_gain(gain_ref, 0, mask_ref)
    set_row_masks(mask_ref, row_masks)
    weight_turned[...] = jnp.transpose(weight_ref[...])
    for first in range(0, ROWS, SUB):
        if first % CHUNK == 0:
            cell_copies[first // CHUNK].wait()
        rows = []
        for index in range(first, first + SUB):
            row = jnp.transpose(cells_ref[index])
            turned_ref[index] = row
            rows.append(row.astype(F32))
        if (first + SUB) % CHUNK == 0:
            turned_copies[first // CHUNK].start()
        masks = [row_mask(row_masks, first + index) for index in range(SUB)]
        project_rows(rows, masks, gain_mask, weight_turned, left, right, first)
    pair_copies = []
    for first in range(0, CHAN, SPAN):
        emit_projections(left, right, pairs_ref, first, SPAN)
        span = pl.ds(first, SPAN)
        pair_copies.append(
            pltpu.make_async_copy(
                pairs_ref.at[span], pairs_hbm.at[span], sems.at[3 + 2 * chunks + first // SPAN]
            )
        )
        pair_copies[-1].start()
    for copy in turned_copies + pair_copies:
        copy.wait()


def project(mask, gain, cells, weight):
    return pl.pallas_call(
        project_kernel,
        in_specs=[HBM, HBM, HBM, HBM],
        out_specs=[HBM, HBM],
        out_shape=[PAIRS, TURNED],
        scratch_shapes=[
            pltpu.VMEM((ROWS, COLS, CHAN), BF16),
            pltpu.VMEM((CHAN, 4 * CHAN), BF16),
            pltpu.VMEM(mask.shape, jnp.int32),
            pltpu.VMEM(gain.shape, F32),
            pltpu.VMEM((4 * CHAN, CHAN), BF16),
            *PROJ_SCRATCH,
            pltpu.VMEM(PAIRS.shape, BF16),
            pltpu.VMEM(TURNED.shape, BF16),
            pltpu.SemaphoreType.DMA((3 + 2 * (ROWS // CHUNK) + CHAN // SPAN,)),
        ],
        compiler_params=pltpu.CompilerParams(vmem_limit_bytes=56 * MIB),
        name="project",
    )(mask, gain, cells, weight)


def gate_kernel(module, gain_ref, cells_ref, weight_ref, out_ref):
    gain = channel_column(gain_ref, module)
    weight = jnp.transpose(weight_ref[module])
    for first in range(0, ROWS, SUB):
        rows = [layer_norm(cells_ref[first + index].astype(F32), gain).astype(BF16) for index in range(SUB)]
        gate = sigmoid(jnp.dot(weight, jnp.concatenate(rows, axis=1), preferred_element_type=F32))
        for index in range(SUB):
            out_ref[first + index] = gate[:, index * COLS : (index + 1) * COLS]


def output_gate(module, gain, cells, weight):
    call = kernel_call(
        functools.partial(gate_kernel, module),
        "output_gate",
        [VMEM, VMEM, VMEM],
        GATE,
        cost=pl.CostEstimate(
            flops=2 * ROWS * COLS * CHAN * CHAN, bytes_accessed=3 << 20, transcendentals=ROWS * COLS * CHAN
        ),
    )
    return call(gain, cells, weight)


def normed_hidden_rows(module, gain_ref, hidden_ref, gains, scratch):
    gains[...] = channel_column(gain_ref, module)
    for first in range(0, ROWS, 16):
        rows = slice(first, first + 16)
        hidden = hidden_ref[:, rows].astype(F32)
        average = jnp.mean(hidden, axis=0)
        centred = hidden - average[None]
        scale = lax.rsqrt(jnp.mean(centred * centred, axis=0) + EPSILON)

        def body(place, carry):
            for block in range(BLOCKS):
                chan = place % DEPTH * 2 * BLOCKS + place // DEPTH * BLOCKS + block
                values = (hidden_ref[place * BLOCKS + block, rows].astype(F32) - average) * scale
                scratch[pl.ds(chan * ROW_PITCH + first, 16), :] = values * gains[pl.ds(chan, 1), :]
            return carry

        lax.fori_loop(0, GROUPS, body, 0)


def updated_rows(first, scratch, weight, cells_ref, gate_ref):
    hidden = [
        scratch[pl.ds(first + index, CHAN, stride=ROW_PITCH), :].astype(BF16) for index in range(SUB)
    ]
    update = jnp.dot(weight, jnp.concatenate(hidden, axis=1), preferred_element_type=F32)
    return [
        (
            cells_ref[first + index].astype(F32)
            + gate_ref[first + index] * update[:, index * COLS : (index + 1) * COLS]
        ).astype(BF16)
        for index in range(SUB)
    ]


def finish_kernel(gain_ref, hidden_ref, cells_ref, gate_ref, weight_ref, out_hbm, gains, scratch, out_ref, sems):
    normed_hidden_rows(1, gain_ref, hidden_ref, gains, scratch)
    weight = jnp.transpose(weight_ref[1])
    copies = []
    for first in range(0, ROWS, SUB):
        for index, row in enumerate(updated_rows(first, scratch, weight, cells_ref, gate_ref)):
            out_ref[first + index] = jnp.transpose(row)
        if (first + SUB) % CHUNK == 0:
            rows = pl.ds(first + SUB - CHUNK, CHUNK)
            copies.append(pltpu.make_async_copy(out_ref.at[rows], out_hbm.at[rows], sems.at[first // CHUNK]))
            copies[-1].start()
    for copy in copies:
        copy.wait()


def finish(gain, hidden, cells, gate, weight):
    return pl.pallas_call(
        finish_kernel,
        in_specs=[VMEM] * 5,
        out_specs=HBM,
        out_shape=CELLS,
        scratch_shapes=[
            *HIDDEN_SCRATCH,
            pltpu.VMEM((ROWS, COLS, CHAN), BF16),
            pltpu.SemaphoreType.DMA((ROWS // CHUNK,)),
        ],
        compiler_params=pltpu.CompilerParams(vmem_limit_bytes=40 * MIB),
        name="finish",
    )(gain, hidden, cells, gate, weight)


def finish_project_kernel(
    mask_ref, in_gain_ref, out_gain_ref, hidden_ref, cells_ref, gate_ref, weight_ref, proj_ref,
    cells_out, pairs_out, gains, scratch, proj_turned, row_masks, left, right,
):
    gain_mask = masked_gain(in_gain_ref, 1, mask_ref)
    set_row_masks(mask_ref, row_masks)
    normed_hidden_rows(0, out_gain_ref, hidden_ref, gains, scratch)
    weight = jnp.transpose(weight_ref[0])
    proj_turned[...] = jnp.transpose(proj_ref[1])
    for first in range(0, ROWS, SUB):
        rows = updated_rows(first, scratch, weight, cells_ref, gate_ref)
        for index, row in enumerate(rows):
            cells_out[first + index] = row
        masks = [row_mask(row_masks, first + index) for index in range(SUB)]
        rows = [row.astype(F32) for row in rows]
        project_rows(rows, masks, gain_mask, proj_turned, left, right, first)
    emit_projections(left, right, pairs_out)


def finish_project(mask, in_gain, out_gain, hidden, cells, gate, weight, proj):
    call = kernel_call(
        finish_project_kernel,
        "finish_project",
        [VMEM] * 8,
        [TURNED, PAIRS],
        HIDDEN_SCRATCH + [pltpu.VMEM((4 * CHAN, CHAN), BF16)] + PROJ_SCRATCH,
    )
    return call(mask, in_gain, out_gain, hidden, cells, gate, weight, proj)


TOKENS = BLOCKS * COLS
HALF = GROUPS * ROWS
PRODUCT = jax.ShapeDtypeStruct((GROUPS, BLOCKS, ROWS, COLS), BF16)


def block_lanes(block):
    return slice(block * COLS, (block + 1) * COLS)


def side(pairs_ref, block, which):
    return pairs_ref[:, block, :, which].reshape(GROUPS, ROWS, COLS)


def take_right_kernel(pairs_ref, out_ref):
    for block in range(BLOCKS):
        out_ref[:, block] = side(pairs_ref, block, 1)


def take_right(pairs):
    return kernel_call(take_right_kernel, "take_right", [VMEM], PRODUCT)(pairs)


def outgoing_kernel(pairs_ref, other_ref, out_ref, left, right):
    core = lax.axis_index("c")
    for block in range(BLOCKS):
        left[:, :, block_lanes(block)] = side(pairs_ref, block, 0)
        right[:, core, :, block_lanes(block)] = side(pairs_ref, block, 1)
        right[:, 1 - core, :, block_lanes(block)] = other_ref[:, block]
    left_rows = left[...].reshape(HALF, TOKENS)
    for block in range(0, BLOCKS, 2):
        groups = slice(block * 2, block * 2 + 4)
        product = lax.dot_general(
            left_rows,
            right[groups].reshape(2 * COLS, TOKENS),
            (((1,), (1,)), ((), ())),
            preferred_element_type=F32,
        ).astype(BF16)
        for half in range(2):
            out_ref[:, block + half] = product[:, block_lanes(half)].reshape(GROUPS, ROWS, COLS)


def outgoing(pairs, other):
    call = kernel_call(
        outgoing_kernel,
        "outgoing",
        [VMEM, VMEM],
        PRODUCT,
        [pltpu.VMEM((GROUPS, ROWS, TOKENS), BF16), pltpu.VMEM((GROUPS, 2, ROWS, TOKENS), BF16)],
    )
    return call(pairs, other)


def incoming_send_kernel(pairs_ref, send_ref, left_ref, right_ref, turned):
    core = lax.axis_index("c")
    for block in range(BLOCKS):
        right_ref[:, block_lanes(block)] = side(pairs_ref, block, 1).reshape(HALF, COLS)
        left = side(pairs_ref, block, 0).reshape(HALF, COLS)
        turned[2 * block : 2 * block + 2] = jnp.transpose(left).reshape(2, 2, ROWS, HALF)
    left_ref[...] = turned[:, core].reshape(HALF, HALF)
    send_ref[...] = jnp.dot(
        turned[:, 1 - core].reshape(HALF, HALF), right_ref[...], preferred_element_type=F32
    ).astype(BF16)


def incoming_send(pairs):
    call = kernel_call(
        incoming_send_kernel,
        "incoming_send",
        [VMEM],
        [
            jax.ShapeDtypeStruct((HALF, TOKENS), BF16),
            jax.ShapeDtypeStruct((HALF, HALF), BF16),
            jax.ShapeDtypeStruct((HALF, TOKENS), BF16),
        ],
        [pltpu.VMEM((GROUPS, 2, ROWS, HALF), BF16)],
    )
    return call(pairs)


def incoming_kernel(left_ref, right_ref, other_ref, out_ref):
    left = left_ref[...]
    for block in range(0, BLOCKS, 2):
        lanes = slice(block * COLS, (block + 2) * COLS)
        total = jnp.dot(left, right_ref[:, lanes], preferred_element_type=F32)
        product = (total + other_ref[:, lanes].astype(F32)).astype(BF16)
        for half in range(2):
            out_ref[:, block + half] = product[:, block_lanes(half)].reshape(GROUPS, ROWS, COLS)


def incoming(left, right, other):
    return kernel_call(incoming_kernel, "incoming", [VMEM, VMEM, VMEM], PRODUCT)(left, right, other)


def exchange(values):
    return lax.all_to_all(values, PEERS, split_axis=0, concat_axis=0, tiled=True)


def planes_first(pairs):
    pairs = jnp.swapaxes(lax.all_to_all(pairs, "z", split_axis=0, concat_axis=0, tiled=True), 0, 1)
    return lax.all_to_all(pairs, PLANE, split_axis=0, concat_axis=0, tiled=True)


def planes_last(pairs):
    pairs = jnp.swapaxes(pairs, 0, 1)
    pairs = jnp.swapaxes(lax.all_to_all(pairs, PLANE, split_axis=0, concat_axis=0, tiled=True), 0, 1)
    return jnp.swapaxes(lax.all_to_all(pairs, "z", split_axis=0, concat_axis=0, tiled=True), 0, 1)


def exchange_pairs(pairs):
    pairs = pairs.reshape(DEPTH, 2 * BLOCKS, 2 * ROWS, COLS)
    pairs = lax.cond(lax.axis_index("c") == 0, planes_first, planes_last, pairs)
    return pairs.reshape(2, BLOCKS, DEPTH, 2, ROWS, COLS)


def to_other_core(values):
    return lax.ppermute(values, "c", [(0, 1), (1, 0)])


def per_device(pair_input, token_mask, in_gain, proj_weight, gate_weight, out_gain, out_weight):
    mask = token_mask.reshape(BLOCKS, COLS)

    pairs, cells = project(mask, in_gain, pair_input, proj_weight)
    pairs = exchange_pairs(pairs)
    other = to_other_core(take_right(pairs))
    gate = output_gate(0, in_gain, cells, gate_weight)
    product, gate = lax.optimization_barrier((outgoing(pairs, other), gate))
    hidden = exchange(product.reshape(CHAN, ROWS, COLS))
    cells, pairs = finish_project(mask, in_gain, out_gain, hidden, cells, gate, out_weight, proj_weight)

    pairs = exchange_pairs(pairs)
    send, left, right = incoming_send(pairs)
    other = to_other_core(send)
    gate = output_gate(1, in_gain, cells, gate_weight)
    product, gate = lax.optimization_barrier((incoming(left, right, other), gate))
    hidden = exchange(product.reshape(CHAN, ROWS, COLS))
    return finish(out_gain, hidden, cells, gate, out_weight)


def solution(mesh):
    split = Mesh(mesh.devices.reshape(2, 8, 2, 2, 4), ("xh", "z", "c", "xl", "y"))
    cells = P(("xh", "z", "c"), ("xl", "y"), None)
    return jax.shard_map(
        per_device, mesh=split, in_specs=(cells, P(), P(), P(), P(), P(), P()), out_specs=cells, check_vma=False
    )
```

```python
import functools

import jax
import jax.numpy as jnp
from jax import lax
from jax.experimental import pallas as pl
from jax.experimental.pallas import tpu as pltpu
from jax.sharding import Mesh, PartitionSpec as P

EPSILON = 1e-05
CHAN = 128
ROWS = 32
COLS = 128
GROUPS = 16
DEPTH = 8
CHIPS = 16
BLOCKS = 8
SUB = 16
CHUNK = 16
SPAN = 32
CHAN_PITCH = CHAN + 1
ROW_PITCH = ROWS + 1
PLANE = ("xh", "xl", "y")
F32 = jnp.float32
BF16 = jnp.bfloat16
MIB = 1024 * 1024


def sigmoid(values):
    return 0.5 * jnp.tanh(0.5 * values) + 0.5


VMEM = pl.BlockSpec(memory_space=pltpu.VMEM)


def kernel_call(kernel, name, in_specs, out_shape, scratch_shapes=(), cost=None, vmem=40):
    return pl.pallas_call(
        kernel,
        in_specs=in_specs,
        out_specs=jax.tree.map(lambda _: VMEM, out_shape),
        out_shape=out_shape,
        scratch_shapes=scratch_shapes,
        compiler_params=pltpu.CompilerParams(vmem_limit_bytes=vmem * MIB),
        cost_estimate=cost,
        name=name,
    )


HBM = pl.BlockSpec(memory_space=pltpu.HBM)
PROJ_SCRATCH = [pltpu.VMEM((COLS, COLS), F32)] + [pltpu.VMEM((ROWS * CHAN_PITCH + CHAN, COLS), F32)] * 2
HIDDEN_SCRATCH = [pltpu.VMEM((CHAN, COLS), F32), pltpu.VMEM((CHAN * ROW_PITCH + ROWS, COLS), F32)]
PAIRS = jax.ShapeDtypeStruct((CHAN, 2, ROWS, COLS), BF16)
CELLS = jax.ShapeDtypeStruct((ROWS, COLS, CHAN), BF16)
TURNED = jax.ShapeDtypeStruct((ROWS, CHAN, COLS), BF16)
GATE = jax.ShapeDtypeStruct((ROWS, CHAN, COLS), F32)


def layer_norm(turned, factor):
    average = jnp.mean(turned, axis=0, keepdims=True)
    centred = turned - average
    variance = jnp.mean(centred * centred, axis=0, keepdims=True)
    return centred * lax.rsqrt(variance + EPSILON) * factor


def channel_column(gain_ref, module):
    return jnp.transpose(jnp.broadcast_to(gain_ref[module : module + 1, :], (COLS, CHAN)))


def masked_gain(gain_ref, module, col_mask_ref):
    block = lax.axis_index(("xl", "y"))
    return channel_column(gain_ref, module) * col_mask_ref[pl.ds(block, 1), :].astype(F32)


def set_row_masks(mask_ref, scratch):
    block = lax.axis_index(("xh", "z", "c")) // (COLS // ROWS)
    tokens = jnp.broadcast_to(mask_ref[pl.ds(block, 1), :].astype(F32), (COLS, COLS))
    scratch[...] = jnp.transpose(tokens)


def row_mask(scratch, index):
    start = lax.axis_index(("xh", "z", "c")) % (COLS // ROWS) * ROWS
    return scratch[pl.ds(start + index, 1), :]


def project_rows(rows, row_masks, gain_mask, weight, left_scratch, right_scratch, first):
    normed = [layer_norm(row, gain_mask * mask).astype(BF16) for row, mask in zip(rows, row_masks)]
    projected = jnp.dot(weight[...], jnp.concatenate(normed, axis=1), preferred_element_type=F32)
    left = sigmoid(projected[:CHAN]) * projected[CHAN : 2 * CHAN]
    right = sigmoid(projected[2 * CHAN : 3 * CHAN]) * projected[3 * CHAN :]
    for index in range(len(rows)):
        place = pl.ds((first + index) * CHAN_PITCH, CHAN)
        lanes = slice(index * COLS, (index + 1) * COLS)
        left_scratch[place, :] = left[:, lanes]
        right_scratch[place, :] = right[:, lanes]


def emit_projections(left_scratch, right_scratch, out_ref, first=0, count=CHAN):
    def body(chan, carry):
        place = pl.ds(chan, ROWS, stride=CHAN_PITCH)
        out_ref[chan, 0] = left_scratch[place, :].astype(BF16)
        out_ref[chan, 1] = right_scratch[place, :].astype(BF16)
        return carry

    lax.fori_loop(first, first + count, body, 0, unroll=8)


def project_kernel(
    mask_hbm, gain_hbm, cells_hbm, weight_hbm, pairs_hbm, turned_hbm,
    cells_ref, weight_ref, mask_ref, gain_ref, weight_turned, row_masks, left, right, pairs_ref, turned_ref, sems,
):
    chunks = ROWS // CHUNK
    rows_of = [pl.ds(index * CHUNK, CHUNK) for index in range(chunks)]
    small_copies = [
        pltpu.make_async_copy(weight_hbm.at[0], weight_ref, sems.at[0]),
        pltpu.make_async_copy(mask_hbm, mask_ref, sems.at[1]),
        pltpu.make_async_copy(gain_hbm, gain_ref, sems.at[2]),
    ]
    cell_copies = [
        pltpu.make_async_copy(cells_hbm.at[rows], cells_ref.at[rows], sems.at[3 + index])
        for index, rows in enumerate(rows_of)
    ]
    turned_copies = [
        pltpu.make_async_copy(turned_ref.at[rows], turned_hbm.at[rows], sems.at[3 + chunks + index])
        for index, rows in enumerate(rows_of)
    ]
    for copy in small_copies + cell_copies:
        copy.start()
    for copy in small_copies:
        copy.wait()
    gain_mask = masked_gain(gain_ref, 0, mask_ref)
    set_row_masks(mask_ref, row_masks)
    weight_turned[...] = jnp.transpose(weight_ref[...])
    for first in range(0, ROWS, SUB):
        if first % CHUNK == 0:
            cell_copies[first // CHUNK].wait()
        rows = []
        for index in range(first, first + SUB):
            row = jnp.transpose(cells_ref[index])
            turned_ref[index] = row
            rows.append(row.astype(F32))
        if (first + SUB) % CHUNK == 0:
            turned_copies[first // CHUNK].start()
        masks = [row_mask(row_masks, first + index) for index in range(SUB)]
        project_rows(rows, masks, gain_mask, weight_turned, left, right, first)
    pair_copies = []
    for first in range(0, CHAN, SPAN):
        emit_projections(left, right, pairs_ref, first, SPAN)
        span = pl.ds(first, SPAN)
        pair_copies.append(
            pltpu.make_async_copy(
                pairs_ref.at[span], pairs_hbm.at[span], sems.at[3 + 2 * chunks + first // SPAN]
            )
        )
        pair_copies[-1].start()
    for copy in turned_copies + pair_copies:
        copy.wait()


def project(mask, gain, cells, weight):
    return pl.pallas_call(
        project_kernel,
        in_specs=[HBM, HBM, HBM, HBM],
        out_specs=[HBM, HBM],
        out_shape=[PAIRS, TURNED],
        scratch_shapes=[
            pltpu.VMEM((ROWS, COLS, CHAN), BF16),
            pltpu.VMEM((CHAN, 4 * CHAN), BF16),
            pltpu.VMEM(mask.shape, jnp.int32),
            pltpu.VMEM(gain.shape, F32),
            pltpu.VMEM((4 * CHAN, CHAN), BF16),
            *PROJ_SCRATCH,
            pltpu.VMEM(PAIRS.shape, BF16),
            pltpu.VMEM(TURNED.shape, BF16),
            pltpu.SemaphoreType.DMA((3 + 2 * (ROWS // CHUNK) + CHAN // SPAN,)),
        ],
        compiler_params=pltpu.CompilerParams(vmem_limit_bytes=56 * MIB),
        name="project",
    )(mask, gain, cells, weight)


def gate_kernel(module, gain_ref, cells_ref, weight_ref, out_ref):
    gain = channel_column(gain_ref, module)
    weight = jnp.transpose(weight_ref[module])
    for first in range(0, ROWS, SUB):
        rows = [layer_norm(cells_ref[first + index].astype(F32), gain).astype(BF16) for index in range(SUB)]
        gate = sigmoid(jnp.dot(weight, jnp.concatenate(rows, axis=1), preferred_element_type=F32))
        for index in range(SUB):
            out_ref[first + index] = gate[:, index * COLS : (index + 1) * COLS]


def output_gate(module, gain, cells, weight):
    call = kernel_call(
        functools.partial(gate_kernel, module),
        "output_gate",
        [VMEM, VMEM, VMEM],
        GATE,
        cost=pl.CostEstimate(
            flops=2 * ROWS * COLS * CHAN * CHAN, bytes_accessed=3 << 20, transcendentals=ROWS * COLS * CHAN
        ),
    )
    return call(gain, cells, weight)


def normed_hidden_rows(module, gain_ref, hidden_ref, gains, scratch):
    gains[...] = channel_column(gain_ref, module)
    for first in range(0, ROWS, 16):
        rows = slice(first, first + 16)
        hidden = hidden_ref[:, :, rows].astype(F32).reshape(CHAN, 16, COLS)
        average = jnp.mean(hidden, axis=0)
        centred = hidden - average[None]
        scale = lax.rsqrt(jnp.mean(centred * centred, axis=0) + EPSILON)

        def body(chip, carry):
            for plane in range(DEPTH):
                chan = plane * CHIPS + chip
                values = (hidden_ref[chip, plane, rows].astype(F32) - average) * scale
                scratch[pl.ds(chan * ROW_PITCH + first, 16), :] = values * gains[pl.ds(chan, 1), :]
            return carry

        lax.fori_loop(0, CHIPS, body, 0)


def updated_rows(first, scratch, weight, cells_ref, gate_ref):
    hidden = [
        scratch[pl.ds(first + index, CHAN, stride=ROW_PITCH), :].astype(BF16) for index in range(SUB)
    ]
    update = jnp.dot(weight, jnp.concatenate(hidden, axis=1), preferred_element_type=F32)
    return [
        (
            cells_ref[first + index].astype(F32)
            + gate_ref[first + index] * update[:, index * COLS : (index + 1) * COLS]
        ).astype(BF16)
        for index in range(SUB)
    ]


def finish_kernel(gain_ref, hidden_ref, cells_ref, gate_ref, weight_ref, out_hbm, gains, scratch, out_ref, sems):
    normed_hidden_rows(1, gain_ref, hidden_ref, gains, scratch)
    weight = jnp.transpose(weight_ref[1])
    copies = []
    for first in range(0, ROWS, SUB):
        for index, row in enumerate(updated_rows(first, scratch, weight, cells_ref, gate_ref)):
            out_ref[first + index] = jnp.transpose(row)
        if (first + SUB) % CHUNK == 0:
            rows = pl.ds(first + SUB - CHUNK, CHUNK)
            copies.append(pltpu.make_async_copy(out_ref.at[rows], out_hbm.at[rows], sems.at[first // CHUNK]))
            copies[-1].start()
    for copy in copies:
        copy.wait()


def finish(gain, hidden, cells, gate, weight):
    return pl.pallas_call(
        finish_kernel,
        in_specs=[VMEM] * 5,
        out_specs=HBM,
        out_shape=CELLS,
        scratch_shapes=[
            *HIDDEN_SCRATCH,
            pltpu.VMEM((ROWS, COLS, CHAN), BF16),
            pltpu.SemaphoreType.DMA((ROWS // CHUNK,)),
        ],
        compiler_params=pltpu.CompilerParams(vmem_limit_bytes=40 * MIB),
        name="finish",
    )(gain, hidden, cells, gate, weight)


def finish_project_kernel(
    mask_ref, in_gain_ref, out_gain_ref, hidden_ref, cells_ref, gate_ref, weight_ref, proj_ref,
    cells_out, pairs_out, gains, scratch, proj_turned, row_masks, left, right,
):
    gain_mask = masked_gain(in_gain_ref, 1, mask_ref)
    set_row_masks(mask_ref, row_masks)
    normed_hidden_rows(0, out_gain_ref, hidden_ref, gains, scratch)
    weight = jnp.transpose(weight_ref[0])
    proj_turned[...] = jnp.transpose(proj_ref[1])
    for first in range(0, ROWS, SUB):
        rows = updated_rows(first, scratch, weight, cells_ref, gate_ref)
        for index, row in enumerate(rows):
            cells_out[first + index] = row
        masks = [row_mask(row_masks, first + index) for index in range(SUB)]
        rows = [row.astype(F32) for row in rows]
        project_rows(rows, masks, gain_mask, proj_turned, left, right, first)
    emit_projections(left, right, pairs_out)


def finish_project(mask, in_gain, out_gain, hidden, cells, gate, weight, proj):
    call = kernel_call(
        finish_project_kernel,
        "finish_project",
        [VMEM] * 8,
        [TURNED, PAIRS],
        HIDDEN_SCRATCH + [pltpu.VMEM((4 * CHAN, CHAN), BF16)] + PROJ_SCRATCH,
    )
    return call(mask, in_gain, out_gain, hidden, cells, gate, weight, proj)


TOKENS = BLOCKS * COLS
HALF = GROUPS * ROWS
PRODUCT = jax.ShapeDtypeStruct((DEPTH, 2, BLOCKS, ROWS, COLS), BF16)


def block_lanes(block):
    return slice(block * COLS, (block + 1) * COLS)


def side(pairs_ref, block, which):
    return pairs_ref[:, block, :, which].reshape(GROUPS, ROWS, COLS)


def take_right_kernel(pairs_ref, out_ref):
    for block in range(BLOCKS):
        out_ref[:, block] = side(pairs_ref, block, 1)


def take_right(pairs):
    shape = jax.ShapeDtypeStruct((GROUPS, BLOCKS, ROWS, COLS), BF16)
    return kernel_call(take_right_kernel, "take_right", [VMEM], shape)(pairs)


def store_product(product, out_ref, block):
    for half in range(2):
        columns = product[:, block_lanes(half)].reshape(2, DEPTH, ROWS, COLS)
        for side_x in range(2):
            out_ref[:, side_x, block + half] = columns[side_x]


def outgoing_kernel(pairs_ref, other_ref, out_ref, left, right):
    core = lax.axis_index("c")
    for block in range(BLOCKS):
        left[:, :, block_lanes(block)] = side(pairs_ref, block, 0)
        right[:, core, :, block_lanes(block)] = side(pairs_ref, block, 1)
        right[:, 1 - core, :, block_lanes(block)] = other_ref[:, block]
    left_rows = left[...].reshape(HALF, TOKENS)
    for block in range(0, BLOCKS, 2):
        groups = slice(block * 2, block * 2 + 4)
        product = lax.dot_general(
            left_rows,
            right[groups].reshape(2 * COLS, TOKENS),
            (((1,), (1,)), ((), ())),
            preferred_element_type=F32,
        ).astype(BF16)
        store_product(product, out_ref, block)


def outgoing(pairs, other):
    call = kernel_call(
        outgoing_kernel,
        "outgoing",
        [VMEM, VMEM],
        PRODUCT,
        [pltpu.VMEM((GROUPS, ROWS, TOKENS), BF16), pltpu.VMEM((GROUPS, 2, ROWS, TOKENS), BF16)],
    )
    return call(pairs, other)


def incoming_send_kernel(pairs_ref, send_ref, left_ref, right_ref, turned):
    core = lax.axis_index("c")
    for block in range(BLOCKS):
        right_ref[:, block_lanes(block)] = side(pairs_ref, block, 1).reshape(HALF, COLS)
        left = side(pairs_ref, block, 0).reshape(HALF, COLS)
        turned[2 * block : 2 * block + 2] = jnp.transpose(left).reshape(2, 2, ROWS, HALF)
    left_ref[...] = turned[:, core].reshape(HALF, HALF)
    send_ref[...] = jnp.dot(
        turned[:, 1 - core].reshape(HALF, HALF), right_ref[...], preferred_element_type=F32
    ).astype(BF16)


def incoming_send(pairs):
    call = kernel_call(
        incoming_send_kernel,
        "incoming_send",
        [VMEM],
        [
            jax.ShapeDtypeStruct((HALF, TOKENS), BF16),
            jax.ShapeDtypeStruct((HALF, HALF), BF16),
            jax.ShapeDtypeStruct((HALF, TOKENS), BF16),
        ],
        [pltpu.VMEM((GROUPS, 2, ROWS, HALF), BF16)],
    )
    return call(pairs)


def incoming_kernel(left_ref, right_ref, other_ref, out_ref):
    left = left_ref[...]
    for block in range(0, BLOCKS, 2):
        lanes = slice(block * COLS, (block + 2) * COLS)
        total = jnp.dot(left, right_ref[:, lanes], preferred_element_type=F32)
        product = (total + other_ref[:, lanes].astype(F32)).astype(BF16)
        store_product(product, out_ref, block)


def incoming(left, right, other):
    return kernel_call(incoming_kernel, "incoming", [VMEM, VMEM, VMEM], PRODUCT)(left, right, other)


def planes_first(pairs):
    pairs = jnp.swapaxes(lax.all_to_all(pairs, "z", split_axis=0, concat_axis=0, tiled=True), 0, 1)
    return lax.all_to_all(pairs, PLANE, split_axis=0, concat_axis=0, tiled=True)


def planes_last(pairs):
    pairs = jnp.swapaxes(pairs, 0, 1)
    pairs = jnp.swapaxes(lax.all_to_all(pairs, PLANE, split_axis=0, concat_axis=0, tiled=True), 0, 1)
    return jnp.swapaxes(lax.all_to_all(pairs, "z", split_axis=0, concat_axis=0, tiled=True), 0, 1)


def exchange(values, first_core):
    return lax.cond(lax.axis_index("c") == first_core, planes_first, planes_last, values)


def exchange_pairs(pairs, first_core):
    pairs = exchange(pairs.reshape(DEPTH, CHIPS, 2 * ROWS, COLS), first_core)
    return pairs.reshape(2, BLOCKS, DEPTH, 2, ROWS, COLS)


def exchange_product(product, first_core):
    return exchange(product.reshape(DEPTH, CHIPS, ROWS, COLS), first_core)


def to_other_core(values):
    return lax.ppermute(values, "c", [(0, 1), (1, 0)])


def per_device(pair_input, token_mask, in_gain, proj_weight, gate_weight, out_gain, out_weight):
    mask = token_mask.reshape(BLOCKS, COLS)

    pairs, cells = project(mask, in_gain, pair_input, proj_weight)
    pairs = exchange_pairs(pairs, 0)
    other = to_other_core(take_right(pairs))
    gate = output_gate(0, in_gain, cells, gate_weight)
    product, gate = lax.optimization_barrier((outgoing(pairs, other), gate))
    hidden = exchange_product(product, 0)
    cells, pairs = finish_project(mask, in_gain, out_gain, hidden, cells, gate, out_weight, proj_weight)

    pairs = exchange_pairs(pairs, 1)
    send, left, right = incoming_send(pairs)
    other = to_other_core(send)
    gate = output_gate(1, in_gain, cells, gate_weight)
    product, gate = lax.optimization_barrier((incoming(left, right, other), gate))
    hidden = exchange_product(product, 0)
    return finish(out_gain, hidden, cells, gate, out_weight)


def solution(mesh):
    split = Mesh(mesh.devices.reshape(2, 8, 2, 2, 4), ("xh", "z", "c", "xl", "y"))
    cells = P(("xh", "z", "c"), ("xl", "y"), None)
    return jax.shard_map(
        per_device, mesh=split, in_specs=(cells, P(), P(), P(), P(), P(), P()), out_specs=cells, check_vma=False
    )
```

```python
import functools

import jax
import jax.numpy as jnp
from jax import lax
from jax.experimental import pallas as pl
from jax.experimental.pallas import tpu as pltpu
from jax.sharding import Mesh, PartitionSpec as P

EPSILON = 1e-05
CHAN = 128
ROWS = 32
COLS = 128
GROUPS = 16
DEPTH = 8
CHIPS = 16
BLOCKS = 8
SUB = 16
CHUNK = 16
SPAN = 32
CHAN_PITCH = CHAN + 1
ROW_PITCH = ROWS + 1
PLANE = ("xh", "xl", "y")
F32 = jnp.float32
BF16 = jnp.bfloat16
MIB = 1024 * 1024


def sigmoid(values):
    return 0.5 * jnp.tanh(0.5 * values) + 0.5


VMEM = pl.BlockSpec(memory_space=pltpu.VMEM)


def kernel_call(kernel, name, in_specs, out_shape, scratch_shapes=(), cost=None, vmem=40):
    return pl.pallas_call(
        kernel,
        in_specs=in_specs,
        out_specs=jax.tree.map(lambda _: VMEM, out_shape),
        out_shape=out_shape,
        scratch_shapes=scratch_shapes,
        compiler_params=pltpu.CompilerParams(vmem_limit_bytes=vmem * MIB),
        cost_estimate=cost,
        name=name,
    )


HBM = pl.BlockSpec(memory_space=pltpu.HBM)
PROJ_SCRATCH = [pltpu.VMEM((COLS, COLS), F32)] + [pltpu.VMEM((ROWS * CHAN_PITCH + CHAN, COLS), F32)] * 2
HIDDEN_SCRATCH = [pltpu.VMEM((CHAN, COLS), F32), pltpu.VMEM((CHAN * ROW_PITCH + ROWS, COLS), F32)]
PAIRS = jax.ShapeDtypeStruct((CHAN, 2, ROWS, COLS), BF16)
CELLS = jax.ShapeDtypeStruct((ROWS, COLS, CHAN), BF16)
TURNED = jax.ShapeDtypeStruct((ROWS, CHAN, COLS), BF16)
GATE = jax.ShapeDtypeStruct((ROWS, CHAN, COLS), F32)


def layer_norm(turned, factor):
    average = jnp.mean(turned, axis=0, keepdims=True)
    centred = turned - average
    variance = jnp.mean(centred * centred, axis=0, keepdims=True)
    return centred * lax.rsqrt(variance + EPSILON) * factor


def channel_column(gain_ref, module):
    return jnp.transpose(jnp.broadcast_to(gain_ref[module : module + 1, :], (COLS, CHAN)))


def masked_gain(gain_ref, module, col_mask_ref):
    block = lax.axis_index(("xl", "y"))
    return channel_column(gain_ref, module) * col_mask_ref[pl.ds(block, 1), :].astype(F32)


def set_row_masks(mask_ref, scratch):
    block = lax.axis_index(("xh", "z", "c")) // (COLS // ROWS)
    tokens = jnp.broadcast_to(mask_ref[pl.ds(block, 1), :].astype(F32), (COLS, COLS))
    scratch[...] = jnp.transpose(tokens)


def row_mask(scratch, index):
    start = lax.axis_index(("xh", "z", "c")) % (COLS // ROWS) * ROWS
    return scratch[pl.ds(start + index, 1), :]


def project_rows(rows, row_masks, gain_mask, weight, left_scratch, right_scratch, first):
    normed = [layer_norm(row, gain_mask * mask).astype(BF16) for row, mask in zip(rows, row_masks)]
    projected = jnp.dot(weight[...], jnp.concatenate(normed, axis=1), preferred_element_type=F32)
    left = sigmoid(projected[:CHAN]) * projected[CHAN : 2 * CHAN]
    right = sigmoid(projected[2 * CHAN : 3 * CHAN]) * projected[3 * CHAN :]
    for index in range(len(rows)):
        place = pl.ds((first + index) * CHAN_PITCH, CHAN)
        lanes = slice(index * COLS, (index + 1) * COLS)
        left_scratch[place, :] = left[:, lanes]
        right_scratch[place, :] = right[:, lanes]


def emit_projections(left_scratch, right_scratch, out_ref, first=0, count=CHAN):
    def body(chan, carry):
        place = pl.ds(chan, ROWS, stride=CHAN_PITCH)
        out_ref[chan, 0] = left_scratch[place, :].astype(BF16)
        out_ref[chan, 1] = right_scratch[place, :].astype(BF16)
        return carry

    lax.fori_loop(first, first + count, body, 0, unroll=8)


def project_kernel(
    mask_hbm, gain_hbm, cells_hbm, weight_hbm, pairs_hbm, turned_hbm,
    cells_ref, weight_ref, mask_ref, gain_ref, weight_turned, row_masks, left, right, pairs_ref, turned_ref, sems,
):
    chunks = ROWS // CHUNK
    rows_of = [pl.ds(index * CHUNK, CHUNK) for index in range(chunks)]
    small_copies = [
        pltpu.make_async_copy(weight_hbm.at[0], weight_ref, sems.at[0]),
        pltpu.make_async_copy(mask_hbm, mask_ref, sems.at[1]),
        pltpu.make_async_copy(gain_hbm, gain_ref, sems.at[2]),
    ]
    cell_copies = [
        pltpu.make_async_copy(cells_hbm.at[rows], cells_ref.at[rows], sems.at[3 + index])
        for index, rows in enumerate(rows_of)
    ]
    turned_copies = [
        pltpu.make_async_copy(turned_ref.at[rows], turned_hbm.at[rows], sems.at[3 + chunks + index])
        for index, rows in enumerate(rows_of)
    ]
    for copy in small_copies + cell_copies:
        copy.start()
    for copy in small_copies:
        copy.wait()
    gain_mask = masked_gain(gain_ref, 0, mask_ref)
    set_row_masks(mask_ref, row_masks)
    weight_turned[...] = jnp.transpose(weight_ref[...])
    for first in range(0, ROWS, SUB):
        if first % CHUNK == 0:
            cell_copies[first // CHUNK].wait()
        rows = []
        for index in range(first, first + SUB):
            row = jnp.transpose(cells_ref[index])
            turned_ref[index] = row
            rows.append(row.astype(F32))
        if (first + SUB) % CHUNK == 0:
            turned_copies[first // CHUNK].start()
        masks = [row_mask(row_masks, first + index) for index in range(SUB)]
        project_rows(rows, masks, gain_mask, weight_turned, left, right, first)
    pair_copies = []
    for first in range(0, CHAN, SPAN):
        emit_projections(left, right, pairs_ref, first, SPAN)
        span = pl.ds(first, SPAN)
        pair_copies.append(
            pltpu.make_async_copy(
                pairs_ref.at[span], pairs_hbm.at[span], sems.at[3 + 2 * chunks + first // SPAN]
            )
        )
        pair_copies[-1].start()
    for copy in turned_copies + pair_copies:
        copy.wait()


def project(mask, gain, cells, weight):
    return pl.pallas_call(
        project_kernel,
        in_specs=[HBM, HBM, HBM, HBM],
        out_specs=[HBM, HBM],
        out_shape=[PAIRS, TURNED],
        scratch_shapes=[
            pltpu.VMEM((ROWS, COLS, CHAN), BF16),
            pltpu.VMEM((CHAN, 4 * CHAN), BF16),
            pltpu.VMEM(mask.shape, jnp.int32),
            pltpu.VMEM(gain.shape, F32),
            pltpu.VMEM((4 * CHAN, CHAN), BF16),
            *PROJ_SCRATCH,
            pltpu.VMEM(PAIRS.shape, BF16),
            pltpu.VMEM(TURNED.shape, BF16),
            pltpu.SemaphoreType.DMA((3 + 2 * (ROWS // CHUNK) + CHAN // SPAN,)),
        ],
        compiler_params=pltpu.CompilerParams(vmem_limit_bytes=56 * MIB),
        name="project",
    )(mask, gain, cells, weight)


def gate_kernel(module, gain_ref, cells_ref, weight_ref, out_ref):
    gain = channel_column(gain_ref, module)
    weight = jnp.transpose(weight_ref[module])
    for first in range(0, ROWS, SUB):
        rows = [layer_norm(cells_ref[first + index].astype(F32), gain).astype(BF16) for index in range(SUB)]
        gate = sigmoid(jnp.dot(weight, jnp.concatenate(rows, axis=1), preferred_element_type=F32))
        for index in range(SUB):
            out_ref[first + index] = gate[:, index * COLS : (index + 1) * COLS]


def output_gate(module, gain, cells, weight):
    call = kernel_call(
        functools.partial(gate_kernel, module),
        "output_gate",
        [VMEM, VMEM, VMEM],
        GATE,
        cost=pl.CostEstimate(
            flops=2 * ROWS * COLS * CHAN * CHAN, bytes_accessed=3 << 20, transcendentals=ROWS * COLS * CHAN
        ),
    )
    return call(gain, cells, weight)


def normed_hidden_rows(module, gain_ref, hidden_ref, gains, scratch):
    gains[...] = channel_column(gain_ref, module)
    for first in range(0, ROWS, 16):
        rows = slice(first, first + 16)
        hidden = hidden_ref[:, :, rows].astype(F32).reshape(CHAN, 16, COLS)
        average = jnp.mean(hidden, axis=0)
        centred = hidden - average[None]
        scale = lax.rsqrt(jnp.mean(centred * centred, axis=0) + EPSILON)

        def body(chip, carry):
            for plane in range(DEPTH):
                chan = plane * CHIPS + chip
                place = (plane, chip) if module == 0 else (chip, plane)
                values = (hidden_ref[place + (rows,)].astype(F32) - average) * scale
                scratch[pl.ds(chan * ROW_PITCH + first, 16), :] = values * gains[pl.ds(chan, 1), :]
            return carry

        lax.fori_loop(0, CHIPS, body, 0)


def updated_rows(first, scratch, weight, cells_ref, gate_ref):
    hidden = [
        scratch[pl.ds(first + index, CHAN, stride=ROW_PITCH), :].astype(BF16) for index in range(SUB)
    ]
    update = jnp.dot(weight, jnp.concatenate(hidden, axis=1), preferred_element_type=F32)
    return [
        (
            cells_ref[first + index].astype(F32)
            + gate_ref[first + index] * update[:, index * COLS : (index + 1) * COLS]
        ).astype(BF16)
        for index in range(SUB)
    ]


def finish_kernel(gain_ref, hidden_ref, cells_ref, gate_ref, weight_ref, out_hbm, gains, scratch, out_ref, sems):
    normed_hidden_rows(1, gain_ref, hidden_ref, gains, scratch)
    weight = jnp.transpose(weight_ref[1])
    copies = []
    for first in range(0, ROWS, SUB):
        for index, row in enumerate(updated_rows(first, scratch, weight, cells_ref, gate_ref)):
            out_ref[first + index] = jnp.transpose(row)
        if (first + SUB) % CHUNK == 0:
            rows = pl.ds(first + SUB - CHUNK, CHUNK)
            copies.append(pltpu.make_async_copy(out_ref.at[rows], out_hbm.at[rows], sems.at[first // CHUNK]))
            copies[-1].start()
    for copy in copies:
        copy.wait()


def finish(gain, hidden, cells, gate, weight):
    return pl.pallas_call(
        finish_kernel,
        in_specs=[VMEM] * 5,
        out_specs=HBM,
        out_shape=CELLS,
        scratch_shapes=[
            *HIDDEN_SCRATCH,
            pltpu.VMEM((ROWS, COLS, CHAN), BF16),
            pltpu.SemaphoreType.DMA((ROWS // CHUNK,)),
        ],
        compiler_params=pltpu.CompilerParams(vmem_limit_bytes=40 * MIB),
        name="finish",
    )(gain, hidden, cells, gate, weight)


def finish_project_kernel(
    mask_ref, in_gain_ref, out_gain_ref, hidden_ref, cells_ref, gate_ref, weight_ref, proj_ref,
    cells_out, pairs_out, gains, scratch, proj_turned, row_masks, left, right,
):
    gain_mask = masked_gain(in_gain_ref, 1, mask_ref)
    set_row_masks(mask_ref, row_masks)
    normed_hidden_rows(0, out_gain_ref, hidden_ref, gains, scratch)
    weight = jnp.transpose(weight_ref[0])
    proj_turned[...] = jnp.transpose(proj_ref[1])
    for first in range(0, ROWS, SUB):
        rows = updated_rows(first, scratch, weight, cells_ref, gate_ref)
        for index, row in enumerate(rows):
            cells_out[first + index] = row
        masks = [row_mask(row_masks, first + index) for index in range(SUB)]
        rows = [row.astype(F32) for row in rows]
        project_rows(rows, masks, gain_mask, proj_turned, left, right, first)
    emit_projections(left, right, pairs_out)


def finish_project(mask, in_gain, out_gain, hidden, cells, gate, weight, proj):
    call = kernel_call(
        finish_project_kernel,
        "finish_project",
        [VMEM] * 8,
        [TURNED, PAIRS],
        HIDDEN_SCRATCH + [pltpu.VMEM((4 * CHAN, CHAN), BF16)] + PROJ_SCRATCH,
    )
    return call(mask, in_gain, out_gain, hidden, cells, gate, weight, proj)


TOKENS = BLOCKS * COLS
HALF = GROUPS * ROWS
PRODUCT = jax.ShapeDtypeStruct((DEPTH, 2, BLOCKS, ROWS, COLS), BF16)


def block_lanes(block):
    return slice(block * COLS, (block + 1) * COLS)


def side(pairs_ref, block, which):
    return pairs_ref[:, block, :, which].reshape(GROUPS, ROWS, COLS)


def take_right_kernel(pairs_ref, out_ref):
    for block in range(BLOCKS):
        out_ref[:, block] = side(pairs_ref, block, 1)


def take_right(pairs):
    shape = jax.ShapeDtypeStruct((GROUPS, BLOCKS, ROWS, COLS), BF16)
    return kernel_call(take_right_kernel, "take_right", [VMEM], shape)(pairs)


def store_product(product, out_ref, block):
    for half in range(2):
        columns = product[:, block_lanes(half)].reshape(2, DEPTH, ROWS, COLS)
        for side_x in range(2):
            out_ref[:, side_x, block + half] = columns[side_x]


def outgoing_kernel(pairs_ref, other_ref, out_ref, left, right):
    core = lax.axis_index("c")
    for block in range(BLOCKS):
        left[:, :, block_lanes(block)] = side(pairs_ref, block, 0)
        right[:, core, :, block_lanes(block)] = side(pairs_ref, block, 1)
        right[:, 1 - core, :, block_lanes(block)] = other_ref[:, block]
    left_rows = left[...].reshape(HALF, TOKENS)
    for block in range(0, BLOCKS, 2):
        groups = slice(block * 2, block * 2 + 4)
        product = lax.dot_general(
            left_rows,
            right[groups].reshape(2 * COLS, TOKENS),
            (((1,), (1,)), ((), ())),
            preferred_element_type=F32,
        ).astype(BF16)
        store_product(product, out_ref, block)


def outgoing(pairs, other):
    call = kernel_call(
        outgoing_kernel,
        "outgoing",
        [VMEM, VMEM],
        PRODUCT,
        [pltpu.VMEM((GROUPS, ROWS, TOKENS), BF16), pltpu.VMEM((GROUPS, 2, ROWS, TOKENS), BF16)],
    )
    return call(pairs, other)


def incoming_send_kernel(pairs_ref, send_ref, left_ref, right_ref, turned):
    core = lax.axis_index("c")
    for block in range(BLOCKS):
        right_ref[:, block_lanes(block)] = side(pairs_ref, block, 1).reshape(HALF, COLS)
        left = side(pairs_ref, block, 0).reshape(HALF, COLS)
        turned[2 * block : 2 * block + 2] = jnp.transpose(left).reshape(2, 2, ROWS, HALF)
    left_ref[...] = turned[:, core].reshape(HALF, HALF)
    send_ref[...] = jnp.dot(
        turned[:, 1 - core].reshape(HALF, HALF), right_ref[...], preferred_element_type=F32
    ).astype(BF16)


def incoming_send(pairs):
    call = kernel_call(
        incoming_send_kernel,
        "incoming_send",
        [VMEM],
        [
            jax.ShapeDtypeStruct((HALF, TOKENS), BF16),
            jax.ShapeDtypeStruct((HALF, HALF), BF16),
            jax.ShapeDtypeStruct((HALF, TOKENS), BF16),
        ],
        [pltpu.VMEM((GROUPS, 2, ROWS, HALF), BF16)],
    )
    return call(pairs)


def incoming_kernel(left_ref, right_ref, other_ref, out_ref):
    left = left_ref[...]
    for block in range(0, BLOCKS, 2):
        lanes = slice(block * COLS, (block + 2) * COLS)
        total = jnp.dot(left, right_ref[:, lanes], preferred_element_type=F32)
        product = (total + other_ref[:, lanes].astype(F32)).astype(BF16)
        store_product(product, out_ref, block)


def incoming(left, right, other):
    return kernel_call(incoming_kernel, "incoming", [VMEM, VMEM, VMEM], PRODUCT)(left, right, other)


def planes_first(pairs):
    pairs = jnp.swapaxes(lax.all_to_all(pairs, "z", split_axis=0, concat_axis=0, tiled=True), 0, 1)
    return lax.all_to_all(pairs, PLANE, split_axis=0, concat_axis=0, tiled=True)


def planes_last(pairs):
    pairs = jnp.swapaxes(pairs, 0, 1)
    pairs = jnp.swapaxes(lax.all_to_all(pairs, PLANE, split_axis=0, concat_axis=0, tiled=True), 0, 1)
    return jnp.swapaxes(lax.all_to_all(pairs, "z", split_axis=0, concat_axis=0, tiled=True), 0, 1)


def exchange(values, first_core):
    return lax.cond(lax.axis_index("c") == first_core, planes_first, planes_last, values)


def exchange_pairs(pairs, first_core):
    pairs = exchange(pairs.reshape(DEPTH, CHIPS, 2 * ROWS, COLS), first_core)
    return pairs.reshape(2, BLOCKS, DEPTH, 2, ROWS, COLS)


def exchange_product(product, first_core):
    return exchange(product.reshape(DEPTH, CHIPS, ROWS, COLS), first_core)


def exchange_at_once(product):
    flat = product.reshape(CHAN, ROWS, COLS)
    flat = lax.all_to_all(flat, ("z",) + PLANE, split_axis=0, concat_axis=0, tiled=True)
    return flat.reshape(DEPTH, CHIPS, ROWS, COLS)


def to_other_core(values):
    return lax.ppermute(values, "c", [(0, 1), (1, 0)])


def per_device(pair_input, token_mask, in_gain, proj_weight, gate_weight, out_gain, out_weight):
    mask = token_mask.reshape(BLOCKS, COLS)

    pairs, cells = project(mask, in_gain, pair_input, proj_weight)
    pairs = exchange_pairs(pairs, 0)
    other = to_other_core(take_right(pairs))
    gate = output_gate(0, in_gain, cells, gate_weight)
    product, gate = lax.optimization_barrier((outgoing(pairs, other), gate))
    hidden = exchange_at_once(product)
    cells, pairs = finish_project(mask, in_gain, out_gain, hidden, cells, gate, out_weight, proj_weight)

    pairs = exchange_pairs(pairs, 1)
    send, left, right = incoming_send(pairs)
    other = to_other_core(send)
    gate = output_gate(1, in_gain, cells, gate_weight)
    product, gate = lax.optimization_barrier((incoming(left, right, other), gate))
    hidden = exchange_product(product, 0)
    return finish(out_gain, hidden, cells, gate, out_weight)


def solution(mesh):
    split = Mesh(mesh.devices.reshape(2, 8, 2, 2, 4), ("xh", "z", "c", "xl", "y"))
    cells = P(("xh", "z", "c"), ("xl", "y"), None)
    return jax.shard_map(
        per_device, mesh=split, in_specs=(cells, P(), P(), P(), P(), P(), P()), out_specs=cells, check_vma=False
    )
```

```python
import functools

import jax
import jax.numpy as jnp
from jax import lax
from jax.experimental import pallas as pl
from jax.experimental.pallas import tpu as pltpu
from jax.sharding import Mesh, PartitionSpec as P

EPSILON = 1e-05
CHAN = 128
ROWS = 32
COLS = 128
GROUPS = 16
DEPTH = 8
CHIPS = 16
BLOCKS = 8
SUB = 16
CHUNK = 16
SPAN = 32
CHAN_PITCH = CHAN + 1
ROW_PITCH = ROWS + 1
PLANE = ("xh", "xl", "y")
F32 = jnp.float32
BF16 = jnp.bfloat16
MIB = 1024 * 1024


def sigmoid(values):
    return 0.5 * jnp.tanh(0.5 * values) + 0.5


VMEM = pl.BlockSpec(memory_space=pltpu.VMEM)


def kernel_call(kernel, name, in_specs, out_shape, scratch_shapes=(), cost=None, vmem=40):
    return pl.pallas_call(
        kernel,
        in_specs=in_specs,
        out_specs=jax.tree.map(lambda _: VMEM, out_shape),
        out_shape=out_shape,
        scratch_shapes=scratch_shapes,
        compiler_params=pltpu.CompilerParams(vmem_limit_bytes=vmem * MIB),
        cost_estimate=cost,
        name=name,
    )


HBM = pl.BlockSpec(memory_space=pltpu.HBM)
PROJ_SCRATCH = [pltpu.VMEM((COLS, COLS), F32)] + [pltpu.VMEM((ROWS * CHAN_PITCH + CHAN, COLS), F32)] * 2
HIDDEN_SCRATCH = [pltpu.VMEM((CHAN, COLS), F32), pltpu.VMEM((CHAN * ROW_PITCH + ROWS, COLS), F32)]
PAIRS = jax.ShapeDtypeStruct((CHAN, 2, ROWS, COLS), BF16)
CELLS = jax.ShapeDtypeStruct((ROWS, COLS, CHAN), BF16)
TURNED = jax.ShapeDtypeStruct((ROWS, CHAN, COLS), BF16)
GATE = jax.ShapeDtypeStruct((ROWS, CHAN, COLS), F32)


def layer_norm(turned, factor):
    average = jnp.mean(turned, axis=0, keepdims=True)
    centred = turned - average
    variance = jnp.mean(centred * centred, axis=0, keepdims=True)
    return centred * lax.rsqrt(variance + EPSILON) * factor


def channel_column(gain_ref, module):
    return jnp.transpose(jnp.broadcast_to(gain_ref[module : module + 1, :], (COLS, CHAN)))


def masked_gain(gain_ref, module, col_mask_ref):
    block = lax.axis_index(("xl", "y"))
    return channel_column(gain_ref, module) * col_mask_ref[pl.ds(block, 1), :].astype(F32)


def set_row_masks(mask_ref, scratch):
    block = lax.axis_index(("xh", "z", "c")) // (COLS // ROWS)
    tokens = jnp.broadcast_to(mask_ref[pl.ds(block, 1), :].astype(F32), (COLS, COLS))
    scratch[...] = jnp.transpose(tokens)


def row_mask(scratch, index):
    start = lax.axis_index(("xh", "z", "c")) % (COLS // ROWS) * ROWS
    return scratch[pl.ds(start + index, 1), :]


def project_rows(rows, row_masks, gain_mask, weight, left_scratch, right_scratch, first):
    normed = [layer_norm(row, gain_mask * mask).astype(BF16) for row, mask in zip(rows, row_masks)]
    projected = jnp.dot(weight[...], jnp.concatenate(normed, axis=1), preferred_element_type=F32)
    left = sigmoid(projected[:CHAN]) * projected[CHAN : 2 * CHAN]
    right = sigmoid(projected[2 * CHAN : 3 * CHAN]) * projected[3 * CHAN :]
    for index in range(len(rows)):
        place = pl.ds((first + index) * CHAN_PITCH, CHAN)
        lanes = slice(index * COLS, (index + 1) * COLS)
        left_scratch[place, :] = left[:, lanes]
        right_scratch[place, :] = right[:, lanes]


def emit_projections(left_scratch, right_scratch, out_ref, first=0, count=CHAN):
    def body(chan, carry):
        place = pl.ds(chan, ROWS, stride=CHAN_PITCH)
        out_ref[chan, 0] = left_scratch[place, :].astype(BF16)
        out_ref[chan, 1] = right_scratch[place, :].astype(BF16)
        return carry

    lax.fori_loop(first, first + count, body, 0, unroll=8)


def project_kernel(
    mask_hbm, gain_hbm, cells_hbm, weight_hbm, pairs_hbm, turned_hbm,
    cells_ref, weight_ref, mask_ref, gain_ref, weight_turned, row_masks, left, right, pairs_ref, turned_ref, sems,
):
    chunks = ROWS // CHUNK
    rows_of = [pl.ds(index * CHUNK, CHUNK) for index in range(chunks)]
    small_copies = [
        pltpu.make_async_copy(weight_hbm.at[0], weight_ref, sems.at[0]),
        pltpu.make_async_copy(mask_hbm, mask_ref, sems.at[1]),
        pltpu.make_async_copy(gain_hbm, gain_ref, sems.at[2]),
    ]
    cell_copies = [
        pltpu.make_async_copy(cells_hbm.at[rows], cells_ref.at[rows], sems.at[3 + index])
        for index, rows in enumerate(rows_of)
    ]
    turned_copies = [
        pltpu.make_async_copy(turned_ref.at[rows], turned_hbm.at[rows], sems.at[3 + chunks + index])
        for index, rows in enumerate(rows_of)
    ]
    for copy in small_copies + cell_copies:
        copy.start()
    for copy in small_copies:
        copy.wait()
    gain_mask = masked_gain(gain_ref, 0, mask_ref)
    set_row_masks(mask_ref, row_masks)
    weight_turned[...] = jnp.transpose(weight_ref[...])
    for first in range(0, ROWS, SUB):
        if first % CHUNK == 0:
            cell_copies[first // CHUNK].wait()
        rows = []
        for index in range(first, first + SUB):
            row = jnp.transpose(cells_ref[index])
            turned_ref[index] = row
            rows.append(row.astype(F32))
        if (first + SUB) % CHUNK == 0:
            turned_copies[first // CHUNK].start()
        masks = [row_mask(row_masks, first + index) for index in range(SUB)]
        project_rows(rows, masks, gain_mask, weight_turned, left, right, first)
    pair_copies = []
    for first in range(0, CHAN, SPAN):
        emit_projections(left, right, pairs_ref, first, SPAN)
        span = pl.ds(first, SPAN)
        pair_copies.append(
            pltpu.make_async_copy(
                pairs_ref.at[span], pairs_hbm.at[span], sems.at[3 + 2 * chunks + first // SPAN]
            )
        )
        pair_copies[-1].start()
    for copy in turned_copies + pair_copies:
        copy.wait()


def project(mask, gain, cells, weight):
    return pl.pallas_call(
        project_kernel,
        in_specs=[HBM, HBM, HBM, HBM],
        out_specs=[HBM, HBM],
        out_shape=[PAIRS, TURNED],
        scratch_shapes=[
            pltpu.VMEM((ROWS, COLS, CHAN), BF16),
            pltpu.VMEM((CHAN, 4 * CHAN), BF16),
            pltpu.VMEM(mask.shape, jnp.int32),
            pltpu.VMEM(gain.shape, F32),
            pltpu.VMEM((4 * CHAN, CHAN), BF16),
            *PROJ_SCRATCH,
            pltpu.VMEM(PAIRS.shape, BF16),
            pltpu.VMEM(TURNED.shape, BF16),
            pltpu.SemaphoreType.DMA((3 + 2 * (ROWS // CHUNK) + CHAN // SPAN,)),
        ],
        compiler_params=pltpu.CompilerParams(vmem_limit_bytes=56 * MIB),
        name="project",
    )(mask, gain, cells, weight)


def gate_kernel(module, gain_ref, cells_ref, weight_ref, out_ref):
    gain = channel_column(gain_ref, module)
    weight = jnp.transpose(weight_ref[module])
    for first in range(0, ROWS, SUB):
        rows = [layer_norm(cells_ref[first + index].astype(F32), gain).astype(BF16) for index in range(SUB)]
        gate = sigmoid(jnp.dot(weight, jnp.concatenate(rows, axis=1), preferred_element_type=F32))
        for index in range(SUB):
            out_ref[first + index] = gate[:, index * COLS : (index + 1) * COLS]


def output_gate(module, gain, cells, weight):
    call = kernel_call(
        functools.partial(gate_kernel, module),
        "output_gate",
        [VMEM, VMEM, VMEM],
        GATE,
        cost=pl.CostEstimate(
            flops=2 * ROWS * COLS * CHAN * CHAN, bytes_accessed=3 << 20, transcendentals=ROWS * COLS * CHAN
        ),
    )
    return call(gain, cells, weight)


def normed_hidden_rows(module, gain_ref, hidden_ref, gains, scratch):
    gains[...] = channel_column(gain_ref, module)
    for first in range(0, ROWS, 16):
        rows = slice(first, first + 16)
        hidden = hidden_ref[:, :, rows].astype(F32).reshape(CHAN, 16, COLS)
        average = jnp.mean(hidden, axis=0)
        centred = hidden - average[None]
        scale = lax.rsqrt(jnp.mean(centred * centred, axis=0) + EPSILON)

        def body(chip, carry):
            for plane in range(DEPTH):
                chan = plane * CHIPS + chip
                place = (plane, chip) if module == 0 else (chip, plane)
                values = (hidden_ref[place + (rows,)].astype(F32) - average) * scale
                scratch[pl.ds(chan * ROW_PITCH + first, 16), :] = values * gains[pl.ds(chan, 1), :]
            return carry

        lax.fori_loop(0, CHIPS, body, 0)


def updated_rows(first, scratch, weight, cells_ref, gate_ref):
    hidden = [
        scratch[pl.ds(first + index, CHAN, stride=ROW_PITCH), :].astype(BF16) for index in range(SUB)
    ]
    update = jnp.dot(weight, jnp.concatenate(hidden, axis=1), preferred_element_type=F32)
    return [
        (
            cells_ref[first + index].astype(F32)
            + gate_ref[first + index] * update[:, index * COLS : (index + 1) * COLS]
        ).astype(BF16)
        for index in range(SUB)
    ]


def finish_kernel(gain_ref, hidden_ref, cells_ref, gate_ref, weight_ref, out_hbm, gains, scratch, out_ref, sems):
    normed_hidden_rows(1, gain_ref, hidden_ref, gains, scratch)
    weight = jnp.transpose(weight_ref[1])
    copies = []
    for first in range(0, ROWS, SUB):
        for index, row in enumerate(updated_rows(first, scratch, weight, cells_ref, gate_ref)):
            out_ref[first + index] = jnp.transpose(row)
        if (first + SUB) % CHUNK == 0:
            rows = pl.ds(first + SUB - CHUNK, CHUNK)
            copies.append(pltpu.make_async_copy(out_ref.at[rows], out_hbm.at[rows], sems.at[first // CHUNK]))
            copies[-1].start()
    for copy in copies:
        copy.wait()


def finish(gain, hidden, cells, gate, weight):
    return pl.pallas_call(
        finish_kernel,
        in_specs=[VMEM] * 5,
        out_specs=HBM,
        out_shape=CELLS,
        scratch_shapes=[
            *HIDDEN_SCRATCH,
            pltpu.VMEM((ROWS, COLS, CHAN), BF16),
            pltpu.SemaphoreType.DMA((ROWS // CHUNK,)),
        ],
        compiler_params=pltpu.CompilerParams(vmem_limit_bytes=40 * MIB),
        name="finish",
    )(gain, hidden, cells, gate, weight)


def finish_project_kernel(
    mask_ref, in_gain_ref, out_gain_ref, hidden_ref, cells_ref, gate_ref, weight_ref, proj_ref,
    cells_out, pairs_out, gains, scratch, proj_turned, row_masks, left, right,
):
    gain_mask = masked_gain(in_gain_ref, 1, mask_ref)
    set_row_masks(mask_ref, row_masks)
    normed_hidden_rows(0, out_gain_ref, hidden_ref, gains, scratch)
    weight = jnp.transpose(weight_ref[0])
    proj_turned[...] = jnp.transpose(proj_ref[1])
    for first in range(0, ROWS, SUB):
        rows = updated_rows(first, scratch, weight, cells_ref, gate_ref)
        for index, row in enumerate(rows):
            cells_out[first + index] = row
        masks = [row_mask(row_masks, first + index) for index in range(SUB)]
        rows = [row.astype(F32) for row in rows]
        project_rows(rows, masks, gain_mask, proj_turned, left, right, first)
    emit_projections(left, right, pairs_out)


def finish_project(mask, in_gain, out_gain, hidden, cells, gate, weight, proj):
    call = kernel_call(
        finish_project_kernel,
        "finish_project",
        [VMEM] * 8,
        [TURNED, PAIRS],
        HIDDEN_SCRATCH + [pltpu.VMEM((4 * CHAN, CHAN), BF16)] + PROJ_SCRATCH,
    )
    return call(mask, in_gain, out_gain, hidden, cells, gate, weight, proj)


TOKENS = BLOCKS * COLS
HALF = GROUPS * ROWS
PRODUCT = jax.ShapeDtypeStruct((DEPTH, 2, BLOCKS, ROWS, COLS), BF16)


def block_lanes(block):
    return slice(block * COLS, (block + 1) * COLS)


def side(pairs_ref, block, which):
    return pairs_ref[:, block, :, which].reshape(GROUPS, ROWS, COLS)


def take_right_kernel(pairs_ref, out_ref):
    for block in range(BLOCKS):
        out_ref[:, block] = side(pairs_ref, block, 1)


def take_right(pairs):
    shape = jax.ShapeDtypeStruct((GROUPS, BLOCKS, ROWS, COLS), BF16)
    return kernel_call(take_right_kernel, "take_right", [VMEM], shape)(pairs)


def store_product(product, out_ref, block):
    for half in range(2):
        columns = product[:, block_lanes(half)].reshape(2, DEPTH, ROWS, COLS)
        for side_x in range(2):
            out_ref[:, side_x, block + half] = columns[side_x]


def outgoing_kernel(pairs_ref, other_ref, out_ref, left, right):
    core = lax.axis_index("c")
    for block in range(BLOCKS):
        left[:, :, block_lanes(block)] = side(pairs_ref, block, 0)
        right[:, core, :, block_lanes(block)] = side(pairs_ref, block, 1)
        right[:, 1 - core, :, block_lanes(block)] = other_ref[:, block]
    left_rows = left[...].reshape(HALF, TOKENS)
    for block in range(0, BLOCKS, 2):
        groups = slice(block * 2, block * 2 + 4)
        product = lax.dot_general(
            left_rows,
            right[groups].reshape(2 * COLS, TOKENS),
            (((1,), (1,)), ((), ())),
            preferred_element_type=F32,
        ).astype(BF16)
        store_product(product, out_ref, block)


def outgoing(pairs, other):
    call = kernel_call(
        outgoing_kernel,
        "outgoing",
        [VMEM, VMEM],
        PRODUCT,
        [pltpu.VMEM((GROUPS, ROWS, TOKENS), BF16), pltpu.VMEM((GROUPS, 2, ROWS, TOKENS), BF16)],
    )
    return call(pairs, other)


def incoming_send_kernel(pairs_ref, send_ref, left_ref, right_ref, turned):
    core = lax.axis_index("c")
    for block in range(BLOCKS):
        right_ref[:, block_lanes(block)] = side(pairs_ref, block, 1).reshape(HALF, COLS)
        left = side(pairs_ref, block, 0).reshape(HALF, COLS)
        turned[2 * block : 2 * block + 2] = jnp.transpose(left).reshape(2, 2, ROWS, HALF)
    left_ref[...] = turned[:, core].reshape(HALF, HALF)
    send_ref[...] = jnp.dot(
        turned[:, 1 - core].reshape(HALF, HALF), right_ref[...], preferred_element_type=F32
    ).astype(BF16)


def incoming_send(pairs):
    call = kernel_call(
        incoming_send_kernel,
        "incoming_send",
        [VMEM],
        [
            jax.ShapeDtypeStruct((HALF, TOKENS), BF16),
            jax.ShapeDtypeStruct((HALF, HALF), BF16),
            jax.ShapeDtypeStruct((HALF, TOKENS), BF16),
        ],
        [pltpu.VMEM((GROUPS, 2, ROWS, HALF), BF16)],
    )
    return call(pairs)


def incoming_kernel(left_ref, right_ref, other_ref, out_ref):
    left = left_ref[...]
    for block in range(0, BLOCKS, 2):
        lanes = slice(block * COLS, (block + 2) * COLS)
        total = jnp.dot(left, right_ref[:, lanes], preferred_element_type=F32)
        product = (total + other_ref[:, lanes].astype(F32)).astype(BF16)
        store_product(product, out_ref, block)


def incoming(left, right, other):
    return kernel_call(incoming_kernel, "incoming", [VMEM, VMEM, VMEM], PRODUCT)(left, right, other)


def planes_first(pairs):
    pairs = jnp.swapaxes(lax.all_to_all(pairs, "z", split_axis=0, concat_axis=0, tiled=True), 0, 1)
    return lax.all_to_all(pairs, PLANE, split_axis=0, concat_axis=0, tiled=True)


def planes_last(pairs):
    pairs = jnp.swapaxes(pairs, 0, 1)
    pairs = jnp.swapaxes(lax.all_to_all(pairs, PLANE, split_axis=0, concat_axis=0, tiled=True), 0, 1)
    return jnp.swapaxes(lax.all_to_all(pairs, "z", split_axis=0, concat_axis=0, tiled=True), 0, 1)


def exchange(values, first_core):
    return lax.cond(lax.axis_index("c") == first_core, planes_first, planes_last, values)


def exchange_pairs(pairs, first_core):
    pairs = exchange(pairs.reshape(DEPTH, CHIPS, 2 * ROWS, COLS), first_core)
    return pairs.reshape(2, BLOCKS, DEPTH, 2, ROWS, COLS)


def exchange_product(product, first_core):
    return exchange(product.reshape(DEPTH, CHIPS, ROWS, COLS), first_core)


def exchange_at_once(product):
    flat = product.reshape(CHAN, ROWS, COLS)
    flat = lax.all_to_all(flat, ("z",) + PLANE, split_axis=0, concat_axis=0, tiled=True)
    return flat.reshape(DEPTH, CHIPS, ROWS, COLS)


def to_other_core(values):
    return lax.ppermute(values, "c", [(0, 1), (1, 0)])


def per_device(pair_input, token_mask, in_gain, proj_weight, gate_weight, out_gain, out_weight):
    mask = token_mask.reshape(BLOCKS, COLS)

    pairs, cells = project(mask, in_gain, pair_input, proj_weight)
    pairs = exchange_pairs(pairs, 0)
    other = to_other_core(take_right(pairs))
    gate = output_gate(0, in_gain, cells, gate_weight)
    product = outgoing(pairs, other)
    hidden = exchange_at_once(product)
    cells, pairs = finish_project(mask, in_gain, out_gain, hidden, cells, gate, out_weight, proj_weight)

    pairs = exchange_pairs(pairs, 1)
    send, left, right = incoming_send(pairs)
    other = to_other_core(send)
    gate = output_gate(1, in_gain, cells, gate_weight)
    product = incoming(left, right, other)
    hidden = exchange_product(product, 0)
    return finish(out_gain, hidden, cells, gate, out_weight)


def solution(mesh):
    split = Mesh(mesh.devices.reshape(2, 8, 2, 2, 4), ("xh", "z", "c", "xl", "y"))
    cells = P(("xh", "z", "c"), ("xl", "y"), None)
    return jax.shard_map(
        per_device, mesh=split, in_specs=(cells, P(), P(), P(), P(), P(), P()), out_specs=cells, check_vma=False
    )
```

```python
import functools

import jax
import jax.numpy as jnp
from jax import lax
from jax.experimental import pallas as pl
from jax.experimental.pallas import tpu as pltpu
from jax.sharding import Mesh, PartitionSpec as P

EPSILON = 1e-05
CHAN = 128
ROWS = 32
COLS = 128
GROUPS = 16
DEPTH = 8
CHIPS = 16
BLOCKS = 8
SUB = 16
CHUNK = 16
SPAN = 32
CHAN_PITCH = CHAN + 1
ROW_PITCH = ROWS + 1
PLANE = ("xh", "xl", "y")
F32 = jnp.float32
BF16 = jnp.bfloat16
MIB = 1024 * 1024


def sigmoid(values):
    return 0.5 * jnp.tanh(0.5 * values) + 0.5


VMEM = pl.BlockSpec(memory_space=pltpu.VMEM)


def kernel_call(kernel, name, in_specs, out_shape, scratch_shapes=(), cost=None, vmem=40):
    return pl.pallas_call(
        kernel,
        in_specs=in_specs,
        out_specs=jax.tree.map(lambda _: VMEM, out_shape),
        out_shape=out_shape,
        scratch_shapes=scratch_shapes,
        compiler_params=pltpu.CompilerParams(vmem_limit_bytes=vmem * MIB),
        cost_estimate=cost,
        name=name,
    )


HBM = pl.BlockSpec(memory_space=pltpu.HBM)
PROJ_SCRATCH = [pltpu.VMEM((COLS, COLS), F32)] + [pltpu.VMEM((ROWS * CHAN_PITCH + CHAN, COLS), F32)] * 2
HIDDEN_SCRATCH = [pltpu.VMEM((CHAN, COLS), F32), pltpu.VMEM((CHAN * ROW_PITCH + ROWS, COLS), F32)]
PAIRS = jax.ShapeDtypeStruct((CHAN, 2, ROWS, COLS), BF16)
CELLS = jax.ShapeDtypeStruct((ROWS, COLS, CHAN), BF16)
TURNED = jax.ShapeDtypeStruct((ROWS, CHAN, COLS), BF16)
GATE = jax.ShapeDtypeStruct((ROWS, CHAN, COLS), F32)


def layer_norm(turned, factor):
    average = jnp.mean(turned, axis=0, keepdims=True)
    centred = turned - average
    variance = jnp.mean(centred * centred, axis=0, keepdims=True)
    return centred * lax.rsqrt(variance + EPSILON) * factor


def channel_column(gain_ref, module):
    return jnp.transpose(jnp.broadcast_to(gain_ref[module : module + 1, :], (COLS, CHAN)))


def masked_gain(gain_ref, module, col_mask_ref):
    block = lax.axis_index(("xl", "y"))
    return channel_column(gain_ref, module) * col_mask_ref[pl.ds(block, 1), :].astype(F32)


def set_row_masks(mask_ref, scratch):
    block = lax.axis_index(("xh", "z", "c")) // (COLS // ROWS)
    tokens = jnp.broadcast_to(mask_ref[pl.ds(block, 1), :].astype(F32), (COLS, COLS))
    scratch[...] = jnp.transpose(tokens)


def row_mask(scratch, index):
    start = lax.axis_index(("xh", "z", "c")) % (COLS // ROWS) * ROWS
    return scratch[pl.ds(start + index, 1), :]


def project_rows(rows, row_masks, gain_mask, weight, left_scratch, right_scratch, first):
    normed = [layer_norm(row, gain_mask * mask).astype(BF16) for row, mask in zip(rows, row_masks)]
    projected = jnp.dot(weight[...], jnp.concatenate(normed, axis=1), preferred_element_type=F32)
    left = sigmoid(projected[:CHAN]) * projected[CHAN : 2 * CHAN]
    right = sigmoid(projected[2 * CHAN : 3 * CHAN]) * projected[3 * CHAN :]
    for index in range(len(rows)):
        place = pl.ds((first + index) * CHAN_PITCH, CHAN)
        lanes = slice(index * COLS, (index + 1) * COLS)
        left_scratch[place, :] = left[:, lanes]
        right_scratch[place, :] = right[:, lanes]


def emit_projections(left_scratch, right_scratch, out_ref, first=0, count=CHAN):
    def body(chan, carry):
        place = pl.ds(chan, ROWS, stride=CHAN_PITCH)
        out_ref[chan, 0] = left_scratch[place, :].astype(BF16)
        out_ref[chan, 1] = right_scratch[place, :].astype(BF16)
        return carry

    lax.fori_loop(first, first + count, body, 0, unroll=8)


def project_kernel(
    mask_hbm, gain_hbm, cells_hbm, weight_hbm, pairs_hbm, turned_hbm,
    cells_ref, weight_ref, mask_ref, gain_ref, weight_turned, row_masks, left, right, pairs_ref, turned_ref, sems,
):
    chunks = ROWS // CHUNK
    rows_of = [pl.ds(index * CHUNK, CHUNK) for index in range(chunks)]
    small_copies = [
        pltpu.make_async_copy(weight_hbm.at[0], weight_ref, sems.at[0]),
        pltpu.make_async_copy(mask_hbm, mask_ref, sems.at[1]),
        pltpu.make_async_copy(gain_hbm, gain_ref, sems.at[2]),
    ]
    cell_copies = [
        pltpu.make_async_copy(cells_hbm.at[rows], cells_ref.at[rows], sems.at[3 + index])
        for index, rows in enumerate(rows_of)
    ]
    turned_copies = [
        pltpu.make_async_copy(turned_ref.at[rows], turned_hbm.at[rows], sems.at[3 + chunks + index])
        for index, rows in enumerate(rows_of)
    ]
    for copy in small_copies + cell_copies:
        copy.start()
    for copy in small_copies:
        copy.wait()
    gain_mask = masked_gain(gain_ref, 0, mask_ref)
    set_row_masks(mask_ref, row_masks)
    weight_turned[...] = jnp.transpose(weight_ref[...])
    for first in range(0, ROWS, SUB):
        if first % CHUNK == 0:
            cell_copies[first // CHUNK].wait()
        rows = []
        for index in range(first, first + SUB):
            row = jnp.transpose(cells_ref[index])
            turned_ref[index] = row
            rows.append(row.astype(F32))
        if (first + SUB) % CHUNK == 0:
            turned_copies[first // CHUNK].start()
        masks = [row_mask(row_masks, first + index) for index in range(SUB)]
        project_rows(rows, masks, gain_mask, weight_turned, left, right, first)
    pair_copies = []
    for first in range(0, CHAN, SPAN):
        emit_projections(left, right, pairs_ref, first, SPAN)
        span = pl.ds(first, SPAN)
        pair_copies.append(
            pltpu.make_async_copy(
                pairs_ref.at[span], pairs_hbm.at[span], sems.at[3 + 2 * chunks + first // SPAN]
            )
        )
        pair_copies[-1].start()
    for copy in turned_copies + pair_copies:
        copy.wait()


def project(mask, gain, cells, weight):
    return pl.pallas_call(
        project_kernel,
        in_specs=[HBM, HBM, HBM, HBM],
        out_specs=[HBM, HBM],
        out_shape=[PAIRS, TURNED],
        scratch_shapes=[
            pltpu.VMEM((ROWS, COLS, CHAN), BF16),
            pltpu.VMEM((CHAN, 4 * CHAN), BF16),
            pltpu.VMEM(mask.shape, jnp.int32),
            pltpu.VMEM(gain.shape, F32),
            pltpu.VMEM((4 * CHAN, CHAN), BF16),
            *PROJ_SCRATCH,
            pltpu.VMEM(PAIRS.shape, BF16),
            pltpu.VMEM(TURNED.shape, BF16),
            pltpu.SemaphoreType.DMA((3 + 2 * (ROWS // CHUNK) + CHAN // SPAN,)),
        ],
        compiler_params=pltpu.CompilerParams(vmem_limit_bytes=56 * MIB),
        name="project",
    )(mask, gain, cells, weight)


def gate_kernel(module, gain_ref, cells_ref, weight_ref, out_ref):
    gain = channel_column(gain_ref, module)
    weight = jnp.transpose(weight_ref[module])
    for first in range(0, ROWS, SUB):
        rows = [layer_norm(cells_ref[first + index].astype(F32), gain).astype(BF16) for index in range(SUB)]
        gate = sigmoid(jnp.dot(weight, jnp.concatenate(rows, axis=1), preferred_element_type=F32))
        for index in range(SUB):
            out_ref[first + index] = gate[:, index * COLS : (index + 1) * COLS]


def output_gate(module, gain, cells, weight):
    call = kernel_call(
        functools.partial(gate_kernel, module),
        "output_gate",
        [VMEM, VMEM, VMEM],
        GATE,
        cost=pl.CostEstimate(
            flops=2 * ROWS * COLS * CHAN * CHAN, bytes_accessed=3 << 20, transcendentals=ROWS * COLS * CHAN
        ),
    )
    return call(gain, cells, weight)


def normed_hidden_rows(module, gain_ref, hidden_ref, gains, scratch):
    gains[...] = channel_column(gain_ref, module)
    for first in range(0, ROWS, 16):
        rows = slice(first, first + 16)
        hidden = hidden_ref[:, :, rows].astype(F32).reshape(CHAN, 16, COLS)
        average = jnp.mean(hidden, axis=0)
        centred = hidden - average[None]
        scale = lax.rsqrt(jnp.mean(centred * centred, axis=0) + EPSILON)

        def body(chip, carry):
            for plane in range(DEPTH):
                chan = plane * CHIPS + chip
                place = (plane, chip) if module == 0 else (chip, plane)
                values = (hidden_ref[place + (rows,)].astype(F32) - average) * scale
                scratch[pl.ds(chan * ROW_PITCH + first, 16), :] = values * gains[pl.ds(chan, 1), :]
            return carry

        lax.fori_loop(0, CHIPS, body, 0)


def updated_rows(first, scratch, weight, cells_ref, gate_ref):
    hidden = [
        scratch[pl.ds(first + index, CHAN, stride=ROW_PITCH), :].astype(BF16) for index in range(SUB)
    ]
    update = jnp.dot(weight, jnp.concatenate(hidden, axis=1), preferred_element_type=F32)
    return [
        (
            cells_ref[first + index].astype(F32)
            + gate_ref[first + index] * update[:, index * COLS : (index + 1) * COLS]
        ).astype(BF16)
        for index in range(SUB)
    ]


def finish_kernel(gain_ref, hidden_ref, cells_ref, gate_ref, weight_ref, out_hbm, gains, scratch, out_ref, sems):
    normed_hidden_rows(1, gain_ref, hidden_ref, gains, scratch)
    weight = jnp.transpose(weight_ref[1])
    copies = []
    for first in range(0, ROWS, SUB):
        for index, row in enumerate(updated_rows(first, scratch, weight, cells_ref, gate_ref)):
            out_ref[first + index] = jnp.transpose(row)
        if (first + SUB) % CHUNK == 0:
            rows = pl.ds(first + SUB - CHUNK, CHUNK)
            copies.append(pltpu.make_async_copy(out_ref.at[rows], out_hbm.at[rows], sems.at[first // CHUNK]))
            copies[-1].start()
    for copy in copies:
        copy.wait()


def finish(gain, hidden, cells, gate, weight):
    return pl.pallas_call(
        finish_kernel,
        in_specs=[VMEM] * 5,
        out_specs=HBM,
        out_shape=CELLS,
        scratch_shapes=[
            *HIDDEN_SCRATCH,
            pltpu.VMEM((ROWS, COLS, CHAN), BF16),
            pltpu.SemaphoreType.DMA((ROWS // CHUNK,)),
        ],
        compiler_params=pltpu.CompilerParams(vmem_limit_bytes=40 * MIB),
        name="finish",
    )(gain, hidden, cells, gate, weight)


def finish_project_kernel(
    mask_ref, in_gain_ref, out_gain_ref, hidden_ref, cells_ref, gate_weight_ref, weight_ref, proj_ref,
    cells_out, pairs_out, gains, scratch, proj_turned, row_masks, left, right,
):
    gain_mask = masked_gain(in_gain_ref, 1, mask_ref)
    set_row_masks(mask_ref, row_masks)
    normed_hidden_rows(0, out_gain_ref, hidden_ref, gains, scratch)
    weight = jnp.transpose(weight_ref[0])
    proj_turned[...] = jnp.transpose(proj_ref[1])
    gate_gain = channel_column(in_gain_ref, 0)
    gate_weight = jnp.transpose(gate_weight_ref[0])
    for first in range(0, ROWS, SUB):
        normed = [
            layer_norm(cells_ref[first + index].astype(F32), gate_gain).astype(BF16) for index in range(SUB)
        ]
        gates = sigmoid(jnp.dot(gate_weight, jnp.concatenate(normed, axis=1), preferred_element_type=F32))
        gate = {first + index: gates[:, index * COLS : (index + 1) * COLS] for index in range(SUB)}
        rows = updated_rows(first, scratch, weight, cells_ref, gate)
        for index, row in enumerate(rows):
            cells_out[first + index] = row
        masks = [row_mask(row_masks, first + index) for index in range(SUB)]
        rows = [row.astype(F32) for row in rows]
        project_rows(rows, masks, gain_mask, proj_turned, left, right, first)
    emit_projections(left, right, pairs_out)


def finish_project(mask, in_gain, out_gain, hidden, cells, gate, weight, proj):
    call = kernel_call(
        finish_project_kernel,
        "finish_project",
        [VMEM] * 8,
        [TURNED, PAIRS],
        HIDDEN_SCRATCH + [pltpu.VMEM((4 * CHAN, CHAN), BF16)] + PROJ_SCRATCH,
    )
    return call(mask, in_gain, out_gain, hidden, cells, gate, weight, proj)


TOKENS = BLOCKS * COLS
HALF = GROUPS * ROWS
PRODUCT = jax.ShapeDtypeStruct((DEPTH, 2, BLOCKS, ROWS, COLS), BF16)


def block_lanes(block):
    return slice(block * COLS, (block + 1) * COLS)


def side(pairs_ref, block, which):
    return pairs_ref[:, block, :, which].reshape(GROUPS, ROWS, COLS)


def take_right_kernel(pairs_ref, out_ref):
    for block in range(BLOCKS):
        out_ref[:, block] = side(pairs_ref, block, 1)


def take_right(pairs):
    shape = jax.ShapeDtypeStruct((GROUPS, BLOCKS, ROWS, COLS), BF16)
    return kernel_call(take_right_kernel, "take_right", [VMEM], shape)(pairs)


def store_product(product, out_ref, block):
    for half in range(2):
        columns = product[:, block_lanes(half)].reshape(2, DEPTH, ROWS, COLS)
        for side_x in range(2):
            out_ref[:, side_x, block + half] = columns[side_x]


def outgoing_kernel(pairs_ref, other_ref, out_ref, left, right):
    core = lax.axis_index("c")
    for block in range(BLOCKS):
        left[:, :, block_lanes(block)] = side(pairs_ref, block, 0)
        right[:, core, :, block_lanes(block)] = side(pairs_ref, block, 1)
        right[:, 1 - core, :, block_lanes(block)] = other_ref[:, block]
    left_rows = left[...].reshape(HALF, TOKENS)
    for block in range(0, BLOCKS, 2):
        groups = slice(block * 2, block * 2 + 4)
        product = lax.dot_general(
            left_rows,
            right[groups].reshape(2 * COLS, TOKENS),
            (((1,), (1,)), ((), ())),
            preferred_element_type=F32,
        ).astype(BF16)
        store_product(product, out_ref, block)


def outgoing(pairs, other):
    call = kernel_call(
        outgoing_kernel,
        "outgoing",
        [VMEM, VMEM],
        PRODUCT,
        [pltpu.VMEM((GROUPS, ROWS, TOKENS), BF16), pltpu.VMEM((GROUPS, 2, ROWS, TOKENS), BF16)],
    )
    return call(pairs, other)


def incoming_send_kernel(pairs_ref, send_ref, left_ref, right_ref, turned):
    core = lax.axis_index("c")
    for block in range(BLOCKS):
        right_ref[:, block_lanes(block)] = side(pairs_ref, block, 1).reshape(HALF, COLS)
        left = side(pairs_ref, block, 0).reshape(HALF, COLS)
        turned[2 * block : 2 * block + 2] = jnp.transpose(left).reshape(2, 2, ROWS, HALF)
    left_ref[...] = turned[:, core].reshape(HALF, HALF)
    send_ref[...] = jnp.dot(
        turned[:, 1 - core].reshape(HALF, HALF), right_ref[...], preferred_element_type=F32
    ).astype(BF16)


def incoming_send(pairs):
    call = kernel_call(
        incoming_send_kernel,
        "incoming_send",
        [VMEM],
        [
            jax.ShapeDtypeStruct((HALF, TOKENS), BF16),
            jax.ShapeDtypeStruct((HALF, HALF), BF16),
            jax.ShapeDtypeStruct((HALF, TOKENS), BF16),
        ],
        [pltpu.VMEM((GROUPS, 2, ROWS, HALF), BF16)],
    )
    return call(pairs)


def incoming_kernel(left_ref, right_ref, other_ref, out_ref):
    left = left_ref[...]
    for block in range(0, BLOCKS, 2):
        lanes = slice(block * COLS, (block + 2) * COLS)
        total = jnp.dot(left, right_ref[:, lanes], preferred_element_type=F32)
        product = (total + other_ref[:, lanes].astype(F32)).astype(BF16)
        store_product(product, out_ref, block)


def incoming(left, right, other):
    return kernel_call(incoming_kernel, "incoming", [VMEM, VMEM, VMEM], PRODUCT)(left, right, other)


def planes_first(pairs):
    pairs = jnp.swapaxes(lax.all_to_all(pairs, "z", split_axis=0, concat_axis=0, tiled=True), 0, 1)
    return lax.all_to_all(pairs, PLANE, split_axis=0, concat_axis=0, tiled=True)


def planes_last(pairs):
    pairs = jnp.swapaxes(pairs, 0, 1)
    pairs = jnp.swapaxes(lax.all_to_all(pairs, PLANE, split_axis=0, concat_axis=0, tiled=True), 0, 1)
    return jnp.swapaxes(lax.all_to_all(pairs, "z", split_axis=0, concat_axis=0, tiled=True), 0, 1)


def exchange(values, first_core):
    return lax.cond(lax.axis_index("c") == first_core, planes_first, planes_last, values)


def exchange_pairs(pairs, first_core):
    pairs = exchange(pairs.reshape(DEPTH, CHIPS, 2 * ROWS, COLS), first_core)
    return pairs.reshape(2, BLOCKS, DEPTH, 2, ROWS, COLS)


def exchange_product(product, first_core):
    return exchange(product.reshape(DEPTH, CHIPS, ROWS, COLS), first_core)


def exchange_at_once(product):
    flat = product.reshape(CHAN, ROWS, COLS)
    flat = lax.all_to_all(flat, ("z",) + PLANE, split_axis=0, concat_axis=0, tiled=True)
    return flat.reshape(DEPTH, CHIPS, ROWS, COLS)


def to_other_core(values):
    return lax.ppermute(values, "c", [(0, 1), (1, 0)])


def per_device(pair_input, token_mask, in_gain, proj_weight, gate_weight, out_gain, out_weight):
    mask = token_mask.reshape(BLOCKS, COLS)

    pairs, cells = project(mask, in_gain, pair_input, proj_weight)
    pairs = exchange_pairs(pairs, 0)
    other = to_other_core(take_right(pairs))
    product = outgoing(pairs, other)
    hidden = exchange_at_once(product)
    cells, pairs = finish_project(mask, in_gain, out_gain, hidden, cells, gate_weight, out_weight, proj_weight)

    pairs = exchange_pairs(pairs, 1)
    send, left, right = incoming_send(pairs)
    other = to_other_core(send)
    gate = output_gate(1, in_gain, cells, gate_weight)
    product = incoming(left, right, other)
    hidden = exchange_product(product, 0)
    return finish(out_gain, hidden, cells, gate, out_weight)


def solution(mesh):
    split = Mesh(mesh.devices.reshape(2, 8, 2, 2, 4), ("xh", "z", "c", "xl", "y"))
    cells = P(("xh", "z", "c"), ("xl", "y"), None)
    return jax.shard_map(
        per_device, mesh=split, in_specs=(cells, P(), P(), P(), P(), P(), P()), out_specs=cells, check_vma=False
    )
```
